32 devices in a mesh: dp: 16 (over z, y, core), fsdp: 2 (over x).
Axes of the slice: x: 2, y: 2, z: 4, core: 2. Of those that a mesh axis runs over, the one named last changes fastest.
Arguments:
- hidden_in: bfloat16 [8192, 960], P(('dp', 'fsdp')), may hold values from -6 to 6
- cotangent: bfloat16 [8192, 960], P(('dp', 'fsdp')), may hold values from -6 to 6
- norm_attn: float32 [960], P('fsdp'), may hold values from 0.5 to 1.5
- norm_ffn: float32 [960], P('fsdp'), may hold values from 0.5 to 1.5
- router: float32 [960, 3], P('fsdp'), may hold values from -0.125 to 0.125
- w_query: float32 [960, 960], P('fsdp'), may hold values from -0.1875 to 0.1875
- key_weight: float32 [960, 320], P('fsdp'), may hold values from -0.1875 to 0.1875
- value_weight: float32 [960, 320], P('fsdp'), may hold values from -0.1875 to 0.1875
- w_out: float32 [960, 960], P('fsdp'), may hold values from -0.75 to 0.75
- w_gate: float32 [960, 2560], P('fsdp'), may hold values from -0.1875 to 0.1875
- w_up: float32 [960, 2560], P('fsdp'), may hold values from -0.1875 to 0.1875
- w_down: float32 [2560, 960], P('fsdp'), may hold values from -0.15625 to 0.15625
- lengths: int32 [32], P(('dp', 'fsdp')), may hold values from 128 to 256, as said below
- chosen_second: int32 [32, 128], P(('dp', 'fsdp')), may hold values from 0 to 255, as said below
- chosen_third: int32 [32, 32], P(('dp', 'fsdp')), may hold values from 0 to 255, as said below
Outputs:
- hidden_out: bfloat16 [8192, 960], P(('dp', 'fsdp'))
- grad_hidden: float32 [8192, 960], P(('dp', 'fsdp'))
- grad_norm_attn: float32 [960], P('fsdp')
- grad_norm_ffn: float32 [960], P('fsdp')
- grad_router: float32 [960, 3], P('fsdp')
- grad_query: float32 [960, 960], P('fsdp')
- grad_key: float32 [960, 320], P('fsdp')
- grad_value: float32 [960, 320], P('fsdp')
- grad_out: float32 [960, 960], P('fsdp')
- grad_gate: float32 [960, 2560], P('fsdp')
- grad_up: float32 [960, 2560], P('fsdp')
- grad_down: float32 [2560, 960], P('fsdp')
The draws below stay inside these ranges and needn't reach their ends.
Inputs may be any that keep to these rules, and one draw needn't show every extreme that they name: `lengths`: some sequence is exactly 256 long and another exactly 128. `chosen_second`: each row holds distinct positions in increasing order, all below that sequence's length, among them position 0 and the sequence's last valid position. `chosen_third`: each row holds distinct positions of the same row of chosen_second, in increasing order, among them its first and its last.
All inputs are finite; a program needn't handle non-finite values.
Results may differ from the reference program's by a relative error of at most 0.024.
Values may be sent and summed in bfloat16 or wider, within the bound.
No kernel may reach another device: no remote copies, remote signals or barrier semaphores. Data moves between devices by JAX's collectives and lax.ppermute only.
A program may use at most 384 MiB of HBM per device.

```python
import jax
import jax.numpy as jnp
from jax import lax

MODEL_WIDTH = 960
QUERY_HEADS = 15
KEY_VALUE_HEADS = 5
HEAD_SIZE = 64
FF = 2560
RECUR = 3
TOK_DEV = 256
KEEP2 = 128
KEEP3 = 32
SEQS = 32
TOKENS = 8192


def length_table(key):
    inner = jax.random.fold_in(key, 11)
    base = jax.random.randint(inner, (SEQS,), TOK_DEV // 2, TOK_DEV + 1)
    shuffled = jax.random.permutation(jax.random.fold_in(inner, 1), SEQS)
    base = base.at[shuffled[0]].set(TOK_DEV)
    base = base.at[shuffled[1]].set(TOK_DEV // 2)
    return base.astype(jnp.int32)


def chosen_table(key):
    lengths = length_table(key)
    noise = jax.random.randint(jax.random.fold_in(key, 12), (SEQS, TOK_DEV), 0, 2 ** 18)
    places = jnp.arange(TOK_DEV, dtype=jnp.int32)
    ranking = (noise + 1) * TOK_DEV + places[None, :]
    forced = (places[None, :] == 0) | (places[None, :] == lengths[:, None] - 1)
    ranking = jnp.where(forced, places[None, :], ranking)
    ranking = jnp.where(places[None, :] < lengths[:, None], ranking, ranking + 2 ** 30)
    chosen_two = jnp.sort(jnp.argsort(ranking, axis=1)[:, :KEEP2], axis=1).astype(jnp.int32)
    slot_noise = jax.random.randint(jax.random.fold_in(key, 13), (SEQS, KEEP2), 0, 2 ** 18)
    slots = jnp.arange(KEEP2, dtype=jnp.int32)
    slot_ranking = (slot_noise + 1) * KEEP2 + slots[None, :]
    slot_forced = (slots[None, :] == 0) | (slots[None, :] == KEEP2 - 1)
    slot_ranking = jnp.where(slot_forced, slots[None, :], slot_ranking)
    picked = jnp.sort(jnp.argsort(slot_ranking, axis=1)[:, :KEEP3], axis=1)
    chosen_three = jnp.take_along_axis(chosen_two, picked, axis=1).astype(jnp.int32)
    return (chosen_two, chosen_three)


def draw_lengths(key, part):
    return length_table(key)


def draw_chosen_second(key, part):
    return chosen_table(key)[0]


def draw_chosen_third(key, part):
    return chosen_table(key)[1]


def shard_levels(stream_key, dims, pieces, smallest, largest):
    factor_of, own = 1.0, jax.random.fold_in(stream_key, 6)
    for axis_at, parts in pieces:
        steps = jnp.exp(jax.random.uniform(jax.random.fold_in(own, axis_at), (parts,), jnp.float32, smallest / len(pieces), largest / len(pieces)))
        factor_of = factor_of * jnp.repeat(steps, dims[axis_at] // parts).reshape([-1 if axis == axis_at else 1 for axis in range(len(dims))])
    return factor_of


def normal_values(key, extent, deviation, bound, split=(), kind=jnp.bfloat16):
    level = shard_levels(key, extent, split, -0.22, 0.18) if split else 1.0
    values = jax.random.normal(key, extent, jnp.float32) * deviation * level
    return jnp.minimum(jnp.maximum(values, -bound), bound).astype(kind)


def setup_inputs(seed: int = 0) -> dict:
    streams_of = jax.random.split(jax.random.key(seed), 16)
    hidden_in = normal_values(streams_of[0], (TOKENS, MODEL_WIDTH), 1.0, 6.0, ((0, 32),))
    cotangent = normal_values(streams_of[1], (TOKENS, MODEL_WIDTH), 1.0, 6.0, ((0, 32),))
    norm_attn = jnp.clip(1.0 + 0.1 * jax.random.normal(streams_of[2], (MODEL_WIDTH,), jnp.float32), 0.5, 1.5)
    norm_ffn = jnp.clip(1.0 + 0.1 * jax.random.normal(streams_of[3], (MODEL_WIDTH,), jnp.float32), 0.5, 1.5)
    router = normal_values(streams_of[4], (MODEL_WIDTH, RECUR), (2 * MODEL_WIDTH) ** -0.5, 0.125, ((0, 2),), jnp.float32)
    w_query = normal_values(streams_of[5], (MODEL_WIDTH, QUERY_HEADS * HEAD_SIZE), MODEL_WIDTH ** -0.5, 0.1875, ((0, 2),), jnp.float32)
    key_weight = normal_values(streams_of[6], (MODEL_WIDTH, KEY_VALUE_HEADS * HEAD_SIZE), MODEL_WIDTH ** -0.5, 0.1875, ((0, 2),), jnp.float32)
    value_weight = normal_values(streams_of[7], (MODEL_WIDTH, KEY_VALUE_HEADS * HEAD_SIZE), MODEL_WIDTH ** -0.5, 0.1875, ((0, 2),), jnp.float32)
    w_out = normal_values(streams_of[8], (QUERY_HEADS * HEAD_SIZE, MODEL_WIDTH), (QUERY_HEADS * HEAD_SIZE // 16) ** -0.5, 0.75, ((0, 2),), jnp.float32)
    w_gate = normal_values(streams_of[9], (MODEL_WIDTH, FF), MODEL_WIDTH ** -0.5, 0.1875, ((0, 2),), jnp.float32)
    w_up = normal_values(streams_of[10], (MODEL_WIDTH, FF), MODEL_WIDTH ** -0.5, 0.1875, ((0, 2),), jnp.float32)
    w_down = normal_values(streams_of[11], (FF, MODEL_WIDTH), (FF // 2) ** -0.5, 0.15625, ((0, 2),), jnp.float32)
    lengths = draw_lengths(jax.random.fold_in(streams_of[15], 71), 0)
    chosen_second = draw_chosen_second(jax.random.fold_in(streams_of[15], 71), 0)
    chosen_third = draw_chosen_third(jax.random.fold_in(streams_of[15], 71), 0)
    return dict(hidden_in=hidden_in, cotangent=cotangent, norm_attn=norm_attn, norm_ffn=norm_ffn, router=router, w_query=w_query, key_weight=key_weight, value_weight=value_weight, w_out=w_out, w_gate=w_gate, w_up=w_up, w_down=w_down, lengths=lengths, chosen_second=chosen_second, chosen_third=chosen_third)


@jax.custom_vjp
def narrow_cast(v):
    return lax.optimization_barrier(v.astype(jnp.bfloat16)).astype(jnp.float32)

@jax.custom_vjp
def narrow_cast_backward(v):
    return v

def low_keep(v):
    return (narrow_cast(v), None)

def low_pass(kept, grad):
    return (grad,)

def back_keep(v):
    return (v, None)

def back_low(kept, grad):
    return (narrow_cast(grad),)
narrow_cast.defvjp(low_keep, low_pass)
narrow_cast_backward.defvjp(back_keep, back_low)
epsilon = 1e-05
negative = -1e+30
highest = lax.Precision.HIGHEST

def matrix_product(left, right):
    return jnp.dot(left, right, precision=highest, preferred_element_type=jnp.float32)

def rms_scaled(value_rows, gain):
    return value_rows * lax.rsqrt(lax.optimization_barrier(jnp.mean(value_rows * value_rows, axis=-1, keepdims=True)) + epsilon) * gain

def rotation(positions):
    half_width = HEAD_SIZE // 2
    frequency = 10000.0 ** (-jnp.arange(half_width, dtype=jnp.float32) / half_width)
    angles = positions.astype(jnp.float32)[:, None] * frequency[None, :]
    return (jnp.cos(angles)[:, None, :], jnp.sin(angles)[:, None, :])

def apply_rotary(value_rows, cosine_table, sine_values):
    half_width = value_rows.shape[-1] // 2
    leading = value_rows[..., :half_width]
    trailing = value_rows[..., half_width:]
    return jnp.concatenate([leading * cosine_table - trailing * sine_values, trailing * cosine_table + leading * sine_values], axis=-1)

def shared_block(current, positions, key_valid, column, weights):
    gain_attn, gain_ffn, router, w_query, key_weight, value_weight, w_out, w_gate, w_up, w_down = weights
    count_of_rows = current.shape[0]
    normalized_input = narrow_cast(rms_scaled(current, gain_attn))
    gating = jax.nn.sigmoid(matrix_product(normalized_input, router[:, column]))
    cosine_table, sine_values = rotation(positions)
    query_rows = narrow_cast(apply_rotary(narrow_cast_backward(matrix_product(normalized_input, w_query)).reshape(count_of_rows, QUERY_HEADS, HEAD_SIZE), cosine_table, sine_values))
    rotated_keys = narrow_cast(apply_rotary(narrow_cast_backward(matrix_product(normalized_input, key_weight)).reshape(count_of_rows, KEY_VALUE_HEADS, HEAD_SIZE), cosine_table, sine_values))
    value_rows = narrow_cast(narrow_cast_backward(matrix_product(normalized_input, value_weight))).reshape(count_of_rows, KEY_VALUE_HEADS, HEAD_SIZE)
    grouped_queries = query_rows.reshape(count_of_rows, KEY_VALUE_HEADS, QUERY_HEADS // KEY_VALUE_HEADS, HEAD_SIZE)
    raw_scores = jnp.einsum('qhgd,khd->hgqk', grouped_queries, rotated_keys, precision=highest)
    row_order = jnp.arange(count_of_rows)
    allowed = (row_order[None, :] <= row_order[:, None]) & key_valid[None, :]
    scores = jnp.where(allowed, narrow_cast_backward(raw_scores) * HEAD_SIZE ** (-0.5), negative)
    row_peak = lax.optimization_barrier(jnp.max(scores, axis=-1, keepdims=True))
    expanded = jnp.exp(scores - row_peak)
    probabilities = expanded / lax.optimization_barrier(jnp.sum(expanded, axis=-1, keepdims=True))
    attended = jnp.einsum('hgqk,khd->qhgd', narrow_cast(probabilities), value_rows, precision=highest).reshape(count_of_rows, QUERY_HEADS * HEAD_SIZE)
    attn_out = narrow_cast_backward(matrix_product(narrow_cast(narrow_cast_backward(attended)), w_out))
    after_attn = current + attn_out
    normed_ffn = narrow_cast(rms_scaled(after_attn, gain_ffn))
    gate_proj = narrow_cast_backward(matrix_product(normed_ffn, w_gate))
    up_proj = narrow_cast_backward(matrix_product(normed_ffn, w_up))
    hidden = narrow_cast(jax.nn.silu(gate_proj) * up_proj)
    ffn_out = narrow_cast_backward(matrix_product(hidden, w_down))
    return (attn_out + ffn_out, gating)

def recursions(current, weights, length, chosen_two, chosen_three):
    positions = jnp.arange(TOK_DEV, dtype=jnp.int32)
    valid = positions < length
    change, gating = shared_block(current, positions, valid, 0, weights)
    current = current + jnp.where(valid, gating, 0.0)[:, None] * change
    for column, chosen in ((1, chosen_two), (2, chosen_three)):
        picked = jnp.take(current, chosen, axis=0)
        change, gating = shared_block(picked, chosen, jnp.ones(chosen.shape, dtype=jnp.bool_), column, weights)
        current = current.at[chosen].set(picked + gating[:, None] * change)
    return current

def reference(hidden_in, cotangent, norm_attn, norm_ffn, router, w_query, key_weight, value_weight, w_out, w_gate, w_up, w_down, lengths, chosen_second, chosen_third):
    masters = (norm_attn, norm_ffn, router, w_query, key_weight, value_weight, w_out, w_gate, w_up, w_down)
    states = hidden_in.astype(jnp.float32).reshape(SEQS, TOK_DEV, MODEL_WIDTH)
    incoming_all = cotangent.astype(jnp.float32).reshape(SEQS, TOK_DEV, MODEL_WIDTH)

    def one_sequence(running, seq_item):
        current, incoming, length, chosen_two, chosen_three = seq_item

        def forward(start, *params):
            return recursions(start, tuple((narrow_cast(master) for master in params)), length, chosen_two, chosen_three)
        result, pullback = jax.vjp(forward, current, *masters)
        gradients = pullback(incoming)
        running = tuple((summed + gradient for summed, gradient in zip(running, gradients[1:])))
        return (running, (result.astype(jnp.bfloat16), gradients[0]))
    zeros_init = tuple((jnp.zeros(master.shape, jnp.float32) for master in masters))
    running, (results, input_grads) = lax.scan(one_sequence, zeros_init, (states, incoming_all, lengths, chosen_second, chosen_third))
    return (results.reshape(TOKENS, MODEL_WIDTH), input_grads.reshape(TOKENS, MODEL_WIDTH), running[0], running[1], running[2], running[3], running[4], running[5], running[6], running[7], running[8], running[9])
```

```python
from functools import partial

import jax
import jax.numpy as jnp
from jax import lax
from jax.sharding import PartitionSpec as P

QUERY_HEADS = 15
KEY_VALUE_HEADS = 5
HEAD_SIZE = 64


epsilon = 1e-05
negative = -1e30
narrow_dtype = jnp.bfloat16
wide_type = jnp.float32


def rotation(positions):
    half_width = HEAD_SIZE // 2
    frequency = 10000.0 ** (-jnp.arange(half_width, dtype=jnp.float32) / half_width)
    angles = positions.astype(jnp.float32)[:, None] * frequency[None, :]
    return (jnp.cos(angles)[:, None, :], jnp.sin(angles)[:, None, :])


def apply_rotary(value_rows, cosine_table, sine_values):
    half_width = value_rows.shape[-1] // 2
    leading = value_rows[..., :half_width]
    trailing = value_rows[..., half_width:]
    return jnp.concatenate(
        [
            leading * cosine_table - trailing * sine_values,
            trailing * cosine_table + leading * sine_values,
        ],
        axis=-1,
    )


def norm_forward(value_rows, gain):
    inverse = lax.rsqrt(jnp.mean(value_rows * value_rows, axis=-1, keepdims=True) + epsilon)
    return (value_rows * inverse * gain, inverse)


def norm_backward(value_rows, inverse, gain, incoming):
    weighted = incoming * gain
    d_values = inverse * weighted - value_rows * inverse**3 * jnp.mean(
        weighted * value_rows, axis=-1, keepdims=True
    )
    return (d_values, jnp.sum(incoming * value_rows * inverse, axis=0))


def build_mask(count_of_rows, key_valid):
    row_order = jnp.arange(count_of_rows)
    return (row_order[None, :] <= row_order[:, None]) & key_valid[None, :]


def head_forward(pieces, allowed, factor):
    query_rows, rotated_keys, value_rows = pieces
    raw_scores = jnp.einsum(
        "qgd,kd->gqk", query_rows, rotated_keys, preferred_element_type=wide_type
    )
    scores = jnp.where(allowed, raw_scores * factor, negative)
    row_peak = jnp.max(scores, axis=-1, keepdims=True)
    expanded = jnp.exp(scores - row_peak)
    row_total = jnp.sum(expanded, axis=-1, keepdims=True)
    probabilities = (expanded / row_total).astype(narrow_dtype)
    attended = jnp.einsum(
        "gqk,kd->qgd", probabilities, value_rows, preferred_element_type=wide_type
    )
    return (attended, row_peak + jnp.log(row_total))


def head_backward(pieces, allowed, factor):
    query_rows, rotated_keys, value_rows, log_total, attended_gradient = pieces
    raw_scores = jnp.einsum(
        "qgd,kd->gqk", query_rows, rotated_keys, preferred_element_type=wide_type
    )
    scores = jnp.where(allowed, raw_scores * factor, negative)
    probabilities = jnp.exp(scores - log_total)
    d_probs = jnp.einsum(
        "qgd,kd->gqk", attended_gradient, value_rows, preferred_element_type=wide_type
    )
    row_dot = jnp.sum(probabilities * d_probs, axis=-1, keepdims=True)
    d_raw = (probabilities * (d_probs - row_dot) * factor).astype(narrow_dtype)
    d_queries = jnp.einsum("gqk,kd->qgd", d_raw, rotated_keys, preferred_element_type=wide_type)
    d_keys = jnp.einsum("gqk,qgd->kd", d_raw, query_rows, preferred_element_type=wide_type)
    d_values = jnp.einsum(
        "gqk,qgd->kd",
        probabilities.astype(narrow_dtype),
        attended_gradient,
        preferred_element_type=wide_type,
    )
    return (d_queries, d_keys, d_values)


def block_forward(current, positions, key_valid, column, weights):
    gain_attn, gain_ffn, router, w_query, key_weight, value_weight, w_out, w_gate, w_up, w_down = (
        weights
    )
    count_of_rows = current.shape[0]
    group_count = QUERY_HEADS // KEY_VALUE_HEADS
    normalized_input, inv_attn = norm_forward(current, gain_attn.astype(wide_type))
    normed_low = normalized_input.astype(narrow_dtype)
    gating = jax.nn.sigmoid(
        jnp.dot(normed_low, router[:, column], preferred_element_type=wide_type)
    )
    cosine_table, sine_values = rotation(positions)
    query_lin = jnp.dot(normed_low, w_query, preferred_element_type=wide_type).reshape(
        count_of_rows, QUERY_HEADS, HEAD_SIZE
    )
    key_lin = jnp.dot(normed_low, key_weight, preferred_element_type=wide_type).reshape(
        count_of_rows, KEY_VALUE_HEADS, HEAD_SIZE
    )
    query_rows = apply_rotary(query_lin, cosine_table, sine_values).astype(narrow_dtype)
    rotated_keys = apply_rotary(key_lin, cosine_table, sine_values).astype(narrow_dtype)
    value_rows = (
        jnp.dot(normed_low, value_weight, preferred_element_type=wide_type)
        .astype(narrow_dtype)
        .reshape(count_of_rows, KEY_VALUE_HEADS, HEAD_SIZE)
    )
    query_per_head = jnp.moveaxis(
        query_rows.reshape(count_of_rows, KEY_VALUE_HEADS, group_count, HEAD_SIZE), 1, 0
    )
    head_key = jnp.moveaxis(rotated_keys, 1, 0)
    head_value = jnp.moveaxis(value_rows, 1, 0)
    allowed = build_mask(count_of_rows, key_valid)
    attended, log_total = lax.map(
        partial(head_forward, allowed=allowed, factor=HEAD_SIZE ** (-0.5)),
        (query_per_head, head_key, head_value),
    )
    attended_low = (
        jnp.moveaxis(attended, 0, 1)
        .reshape(count_of_rows, QUERY_HEADS * HEAD_SIZE)
        .astype(narrow_dtype)
    )
    attn_out = jnp.dot(attended_low, w_out, preferred_element_type=wide_type)
    after_attn = current + attn_out
    normed_ffn, inv_ffn = norm_forward(after_attn, gain_ffn.astype(wide_type))
    ffn_low = normed_ffn.astype(narrow_dtype)
    gate_proj = jnp.dot(ffn_low, w_gate, preferred_element_type=wide_type)
    up_proj = jnp.dot(ffn_low, w_up, preferred_element_type=wide_type)
    hidden = (jax.nn.silu(gate_proj) * up_proj).astype(narrow_dtype)
    ffn_out = jnp.dot(hidden, w_down, preferred_element_type=wide_type)
    kept = (
        current,
        positions,
        normed_low,
        inv_attn,
        query_per_head,
        head_key,
        head_value,
        log_total,
        attended_low,
        after_attn,
        inv_ffn,
        ffn_low,
        gate_proj,
        up_proj,
        hidden,
        gating,
    )
    return (attn_out + ffn_out, gating, kept)


def block_backward(kept, d_change, d_gating, key_valid, column, weights):
    (
        current,
        positions,
        normed_low,
        inv_attn,
        query_per_head,
        head_key,
        head_value,
        log_total,
        attended_low,
        after_attn,
        inv_ffn,
        ffn_low,
        gate_proj,
        up_proj,
        hidden,
        gating,
    ) = kept
    gain_attn, gain_ffn, router, w_query, key_weight, value_weight, w_out, w_gate, w_up, w_down = (
        weights
    )
    count_of_rows = current.shape[0]
    group_count = QUERY_HEADS // KEY_VALUE_HEADS
    d_ffn = d_change.astype(narrow_dtype)
    d_hidden = jnp.einsum("nd,fd->nf", d_ffn, w_down, preferred_element_type=wide_type)
    sigmoid_gate = jax.nn.sigmoid(gate_proj)
    d_gate_low = (
        d_hidden * up_proj * sigmoid_gate * (1.0 + gate_proj * (1.0 - sigmoid_gate))
    ).astype(narrow_dtype)
    d_up_low = (d_hidden * gate_proj * sigmoid_gate).astype(narrow_dtype)
    d_normed_ffn = jnp.einsum("nf,df->nd", d_gate_low, w_gate, preferred_element_type=wide_type)
    d_normed_ffn = d_normed_ffn + jnp.einsum(
        "nf,df->nd", d_up_low, w_up, preferred_element_type=wide_type
    )
    d_after, grad_gain_ffn = norm_backward(
        after_attn, inv_ffn, gain_ffn.astype(wide_type), d_normed_ffn
    )
    d_attn_low = (d_change + d_after).astype(narrow_dtype)
    attended_gradient = jnp.einsum(
        "nd,ad->na", d_attn_low, w_out, preferred_element_type=wide_type
    ).astype(narrow_dtype)
    head_gradient = jnp.moveaxis(
        attended_gradient.reshape(count_of_rows, KEY_VALUE_HEADS, group_count, HEAD_SIZE), 1, 0
    )
    allowed = build_mask(count_of_rows, key_valid)
    d_query_rot, d_key_rot, value_gradient = lax.map(
        partial(head_backward, allowed=allowed, factor=HEAD_SIZE ** (-0.5)),
        (query_per_head, head_key, head_value, log_total, head_gradient),
    )
    cosine_table, sine_values = rotation(positions)
    d_query_low = (
        apply_rotary(
            jnp.moveaxis(d_query_rot, 0, 1).reshape(count_of_rows, QUERY_HEADS, HEAD_SIZE),
            cosine_table,
            -sine_values,
        )
        .astype(narrow_dtype)
        .reshape(count_of_rows, QUERY_HEADS * HEAD_SIZE)
    )
    d_key_low = (
        apply_rotary(jnp.moveaxis(d_key_rot, 0, 1), cosine_table, -sine_values)
        .astype(narrow_dtype)
        .reshape(count_of_rows, KEY_VALUE_HEADS * HEAD_SIZE)
    )
    value_gradient_narrow = (
        jnp.moveaxis(value_gradient, 0, 1)
        .astype(narrow_dtype)
        .reshape(count_of_rows, KEY_VALUE_HEADS * HEAD_SIZE)
    )
    d_logit = d_gating * gating * (1.0 - gating)
    router_column = router[:, column].astype(wide_type)
    d_normed = jnp.einsum("nh,dh->nd", d_query_low, w_query, preferred_element_type=wide_type)
    d_normed = d_normed + jnp.einsum(
        "nh,dh->nd", d_key_low, key_weight, preferred_element_type=wide_type
    )
    d_normed = d_normed + jnp.einsum(
        "nh,dh->nd", value_gradient_narrow, value_weight, preferred_element_type=wide_type
    )
    d_normed = d_normed + d_logit[:, None] * router_column[None, :]
    router_piece = jnp.dot(d_logit, normed_low, preferred_element_type=wide_type)
    d_input, grad_gain_attn = norm_backward(
        current, inv_attn, gain_attn.astype(wide_type), d_normed
    )
    return (
        d_input + d_after,
        (grad_gain_attn, grad_gain_ffn, router_piece),
        (hidden, d_ffn, ffn_low, d_gate_low, d_up_low, attended_low, d_attn_low, normed_low,
         jnp.concatenate([d_query_low, d_key_low], axis=1), value_gradient_narrow),
    )


def partner(value, axis, bit):
    count = lax.axis_size(axis)
    return lax.ppermute(value, axis, [(i, i ^ bit) for i in range(count)])


def side(axis, bit):
    return (lax.axis_index(axis) // bit) % 2


def take_half(value, axis, bit, dim):
    size = value.shape[dim] // 2
    which = side(axis, bit)
    keep = lax.dynamic_slice_in_dim(value, which * size, size, dim)
    send = lax.dynamic_slice_in_dim(value, (1 - which) * size, size, dim)
    return keep, send


def add_half(value, axis, bit, dim):
    keep, send = take_half(value, axis, bit, dim)
    received = partner(send, axis, bit)
    return (keep.astype(wide_type) + received.astype(wide_type)).astype(narrow_dtype)


def join_half(value, axis, bit, dim):
    received = partner(value, axis, bit)
    first = side(axis, bit) == 0
    return jnp.where(
        first,
        jnp.concatenate([value, received], axis=dim),
        jnp.concatenate([received, value], axis=dim),
    )


def bits_of(axis, low):
    found = []
    bit = low
    while bit < lax.axis_size(axis):
        found.append(bit)
        bit = bit * 2
    return found


def split_steps(row_steps):
    steps = [("dp", 1, 0), ("dp", 2, 0)]
    return steps + [("dp", bit, 0 if row_steps else 1) for bit in bits_of("dp", 4)]


def reduce_matrix(gradient, row_steps):
    owners = lax.axis_size("fsdp")
    rows, columns = gradient.shape
    value = gradient.reshape(owners, rows // owners, columns)
    value = add_half(value, "dp", 1, 1)
    for bit in reversed(bits_of("fsdp", 1)):
        value = add_half(value, "fsdp", bit, 0)
    value = value[0]
    steps = split_steps(row_steps)
    for axis, bit, dim in steps[1:]:
        value = add_half(value, axis, bit, dim)
    for axis, bit, dim in reversed(steps):
        value = join_half(value, axis, bit, dim)
    return value


def place(parts, rows, shape):
    full = jnp.zeros(shape, narrow_dtype)
    for index, part in parts:
        full = lax.dynamic_update_slice_in_dim(full, part, index * rows, 0)
    return full


def gather_near(shard):
    owners = lax.axis_size("fsdp")
    mine = lax.axis_index("fsdp")
    half, _ = take_half(shard, "dp", 1, 0)
    parts = [(mine, shard)]
    for offset in range(1, owners):
        parts.append((mine ^ offset, join_half(partner(half, "fsdp", offset), "dp", 1, 0)))
    return place(parts, shard.shape[0], (shard.shape[0] * owners,) + shard.shape[1:])


def gather_far(shard, row_steps):
    owners = lax.axis_size("fsdp")
    mine = lax.axis_index("fsdp")
    steps = split_steps(row_steps)
    piece = shard
    for axis, bit, dim in steps:
        piece, _ = take_half(piece, axis, bit, dim)
    parts = [(mine, shard)]
    for offset in range(1, owners):
        other = partner(piece, "fsdp", offset)
        for axis, bit, dim in reversed(steps):
            other = join_half(other, axis, bit, dim)
        parts.append((mine ^ offset, other))
    return place(parts, shard.shape[0], (shard.shape[0] * owners,) + shard.shape[1:])


def local(
    hidden_in,
    cotangent,
    norm_attn,
    norm_ffn,
    router,
    w_query,
    key_weight,
    value_weight,
    w_out,
    w_gate,
    w_up,
    w_down,
    lengths,
    chosen_second,
    chosen_third,
):
    owners = lax.axis_size("fsdp")
    mine = lax.axis_index("fsdp")
    small = jnp.concatenate(
        [norm_attn[None, :], norm_ffn[None, :], router.T, jnp.zeros((11, norm_attn.shape[0]), wide_type)]
    ).astype(narrow_dtype)
    small_parts = [(mine, small)] + [
        (mine ^ offset, partner(small, "fsdp", offset)) for offset in range(1, owners)
    ]
    small_rows = jnp.zeros((16, owners * small.shape[1]), narrow_dtype)
    for index, part in small_parts:
        small_rows = lax.dynamic_update_slice_in_dim(small_rows, part, index * small.shape[1], 1)
    width = w_query.shape[1]
    kv_width = key_weight.shape[1]
    attn_shard = jnp.concatenate([w_query, key_weight, w_out, value_weight], axis=1).astype(narrow_dtype)
    attn_full = gather_near(attn_shard)
    gate_full = gather_far(w_gate.astype(narrow_dtype), False)
    up_full = gather_far(w_up.astype(narrow_dtype), False)
    down_full = gather_far(w_down.astype(narrow_dtype), True)
    weights = (
        small_rows[0],
        small_rows[1],
        small_rows[2:5].T,
        attn_full[:, :width],
        attn_full[:, width : width + kv_width],
        attn_full[:, 2 * width + kv_width :],
        attn_full[:, width + kv_width : 2 * width + kv_width],
        gate_full,
        up_full,
        down_full,
    )
    token_count = hidden_in.shape[0]
    positions = jnp.arange(token_count, dtype=jnp.int32)
    valid = positions < lengths[0]
    chosen_two = chosen_second[0]
    chosen_three = chosen_third[0]
    every_two = jnp.ones(chosen_two.shape, jnp.bool_)
    every_three = jnp.ones(chosen_three.shape, jnp.bool_)
    start = hidden_in.astype(wide_type)
    change_one, gating_one, kept_one = block_forward(start, positions, valid, 0, weights)
    scale_one = jnp.where(valid, gating_one, 0.0)
    state_one = start + scale_one[:, None] * change_one
    picked_two = jnp.take(state_one, chosen_two, axis=0)
    change_two, gating_two, kept_two = block_forward(picked_two, chosen_two, every_two, 1, weights)
    state_two = state_one.at[chosen_two].set(picked_two + gating_two[:, None] * change_two)
    picked_three = jnp.take(state_two, chosen_three, axis=0)
    change_three, gating_three, kept_three = block_forward(
        picked_three, chosen_three, every_three, 2, weights
    )
    state_three = state_two.at[chosen_three].set(
        picked_three + gating_three[:, None] * change_three
    )
    hidden_out = state_three.astype(narrow_dtype)
    incoming = cotangent.astype(wide_type)
    d_picked = jnp.take(incoming, chosen_three, axis=0)
    d_inner, small_three, factors_three = block_backward(
        kept_three,
        gating_three[:, None] * d_picked,
        jnp.sum(change_three * d_picked, axis=-1),
        every_three,
        2,
        weights,
    )
    incoming = incoming.at[chosen_three].set(d_picked + d_inner)
    d_picked = jnp.take(incoming, chosen_two, axis=0)
    d_inner, small_two, factors_two = block_backward(
        kept_two,
        gating_two[:, None] * d_picked,
        jnp.sum(change_two * d_picked, axis=-1),
        every_two,
        1,
        weights,
    )
    incoming = incoming.at[chosen_two].set(d_picked + d_inner)
    d_inner, small_one, factors_one = block_backward(
        kept_one,
        scale_one[:, None] * incoming,
        jnp.where(valid, jnp.sum(change_one * incoming, axis=-1), 0.0),
        valid,
        0,
        weights,
    )
    grad_hidden = incoming + d_inner
    hidden, d_ffn, ffn_low, d_gate, d_up, attended, d_attn, normed, d_qk, d_v = (
        jnp.concatenate(rows, axis=0) for rows in zip(factors_one, factors_two, factors_three)
    )

    def outer(left, right):
        return jnp.einsum("na,nb->ab", left, right, preferred_element_type=wide_type).astype(narrow_dtype)

    down_shard = reduce_matrix(outer(hidden, d_ffn), True).astype(wide_type)
    gate_shard = reduce_matrix(outer(ffn_low, d_gate), False).astype(wide_type)
    up_shard = reduce_matrix(outer(ffn_low, d_up), False).astype(wide_type)
    attn_grad = jnp.concatenate([outer(normed, d_qk), outer(attended, d_attn), outer(normed, d_v)], axis=1)
    attn_out_shard = reduce_matrix(attn_grad, False).astype(wide_type)
    small_grads = jnp.stack(
        [
            small_one[0] + small_two[0] + small_three[0],
            small_one[1] + small_two[1] + small_three[1],
            small_one[2],
            small_two[2],
            small_three[2],
        ]
        + [jnp.zeros_like(small_one[0])] * 3
    )
    small_sum = lax.psum(small_grads, ("dp", "fsdp"))
    small_sum = lax.dynamic_slice_in_dim(small_sum, mine * small.shape[1], small.shape[1], 1)
    return (
        hidden_out,
        grad_hidden,
        small_sum[0],
        small_sum[1],
        small_sum[2:5].T,
        attn_out_shard[:, :width],
        attn_out_shard[:, width : width + kv_width],
        attn_out_shard[:, 2 * width + kv_width :],
        attn_out_shard[:, width + kv_width : 2 * width + kv_width],
        gate_shard,
        up_shard,
        down_shard,
    )


def solution(mesh):
    in_specs = (
        P(("dp", "fsdp"), None),
        P(("dp", "fsdp"), None),
        P("fsdp"),
        P("fsdp"),
        P("fsdp", None),
        P("fsdp", None),
        P("fsdp", None),
        P("fsdp", None),
        P("fsdp", None),
        P("fsdp", None),
        P("fsdp", None),
        P("fsdp", None),
        P(("dp", "fsdp")),
        P(("dp", "fsdp"), None),
        P(("dp", "fsdp"), None),
    )
    out_specs = (
        P(("dp", "fsdp"), None),
        P(("dp", "fsdp"), None),
        P("fsdp"),
        P("fsdp"),
        P("fsdp", None),
        P("fsdp", None),
        P("fsdp", None),
        P("fsdp", None),
        P("fsdp", None),
        P("fsdp", None),
        P("fsdp", None),
        P("fsdp", None),
    )
    return jax.shard_map(local, mesh=mesh, in_specs=in_specs, out_specs=out_specs, check_vma=False)
```

```python
from functools import partial

import jax
import jax.numpy as jnp
from jax import lax
from jax.experimental import pallas as pl
from jax.experimental.pallas import tpu as pltpu
from jax.sharding import PartitionSpec as P

QUERY_HEADS = 15
KEY_VALUE_HEADS = 5
HEAD_SIZE = 64
GROUP = QUERY_HEADS // KEY_VALUE_HEADS
MODEL = QUERY_HEADS * HEAD_SIZE
QK_WIDTH = (QUERY_HEADS + KEY_VALUE_HEADS) * HEAD_SIZE
V_START = QK_WIDTH + MODEL - HEAD_SIZE
V_HEAD = 1
SCALE = HEAD_SIZE ** (-0.5)
CHUNK = 512
VMEM_LIMIT = 60 * 2**20

epsilon = 1e-05
negative = -1e30
narrow_dtype = jnp.bfloat16
wide_type = jnp.float32


def rows_dot(left, right):
    return lax.dot_general(left, right, (((1,), (0,)), ((), ())), preferred_element_type=wide_type)


def rows_dot_t(left, right):
    return lax.dot_general(left, right, (((1,), (1,)), ((), ())), preferred_element_type=wide_type)


def columns_dot(left, right):
    return lax.dot_general(left, right, (((0,), (0,)), ((), ())), preferred_element_type=wide_type)


def inverse_rms(rows):
    return lax.rsqrt(jnp.mean(rows * rows, axis=-1, keepdims=True) + epsilon)


def norm_back(rows, inverse, gain, incoming):
    weighted = incoming * gain
    mean = jnp.mean(weighted * rows, axis=-1, keepdims=True)
    d_rows = inverse * weighted - rows * (inverse * inverse * inverse * mean)
    return d_rows, jnp.sum(incoming * rows * inverse, axis=0, keepdims=True)


def rotate(block, cosines, sines):
    lanes = lax.broadcasted_iota(jnp.int32, block.shape, 1)
    swapped = jnp.where(lanes % HEAD_SIZE < HEAD_SIZE // 2, pltpu.roll(block, 96, 1), pltpu.roll(block, 32, 1))
    return block * cosines + swapped * sines


def causal_bias(count, length):
    row = lax.broadcasted_iota(jnp.int32, (count, count), 0)
    column = lax.broadcasted_iota(jnp.int32, (count, count), 1)
    allowed = column <= row
    if length is not None:
        allowed = allowed & (column < length)
    bias = jnp.where(allowed, 0.0, negative)
    return jnp.concatenate([bias] * GROUP, axis=0)


def head_columns(ref, first, count):
    return jnp.concatenate(
        [ref[:, (first + i) * HEAD_SIZE : (first + i + 1) * HEAD_SIZE] for i in range(count)], axis=0
    )


def attention_forward(rows, gain, router_row, cosines, sines, bias, weight, normed_ref, qk_ref, v_ref, att_ref, log_ref):
    count = rows.shape[0]
    normed_ref[...] = (rows * inverse_rms(rows) * gain).astype(narrow_dtype)
    normed = normed_ref[...]
    gating = jax.nn.sigmoid(jnp.sum(normed.astype(wide_type) * router_row, axis=-1, keepdims=True))
    for block in range(QK_WIDTH // 256):
        product = rows_dot(normed, weight[:, block * 256 : (block + 1) * 256])
        for part in range(2):
            piece = rotate(product[:, part * 128 : (part + 1) * 128], cosines, sines)
            at = block * 256 + part * 128
            qk_ref[:, at : at + 128] = piece.astype(narrow_dtype)
    v_ref[...] = rows_dot(normed, weight[:, V_START:]).astype(narrow_dtype)
    for head in range(KEY_VALUE_HEADS):
        queries = head_columns(qk_ref, head * GROUP, GROUP)
        keys = head_columns(qk_ref, QUERY_HEADS + head, 1)
        values = head_columns(v_ref, V_HEAD + head, 1)
        scores = rows_dot_t(queries, keys) * SCALE + bias
        peak = jnp.max(scores, axis=-1, keepdims=True)
        expanded = jnp.exp(scores - peak)
        total = jnp.sum(expanded, axis=-1, keepdims=True)
        log_ref[:, head : head + 1] = peak + jnp.log(total)
        attended = rows_dot((expanded / total).astype(narrow_dtype), values).astype(narrow_dtype)
        for i in range(GROUP):
            at = (head * GROUP + i) * HEAD_SIZE
            att_ref[:, at : at + HEAD_SIZE] = attended[i * count : (i + 1) * count]
    return rows_dot(att_ref[...], weight[:, QK_WIDTH : QK_WIDTH + MODEL]), gating


def attention_backward(
    rows, gain, router_row, cosines, sines, bias, weight, normed_ref, qk_ref, v_ref, log_ref,
    d_attn_low, d_gating, gating, d_att_ref, d_raw_ref, d_qk_ref, d_v_ref,
):
    count = rows.shape[0]
    d_att_ref[...] = rows_dot_t(d_attn_low, weight[:, QK_WIDTH : QK_WIDTH + MODEL]).astype(narrow_dtype)
    d_v_ref[...] = jnp.zeros_like(d_v_ref)
    for head in range(KEY_VALUE_HEADS):
        queries = head_columns(qk_ref, head * GROUP, GROUP)
        keys = head_columns(qk_ref, QUERY_HEADS + head, 1)
        values = head_columns(v_ref, V_HEAD + head, 1)
        d_attended = head_columns(d_att_ref, head * GROUP, GROUP)
        scores = rows_dot_t(queries, keys) * SCALE + bias
        probabilities = jnp.exp(scores - log_ref[:, head : head + 1])
        d_probs = rows_dot_t(d_attended, values)
        row_dot = jnp.sum(probabilities * d_probs, axis=-1, keepdims=True)
        d_raw = (probabilities * (d_probs - row_dot) * SCALE).astype(narrow_dtype)
        d_queries = rows_dot(d_raw, keys)
        for i in range(GROUP):
            at = (head * GROUP + i) * HEAD_SIZE
            d_raw_ref[:, at : at + HEAD_SIZE] = d_queries[i * count : (i + 1) * count]
        at = (QUERY_HEADS + head) * HEAD_SIZE
        d_raw_ref[:, at : at + HEAD_SIZE] = columns_dot(queries, d_raw).T
        at = (V_HEAD + head) * HEAD_SIZE
        d_values = columns_dot(d_attended, probabilities.astype(narrow_dtype)).T
        d_v_ref[:, at : at + HEAD_SIZE] = d_values.astype(narrow_dtype)
    for block in range(QK_WIDTH // 128):
        at = block * 128
        d_qk_ref[:, at : at + 128] = rotate(d_raw_ref[:, at : at + 128], cosines, -sines).astype(narrow_dtype)
    d_normed = rows_dot_t(d_qk_ref[...], weight[:, :QK_WIDTH]) + rows_dot_t(d_v_ref[...], weight[:, V_START:])
    d_logit = d_gating * gating * (1.0 - gating)
    d_normed = d_normed + d_logit * router_row
    router_gradient = jnp.sum(d_logit * normed_ref[...].astype(wide_type), axis=0, keepdims=True)
    d_rows, gain_gradient = norm_back(rows, inverse_rms(rows), gain, d_normed)
    return d_rows, gain_gradient, router_gradient


def ffn_forward(after, gain, w_gate, w_up, w_down, ffn_ref, gate_ref, up_ref, hidden_ref, total_ref, chunk):
    ffn_ref[...] = (after * inverse_rms(after) * gain).astype(narrow_dtype)
    total_ref[...] = jnp.zeros_like(total_ref)

    def step(index, carry):
        columns = pl.ds(pl.multiple_of(index * chunk, chunk), chunk)
        gate = rows_dot(ffn_ref[...], w_gate[:, columns])
        up = rows_dot(ffn_ref[...], w_up[:, columns])
        gate_ref[:, columns] = gate
        up_ref[:, columns] = up
        hidden = (gate * jax.nn.sigmoid(gate) * up).astype(narrow_dtype)
        hidden_ref[:, columns] = hidden
        total_ref[...] += rows_dot(hidden, w_down[columns, :])
        return carry

    lax.fori_loop(0, gate_ref.shape[1] // chunk, step, 0)


def ffn_backward(after, gain, w_gate, w_up, w_down, d_ffn_ref, gate_ref, up_ref, d_gate_ref, d_up_ref, total_ref, chunk):
    total_ref[...] = jnp.zeros_like(total_ref)

    def step(index, carry):
        columns = pl.ds(pl.multiple_of(index * chunk, chunk), chunk)
        d_hidden = rows_dot_t(d_ffn_ref[...], w_down[columns, :])
        gate = gate_ref[:, columns]
        sig = jax.nn.sigmoid(gate)
        d_gate = (d_hidden * up_ref[:, columns] * sig * (1.0 + gate * (1.0 - sig))).astype(narrow_dtype)
        d_up = (d_hidden * gate * sig).astype(narrow_dtype)
        d_gate_ref[:, columns] = d_gate
        d_up_ref[:, columns] = d_up
        total_ref[...] += rows_dot_t(d_gate, w_gate[:, columns]) + rows_dot_t(d_up, w_up[:, columns])
        return carry

    lax.fori_loop(0, gate_ref.shape[1] // chunk, step, 0)
    return norm_back(after, inverse_rms(after), gain, total_ref[...])


def pick_exact(selector, rows):
    high = rows.astype(narrow_dtype)
    rest = rows - high.astype(wide_type)
    middle = rest.astype(narrow_dtype)
    low = (rest - middle.astype(wide_type)).astype(narrow_dtype)
    return rows_dot(selector, high) + rows_dot(selector, middle) + rows_dot(selector, low)


def first_attention_kernel(
    length_ref, hidden_in, small, cosines, sines, weight, normed_ref, qk_ref, v_ref, att_ref, log_ref, out_ref, gating_ref
):
    rows = hidden_in[...].astype(wide_type)
    bias = causal_bias(rows.shape[0], length_ref[0])
    attn_out, gating = attention_forward(
        rows, small[0:1], small[2:3], cosines[...], sines[...], bias, weight, normed_ref, qk_ref, v_ref, att_ref, log_ref
    )
    out_ref[...] = attn_out
    gating_ref[...] = jnp.broadcast_to(gating, gating_ref.shape)


def last_attention_kernel(
    length_ref, hidden_in, small, cosines, sines, weight, normed_ref, qk_ref, v_ref, log_ref, gating_ref, d_gating_ref,
    d_attn_ref, d_input_ref, d_qk_ref, d_v_ref, grad_hidden_ref, small_out, d_att_ref, d_raw_ref,
):
    rows = hidden_in[...].astype(wide_type)
    bias = causal_bias(rows.shape[0], length_ref[0])
    d_rows, gain_gradient, router_gradient = attention_backward(
        rows, small[0:1], small[2:3], cosines[...], sines[...], bias, weight, normed_ref, qk_ref, v_ref, log_ref,
        d_attn_ref[...], d_gating_ref[:, 0:1], gating_ref[:, 0:1], d_att_ref, d_raw_ref, d_qk_ref, d_v_ref,
    )
    grad_hidden_ref[...] = d_input_ref[...] + d_rows
    small_out[...] = jnp.zeros_like(small_out)
    small_out[0:1] = gain_gradient
    small_out[2:3] = router_gradient


def middle_kernel(
    length_ref, hidden_in, cotangent, small, attn_out_ref, gating_ref, cos_two, sin_two, cos_three, sin_three,
    column_two, row_two, column_three, row_three, w_attn_hbm, w_gate_hbm, w_up_hbm, w_down_hbm,
    hidden_out, d_input_ref, d_gating_ref, small_out,
    hidden_one, d_ffn_one, ffn_one, d_gate_one, d_up_one, d_attn_one,
    hidden_in_r, d_ffn_in_r, ffn_in_r, d_gate_in_r, d_up_in_r, d_attn_in_r, att_in_r, normed_in_r, d_qk_in_r, d_v_in_r,
    w_attn, w_gate, w_up, w_down, sems,
    gate_one, up_one, gate_two, up_two, gate_three, up_three, total_one, total_two, total_three,
    qk_two, v_two, log_two, qk_three, v_three, log_three, d_att_two, d_raw_two, d_att_three, d_raw_three,
):
    copies = [
        pltpu.make_async_copy(source, target, sems.at[i])
        for i, (source, target) in enumerate(
            ((w_gate_hbm, w_gate), (w_up_hbm, w_up), (w_down_hbm, w_down), (w_attn_hbm, w_attn))
        )
    ]
    for copy in copies:
        copy.start()
    count_two, count_three = column_two.shape[0], column_three.shape[0]
    count_one = hidden_in.shape[0]
    two = pl.ds(0, count_two)
    three = pl.ds(count_two, count_three)
    gain_attn, gain_ffn = small[0:1], small[1:2]

    def selector(shape, hit):
        return jnp.where(hit, 1.0, 0.0).astype(narrow_dtype)

    pick_two = selector(
        None, lax.broadcasted_iota(jnp.int32, (count_two, count_one), 1) == column_two[...]
    )
    put_two = selector(None, lax.broadcasted_iota(jnp.int32, (count_one, count_two), 0) == row_two[...])
    pick_three = selector(None, column_three[...] == row_two[...])
    put_three = selector(None, column_two[...] == row_three[...])

    after_one = hidden_in[...].astype(wide_type) + attn_out_ref[...]
    for copy in copies[:3]:
        copy.wait()
    ffn_forward(after_one, gain_ffn, w_gate, w_up, w_down, ffn_one, gate_one, up_one, hidden_one, total_one, CHUNK)
    valid = lax.broadcasted_iota(jnp.int32, (count_one, 1), 0) < length_ref[0]
    scale_one = jnp.where(valid, gating_ref[:, 0:1], 0.0)
    change_one = attn_out_ref[...] + total_one[...]
    d_input_ref[...] = hidden_in[...].astype(wide_type) + scale_one * change_one
    total_one[...] = change_one

    copies[3].wait()
    state_two = pick_exact(pick_two, d_input_ref[...])
    bias_two = causal_bias(count_two, None)
    attn_two, gating_two = attention_forward(
        state_two, gain_attn, small[3:4], cos_two[...], sin_two[...], bias_two, w_attn,
        normed_in_r.at[two], qk_two, v_two, att_in_r.at[two], log_two,
    )
    after_two = state_two + attn_two
    ffn_forward(
        after_two, gain_ffn, w_gate, w_up, w_down, ffn_in_r.at[two], gate_two, up_two, hidden_in_r.at[two], total_two, CHUNK
    )
    change_two = attn_two + total_two[...]
    delta_two = gating_two * change_two

    state_three = pick_exact(pick_three, state_two + delta_two)
    bias_three = causal_bias(count_three, None)
    attn_three, gating_three = attention_forward(
        state_three, gain_attn, small[4:5], cos_three[...], sin_three[...], bias_three, w_attn,
        normed_in_r.at[three], qk_three, v_three, att_in_r.at[three], log_three,
    )
    after_three = state_three + attn_three
    ffn_forward(
        after_three, gain_ffn, w_gate, w_up, w_down, ffn_in_r.at[three], gate_three, up_three,
        hidden_in_r.at[three], total_three, CHUNK,
    )
    change_three = attn_three + total_three[...]
    added = delta_two + pick_exact(put_three, gating_three * change_three)
    hidden_out[...] = (d_input_ref[...] + pick_exact(put_two, added)).astype(narrow_dtype)

    incoming_two = rows_dot(pick_two, cotangent[...])
    incoming_three = rows_dot(pick_three, incoming_two.astype(narrow_dtype))
    d_change = gating_three * incoming_three
    d_gating = jnp.sum(change_three * incoming_three, axis=-1, keepdims=True)
    d_ffn_in_r[three] = d_change.astype(narrow_dtype)
    d_after, gain_ffn_three = ffn_backward(
        after_three, gain_ffn, w_gate, w_up, w_down, d_ffn_in_r.at[three], gate_three, up_three,
        d_gate_in_r.at[three], d_up_in_r.at[three], total_three, CHUNK,
    )
    d_attn_in_r[three] = (d_change + d_after).astype(narrow_dtype)
    d_rows, gain_attn_three, router_three = attention_backward(
        state_three, gain_attn, small[4:5], cos_three[...], sin_three[...], bias_three, w_attn, normed_in_r.at[three],
        qk_three, v_three, log_three, d_attn_in_r[three], d_gating, gating_three, d_att_three, d_raw_three,
        d_qk_in_r.at[three], d_v_in_r.at[three],
    )
    back_three = pick_exact(put_three, d_rows + d_after)

    incoming_two = incoming_two + back_three
    d_change = gating_two * incoming_two
    d_gating = jnp.sum(change_two * incoming_two, axis=-1, keepdims=True)
    d_ffn_in_r[two] = d_change.astype(narrow_dtype)
    d_after, gain_ffn_two = ffn_backward(
        after_two, gain_ffn, w_gate, w_up, w_down, d_ffn_in_r.at[two], gate_two, up_two,
        d_gate_in_r.at[two], d_up_in_r.at[two], total_two, CHUNK,
    )
    d_attn_in_r[two] = (d_change + d_after).astype(narrow_dtype)
    d_rows, gain_attn_two, router_two = attention_backward(
        state_two, gain_attn, small[3:4], cos_two[...], sin_two[...], bias_two, w_attn, normed_in_r.at[two],
        qk_two, v_two, log_two, d_attn_in_r[two], d_gating, gating_two, d_att_two, d_raw_two,
        d_qk_in_r.at[two], d_v_in_r.at[two],
    )
    back_two = back_three + d_rows + d_after

    incoming = cotangent[...].astype(wide_type) + pick_exact(put_two, back_two)
    d_input_ref[...] = incoming
    d_change = scale_one * incoming
    d_gating = jnp.where(valid, jnp.sum(total_one[...] * incoming, axis=-1, keepdims=True), 0.0)
    d_gating_ref[...] = jnp.broadcast_to(d_gating, d_gating_ref.shape)
    d_ffn_one[...] = d_change.astype(narrow_dtype)
    after_one = hidden_in[...].astype(wide_type) + attn_out_ref[...]
    d_after, gain_ffn_one = ffn_backward(
        after_one, gain_ffn, w_gate, w_up, w_down, d_ffn_one, gate_one, up_one, d_gate_one, d_up_one, total_one, CHUNK
    )
    d_attn_one[...] = (scale_one * d_input_ref[...] + d_after).astype(narrow_dtype)
    d_input_ref[...] += d_after
    small_out[...] = jnp.zeros_like(small_out)
    small_out[0:1] = gain_attn_two + gain_attn_three
    small_out[1:2] = gain_ffn_one + gain_ffn_two + gain_ffn_three
    small_out[3:4] = router_two
    small_out[4:5] = router_three


def rotary_tables(positions):
    half = HEAD_SIZE // 2
    lanes = jnp.arange(2 * HEAD_SIZE)
    frequency = 10000.0 ** (-(lanes % half).astype(wide_type) / half)
    angles = positions.astype(wide_type)[:, None] * frequency[None, :]
    sign = jnp.where(lanes % HEAD_SIZE < half, -1.0, 1.0)
    return jnp.cos(angles), jnp.sin(angles) * sign[None, :]


def call(kernel, operands, outputs, scratch=(), hbm=(), scalars=1, flops=0):
    specs = [
        pl.BlockSpec(memory_space=pltpu.SMEM if i < scalars else (pl.ANY if i in hbm else pltpu.VMEM))
        for i in range(len(operands))
    ]
    return pl.pallas_call(
        kernel,
        out_shape=[jax.ShapeDtypeStruct(shape, kind) for shape, kind in outputs],
        in_specs=specs,
        out_specs=[pl.BlockSpec(memory_space=pltpu.VMEM)] * len(outputs),
        scratch_shapes=list(scratch),
        compiler_params=pltpu.CompilerParams(vmem_limit_bytes=VMEM_LIMIT),
        cost_estimate=pl.CostEstimate(flops=flops, bytes_accessed=flops // 400, transcendentals=0),
    )(*operands)


def partner(value, axis, bit):
    count = lax.axis_size(axis)
    return lax.ppermute(value, axis, [(i, i ^ bit) for i in range(count)])


def side(axis, bit):
    return (lax.axis_index(axis) // bit) % 2


def take_half(value, axis, bit, dim):
    size = value.shape[dim] // 2
    which = side(axis, bit)
    keep = lax.dynamic_slice_in_dim(value, which * size, size, dim)
    send = lax.dynamic_slice_in_dim(value, (1 - which) * size, size, dim)
    return keep, send


def add_half(value, axis, bit, dim):
    keep, send = take_half(value, axis, bit, dim)
    received = partner(send, axis, bit)
    return (keep.astype(wide_type) + received.astype(wide_type)).astype(narrow_dtype)


def join_half(value, axis, bit, dim):
    received = partner(value, axis, bit)
    first = side(axis, bit) == 0
    return jnp.where(
        first,
        jnp.concatenate([value, received], axis=dim),
        jnp.concatenate([received, value], axis=dim),
    )


def bits_of(axis, low):
    found = []
    bit = low
    while bit < lax.axis_size(axis):
        found.append(bit)
        bit = bit * 2
    return found


def split_steps(row_steps):
    steps = [("dp", 1, 0), ("dp", 2, 0)]
    return steps + [("dp", bit, 0 if row_steps else 1) for bit in bits_of("dp", 4)]


def reduce_matrix(gradient, row_steps):
    owners = lax.axis_size("fsdp")
    rows, columns = gradient.shape
    value = gradient.reshape(owners, rows // owners, columns)
    value = add_half(value, "dp", 1, 1)
    for bit in reversed(bits_of("fsdp", 1)):
        value = add_half(value, "fsdp", bit, 0)
    value = value[0]
    steps = split_steps(row_steps)
    for axis, bit, dim in steps[1:]:
        value = add_half(value, axis, bit, dim)
    for axis, bit, dim in reversed(steps):
        value = join_half(value, axis, bit, dim)
    return value


def place(parts, rows, shape):
    full = jnp.zeros(shape, narrow_dtype)
    for index, part in parts:
        full = lax.dynamic_update_slice_in_dim(full, part, index * rows, 0)
    return full


def gather_near(shard):
    owners = lax.axis_size("fsdp")
    mine = lax.axis_index("fsdp")
    half, _ = take_half(shard, "dp", 1, 0)
    parts = [(mine, shard)]
    for offset in range(1, owners):
        parts.append((mine ^ offset, join_half(partner(half, "fsdp", offset), "dp", 1, 0)))
    return place(parts, shard.shape[0], (shard.shape[0] * owners,) + shard.shape[1:])


def gather_far(shard, row_steps):
    owners = lax.axis_size("fsdp")
    mine = lax.axis_index("fsdp")
    steps = split_steps(row_steps)
    piece = shard
    for axis, bit, dim in steps:
        piece, _ = take_half(piece, axis, bit, dim)
    parts = [(mine, shard)]
    for offset in range(1, owners):
        other = partner(piece, "fsdp", offset)
        for axis, bit, dim in reversed(steps):
            other = join_half(other, axis, bit, dim)
        parts.append((mine ^ offset, other))
    return place(parts, shard.shape[0], (shard.shape[0] * owners,) + shard.shape[1:])


def local(
    hidden_in,
    cotangent,
    norm_attn,
    norm_ffn,
    router,
    w_query,
    key_weight,
    value_weight,
    w_out,
    w_gate,
    w_up,
    w_down,
    lengths,
    chosen_second,
    chosen_third,
):
    owners = lax.axis_size("fsdp")
    mine = lax.axis_index("fsdp")
    small = jnp.concatenate(
        [norm_attn[None, :], norm_ffn[None, :], router.T, jnp.zeros((11, norm_attn.shape[0]), wide_type)]
    ).astype(narrow_dtype)
    small_parts = [(mine, small)] + [
        (mine ^ offset, partner(small, "fsdp", offset)) for offset in range(1, owners)
    ]
    small_rows = jnp.zeros((16, owners * small.shape[1]), narrow_dtype)
    for index, part in small_parts:
        small_rows = lax.dynamic_update_slice_in_dim(small_rows, part, index * small.shape[1], 1)
    width = w_query.shape[1]
    kv_width = key_weight.shape[1]
    attn_shard = jnp.concatenate([w_query, key_weight, w_out, value_weight], axis=1).astype(narrow_dtype)
    attn_full = gather_near(attn_shard)
    gate_full = gather_far(w_gate.astype(narrow_dtype), False)
    up_full = gather_far(w_up.astype(narrow_dtype), False)
    down_full = gather_far(w_down.astype(narrow_dtype), True)
    small_wide = small_rows[:8].astype(wide_type)
    count_one, model = hidden_in.shape
    ff = gate_full.shape[1]
    chosen_two, chosen_three = chosen_second[0], chosen_third[0]
    count_two, count_three = chosen_two.shape[0], chosen_three.shape[0]
    count_rest = count_two + count_three
    cos_one, sin_one = rotary_tables(jnp.arange(count_one))
    cos_two, sin_two = rotary_tables(chosen_two)
    cos_three, sin_three = rotary_tables(chosen_three)
    v_width = attn_full.shape[1] - V_START

    normed_one, qk_one, v_one, att_one, log_one, attn_out_one, gating_one = call(
        first_attention_kernel,
        (lengths, hidden_in, small_wide, cos_one, sin_one, attn_full),
        [
            ((count_one, model), narrow_dtype),
            ((count_one, QK_WIDTH), narrow_dtype),
            ((count_one, v_width), narrow_dtype),
            ((count_one, model), narrow_dtype),
            ((GROUP * count_one, 128), wide_type),
            ((count_one, model), wide_type),
            ((count_one, 128), wide_type),
        ],
    )
    rest = lambda width: ((count_rest, width), narrow_dtype)
    first = lambda width: ((count_one, width), narrow_dtype)
    scratch_for = lambda count: [
        pltpu.VMEM((count, QK_WIDTH), narrow_dtype),
        pltpu.VMEM((count, v_width), narrow_dtype),
        pltpu.VMEM((GROUP * count, 128), wide_type),
    ]
    back_scratch = lambda count: [
        pltpu.VMEM((count, model), narrow_dtype),
        pltpu.VMEM((count, QK_WIDTH), wide_type),
    ]
    wide = lambda count, width: pltpu.VMEM((count, width), wide_type)
    (
        hidden_out, d_input, d_gating_one, small_middle,
        hidden_one, d_ffn_one, ffn_one, d_gate_one, d_up_one, d_attn_one,
        hidden_r, d_ffn_r, ffn_r, d_gate_r, d_up_r, d_attn_r, att_r, normed_r, d_qk_r, d_v_r,
    ) = call(
        middle_kernel,
        (
            lengths, hidden_in, cotangent, small_wide, attn_out_one, gating_one, cos_two, sin_two, cos_three, sin_three,
            chosen_two[:, None], chosen_two[None, :], chosen_three[:, None], chosen_three[None, :],
            attn_full, gate_full, up_full, down_full,
        ),
        [
            first(model), ((count_one, model), wide_type), ((count_one, 128), wide_type), ((8, model), wide_type),
            first(ff), first(model), first(model), first(ff), first(ff), first(model),
            rest(ff), rest(model), rest(model), rest(ff), rest(ff), rest(model), rest(model), rest(model),
            rest(QK_WIDTH), rest(v_width),
        ],
        [
            pltpu.VMEM(attn_full.shape, narrow_dtype),
            pltpu.VMEM(gate_full.shape, narrow_dtype),
            pltpu.VMEM(up_full.shape, narrow_dtype),
            pltpu.VMEM(down_full.shape, narrow_dtype),
            pltpu.SemaphoreType.DMA((4,)),
            wide(count_one, ff), wide(count_one, ff), wide(count_two, ff), wide(count_two, ff),
            wide(count_three, ff), wide(count_three, ff),
            wide(count_one, model), wide(count_two, model), wide(count_three, model),
        ]
        + scratch_for(count_two) + scratch_for(count_three) + back_scratch(count_two) + back_scratch(count_three),
        hbm=(14, 15, 16, 17),
    )
    d_qk_one, d_v_one, grad_hidden, small_last = call(
        last_attention_kernel,
        (
            lengths, hidden_in, small_wide, cos_one, sin_one, attn_full, normed_one, qk_one, v_one, log_one, gating_one,
            d_gating_one, d_attn_one, d_input,
        ),
        [
            first(QK_WIDTH), first(v_width), ((count_one, model), wide_type), ((8, model), wide_type),
        ],
        back_scratch(count_one),
    )

    def outer(left, left_r, right, right_r):
        left = jnp.concatenate([left, left_r])
        right = jnp.concatenate([right, right_r])
        return jnp.einsum("na,nb->ab", left, right, preferred_element_type=wide_type).astype(narrow_dtype)

    down_shard = reduce_matrix(outer(hidden_one, hidden_r, d_ffn_one, d_ffn_r), True).astype(wide_type)
    gate_shard = reduce_matrix(outer(ffn_one, ffn_r, d_gate_one, d_gate_r), False).astype(wide_type)
    up_shard = reduce_matrix(outer(ffn_one, ffn_r, d_up_one, d_up_r), False).astype(wide_type)
    skip = V_HEAD * HEAD_SIZE
    attn_grad = jnp.concatenate(
        [
            outer(normed_one, normed_r, d_qk_one, d_qk_r),
            outer(att_one, att_r, d_attn_one, d_attn_r),
            outer(normed_one, normed_r, d_v_one[:, skip:], d_v_r[:, skip:]),
        ],
        axis=1,
    )
    attn_out_shard = reduce_matrix(attn_grad, False).astype(wide_type)
    small_sum = lax.psum(small_middle + small_last, ("dp", "fsdp"))
    small_sum = lax.dynamic_slice_in_dim(small_sum, mine * small.shape[1], small.shape[1], 1)
    return (
        hidden_out,
        grad_hidden,
        small_sum[0],
        small_sum[1],
        small_sum[2:5].T,
        attn_out_shard[:, :width],
        attn_out_shard[:, width : width + kv_width],
        attn_out_shard[:, 2 * width + kv_width :],
        attn_out_shard[:, width + kv_width : 2 * width + kv_width],
        gate_shard,
        up_shard,
        down_shard,
    )


def solution(mesh):
    in_specs = (
        P(("dp", "fsdp"), None),
        P(("dp", "fsdp"), None),
        P("fsdp"),
        P("fsdp"),
        P("fsdp", None),
        P("fsdp", None),
        P("fsdp", None),
        P("fsdp", None),
        P("fsdp", None),
        P("fsdp", None),
        P("fsdp", None),
        P("fsdp", None),
        P(("dp", "fsdp")),
        P(("dp", "fsdp"), None),
        P(("dp", "fsdp"), None),
    )
    out_specs = (
        P(("dp", "fsdp"), None),
        P(("dp", "fsdp"), None),
        P("fsdp"),
        P("fsdp"),
        P("fsdp", None),
        P("fsdp", None),
        P("fsdp", None),
        P("fsdp", None),
        P("fsdp", None),
        P("fsdp", None),
        P("fsdp", None),
        P("fsdp", None),
    )
    return jax.shard_map(local, mesh=mesh, in_specs=in_specs, out_specs=out_specs, check_vma=False)
```

```python
from functools import partial

import jax
import jax.numpy as jnp
from jax import lax
from jax.experimental import pallas as pl
from jax.experimental.pallas import tpu as pltpu
from jax.sharding import PartitionSpec as P

QUERY_HEADS = 15
KEY_VALUE_HEADS = 5
HEAD_SIZE = 64
GROUP = QUERY_HEADS // KEY_VALUE_HEADS
MODEL = QUERY_HEADS * HEAD_SIZE
QK_WIDTH = (QUERY_HEADS + KEY_VALUE_HEADS) * HEAD_SIZE
V_START = QK_WIDTH + MODEL - HEAD_SIZE
V_HEAD = 1
SCALE = HEAD_SIZE ** (-0.5)
CHUNK = 512
VMEM_LIMIT = 60 * 2**20
FLOPS_PER_US = 10**9

epsilon = 1e-05
negative = -1e30
narrow_dtype = jnp.bfloat16
wide_type = jnp.float32


def rows_dot(left, right):
    return lax.dot_general(left, right, (((1,), (0,)), ((), ())), preferred_element_type=wide_type)


def rows_dot_t(left, right):
    return lax.dot_general(left, right, (((1,), (1,)), ((), ())), preferred_element_type=wide_type)


def columns_dot(left, right):
    return lax.dot_general(left, right, (((0,), (0,)), ((), ())), preferred_element_type=wide_type)


def inverse_rms(rows):
    return lax.rsqrt(jnp.mean(rows * rows, axis=-1, keepdims=True) + epsilon)


def norm_back(rows, inverse, gain, incoming):
    weighted = incoming * gain
    mean = jnp.mean(weighted * rows, axis=-1, keepdims=True)
    d_rows = inverse * weighted - rows * (inverse * inverse * inverse * mean)
    return d_rows, jnp.sum(incoming * rows * inverse, axis=0, keepdims=True)


def rotate(block, cosines, sines):
    lanes = lax.broadcasted_iota(jnp.int32, block.shape, 1)
    swapped = jnp.where(lanes % HEAD_SIZE < HEAD_SIZE // 2, pltpu.roll(block, 96, 1), pltpu.roll(block, 32, 1))
    return block * cosines + swapped * sines


def causal_bias(count, length):
    row = lax.broadcasted_iota(jnp.int32, (count, count), 0)
    column = lax.broadcasted_iota(jnp.int32, (count, count), 1)
    allowed = column <= row
    if length is not None:
        allowed = allowed & (column < length)
    bias = jnp.where(allowed, 0.0, negative)
    return jnp.concatenate([bias] * GROUP, axis=0)


def head_columns(ref, first, count):
    return jnp.concatenate(
        [ref[:, (first + i) * HEAD_SIZE : (first + i + 1) * HEAD_SIZE] for i in range(count)], axis=0
    )


def attention_forward(rows, gain, router_row, cosines, sines, bias, weight, normed_ref, qk_ref, v_ref, att_ref, log_ref):
    count = rows.shape[0]
    normed_ref[...] = (rows * inverse_rms(rows) * gain).astype(narrow_dtype)
    normed = normed_ref[...]
    gating = jax.nn.sigmoid(jnp.sum(normed.astype(wide_type) * router_row, axis=-1, keepdims=True))
    for block in range(QK_WIDTH // 256):
        product = rows_dot(normed, weight[:, block * 256 : (block + 1) * 256])
        for part in range(2):
            piece = rotate(product[:, part * 128 : (part + 1) * 128], cosines, sines)
            at = block * 256 + part * 128
            qk_ref[:, at : at + 128] = piece.astype(narrow_dtype)
    v_ref[...] = rows_dot(normed, weight[:, V_START:]).astype(narrow_dtype)
    for head in range(KEY_VALUE_HEADS):
        queries = head_columns(qk_ref, head * GROUP, GROUP)
        keys = head_columns(qk_ref, QUERY_HEADS + head, 1)
        values = head_columns(v_ref, V_HEAD + head, 1)
        scores = rows_dot_t(queries, keys) * SCALE + bias
        peak = jnp.max(scores, axis=-1, keepdims=True)
        expanded = jnp.exp(scores - peak)
        total = jnp.sum(expanded, axis=-1, keepdims=True)
        log_ref[:, head : head + 1] = peak + jnp.log(total)
        attended = rows_dot((expanded / total).astype(narrow_dtype), values).astype(narrow_dtype)
        for i in range(GROUP):
            at = (head * GROUP + i) * HEAD_SIZE
            att_ref[:, at : at + HEAD_SIZE] = attended[i * count : (i + 1) * count]
    return rows_dot(att_ref[...], weight[:, QK_WIDTH : QK_WIDTH + MODEL]), gating


def attention_backward(
    rows, gain, router_row, cosines, sines, bias, weight, normed_ref, qk_ref, v_ref, log_ref,
    d_attn_low, d_gating, gating, d_att_ref, d_raw_ref, d_qk_ref, d_v_ref,
):
    count = rows.shape[0]
    d_att_ref[...] = rows_dot_t(d_attn_low, weight[:, QK_WIDTH : QK_WIDTH + MODEL]).astype(narrow_dtype)
    d_v_ref[...] = jnp.zeros_like(d_v_ref)
    for head in range(KEY_VALUE_HEADS):
        queries = head_columns(qk_ref, head * GROUP, GROUP)
        keys = head_columns(qk_ref, QUERY_HEADS + head, 1)
        values = head_columns(v_ref, V_HEAD + head, 1)
        d_attended = head_columns(d_att_ref, head * GROUP, GROUP)
        scores = rows_dot_t(queries, keys) * SCALE + bias
        probabilities = jnp.exp(scores - log_ref[:, head : head + 1])
        d_probs = rows_dot_t(d_attended, values)
        row_dot = jnp.sum(probabilities * d_probs, axis=-1, keepdims=True)
        d_raw = (probabilities * (d_probs - row_dot) * SCALE).astype(narrow_dtype)
        d_queries = rows_dot(d_raw, keys)
        for i in range(GROUP):
            at = (head * GROUP + i) * HEAD_SIZE
            d_raw_ref[:, at : at + HEAD_SIZE] = d_queries[i * count : (i + 1) * count]
        at = (QUERY_HEADS + head) * HEAD_SIZE
        d_raw_ref[:, at : at + HEAD_SIZE] = columns_dot(queries, d_raw).T
        at = (V_HEAD + head) * HEAD_SIZE
        d_values = columns_dot(d_attended, probabilities.astype(narrow_dtype)).T
        d_v_ref[:, at : at + HEAD_SIZE] = d_values.astype(narrow_dtype)
    for block in range(QK_WIDTH // 128):
        at = block * 128
        d_qk_ref[:, at : at + 128] = rotate(d_raw_ref[:, at : at + 128], cosines, -sines).astype(narrow_dtype)
    d_normed = rows_dot_t(d_qk_ref[...], weight[:, :QK_WIDTH]) + rows_dot_t(d_v_ref[...], weight[:, V_START:])
    d_logit = d_gating * gating * (1.0 - gating)
    d_normed = d_normed + d_logit * router_row
    router_gradient = jnp.sum(d_logit * normed_ref[...].astype(wide_type), axis=0, keepdims=True)
    d_rows, gain_gradient = norm_back(rows, inverse_rms(rows), gain, d_normed)
    return d_rows, gain_gradient, router_gradient


def ffn_forward(after, gain, w_gate, w_up, w_down, ffn_ref, gate_ref, up_ref, hidden_ref, total_ref, chunk):
    ffn_ref[...] = (after * inverse_rms(after) * gain).astype(narrow_dtype)
    total_ref[...] = jnp.zeros_like(total_ref)

    def step(index, carry):
        columns = pl.ds(pl.multiple_of(index * chunk, chunk), chunk)
        gate = rows_dot(ffn_ref[...], w_gate[:, columns])
        up = rows_dot(ffn_ref[...], w_up[:, columns])
        gate_ref[:, columns] = gate
        up_ref[:, columns] = up
        hidden = (gate * jax.nn.sigmoid(gate) * up).astype(narrow_dtype)
        hidden_ref[:, columns] = hidden
        total_ref[...] += rows_dot(hidden, w_down[columns, :])
        return carry

    lax.fori_loop(0, gate_ref.shape[1] // chunk, step, 0)


def ffn_backward(after, gain, w_gate, w_up, w_down, d_ffn_ref, gate_ref, up_ref, d_gate_ref, d_up_ref, total_ref, chunk):
    total_ref[...] = jnp.zeros_like(total_ref)

    def step(index, carry):
        columns = pl.ds(pl.multiple_of(index * chunk, chunk), chunk)
        d_hidden = rows_dot_t(d_ffn_ref[...], w_down[columns, :])
        gate = gate_ref[:, columns]
        sig = jax.nn.sigmoid(gate)
        d_gate = (d_hidden * up_ref[:, columns] * sig * (1.0 + gate * (1.0 - sig))).astype(narrow_dtype)
        d_up = (d_hidden * gate * sig).astype(narrow_dtype)
        d_gate_ref[:, columns] = d_gate
        d_up_ref[:, columns] = d_up
        total_ref[...] += rows_dot_t(d_gate, w_gate[:, columns]) + rows_dot_t(d_up, w_up[:, columns])
        return carry

    lax.fori_loop(0, gate_ref.shape[1] // chunk, step, 0)
    return norm_back(after, inverse_rms(after), gain, total_ref[...])


def pick_exact(selector, rows):
    high = rows.astype(narrow_dtype)
    rest = rows - high.astype(wide_type)
    middle = rest.astype(narrow_dtype)
    low = (rest - middle.astype(wide_type)).astype(narrow_dtype)
    return rows_dot(selector, high) + rows_dot(selector, middle) + rows_dot(selector, low)


def first_attention_kernel(
    length_ref, hidden_in, small, cosines, sines, weight, normed_ref, qk_ref, v_ref, att_ref, log_ref, out_ref, gating_ref
):
    rows = hidden_in[...].astype(wide_type)
    bias = causal_bias(rows.shape[0], length_ref[0])
    attn_out, gating = attention_forward(
        rows, small[0:1], small[2:3], cosines[...], sines[...], bias, weight, normed_ref, qk_ref, v_ref, att_ref, log_ref
    )
    out_ref[...] = attn_out
    gating_ref[...] = jnp.broadcast_to(gating, gating_ref.shape)


def last_attention_kernel(
    length_ref, hidden_in, small, cosines, sines, weight, normed_ref, qk_ref, v_ref, att_ref, log_ref, gating_ref,
    d_gating_ref, d_attn_ref, d_input_ref, normed_rest, att_rest, d_qk_rest, d_v_rest, small_middle,
    d_qk_ref, d_v_ref, normed_t_ref, att_t_ref, grad_hidden_ref, small_out, d_att_ref, d_raw_ref,
):
    count = hidden_in.shape[0]
    one = pl.ds(0, count)
    rest = pl.ds(count, d_qk_ref.shape[0] - count)
    rows = hidden_in[...].astype(wide_type)
    bias = causal_bias(count, length_ref[0])
    d_rows, gain_gradient, router_gradient = attention_backward(
        rows, small[0:1], small[2:3], cosines[...], sines[...], bias, weight, normed_ref, qk_ref, v_ref, log_ref,
        d_attn_ref[one], d_gating_ref[:, 0:1], gating_ref[:, 0:1], d_att_ref, d_raw_ref, d_qk_ref.at[one], d_v_ref.at[one],
    )
    grad_hidden_ref[...] = d_input_ref[...] + d_rows
    small_out[...] = small_middle[...]
    small_out[0:1] += gain_gradient
    small_out[2:3] = router_gradient
    d_qk_ref[rest] = d_qk_rest[...]
    d_v_ref[rest] = d_v_rest[...]
    normed_t_ref[...] = jnp.concatenate([normed_ref[...], normed_rest[...]], axis=0).T
    att_t_ref[...] = jnp.concatenate([att_ref[...], att_rest[...]], axis=0).T


def middle_kernel(
    length_ref, hidden_in, cotangent, small, attn_out_ref, gating_ref, cos_two, sin_two, cos_three, sin_three,
    column_two, row_two, column_three, row_three, w_attn_hbm, w_gate_hbm, w_up_hbm, w_down_hbm,
    hidden_out, d_input_ref, d_gating_ref, small_out, hidden_all, d_ffn_t_ref, ffn_t_ref, d_gate_all, d_up_all, d_attn_all,
    att_rest, normed_rest, d_qk_rest, d_v_rest,
    w_attn, w_gate, w_up, w_down, sems,
    gate_one, up_one, gate_two, up_two, gate_three, up_three, total_one, total_two, total_three,
    qk_two, v_two, log_two, qk_three, v_three, log_three, d_att_two, d_raw_two, d_att_three, d_raw_three,
    ffn_all, d_ffn_all,
):
    copies = [
        pltpu.make_async_copy(source, target, sems.at[i])
        for i, (source, target) in enumerate(
            ((w_gate_hbm, w_gate), (w_up_hbm, w_up), (w_down_hbm, w_down), (w_attn_hbm, w_attn))
        )
    ]
    for copy in copies:
        copy.start()
    count_two, count_three = column_two.shape[0], column_three.shape[0]
    count_one = hidden_in.shape[0]
    in_one, in_two = pl.ds(0, count_one), pl.ds(count_one, count_two)
    in_three = pl.ds(count_one + count_two, count_three)
    two = pl.ds(0, count_two)
    three = pl.ds(count_two, count_three)
    gain_attn, gain_ffn = small[0:1], small[1:2]

    def selector(shape, hit):
        return jnp.where(hit, 1.0, 0.0).astype(narrow_dtype)

    pick_two = selector(
        None, lax.broadcasted_iota(jnp.int32, (count_two, count_one), 1) == column_two[...]
    )
    put_two = selector(None, lax.broadcasted_iota(jnp.int32, (count_one, count_two), 0) == row_two[...])
    pick_three = selector(None, column_three[...] == row_two[...])
    put_three = selector(None, column_two[...] == row_three[...])

    after_one = hidden_in[...].astype(wide_type) + attn_out_ref[...]
    for copy in copies[:3]:
        copy.wait()
    ffn_forward(after_one, gain_ffn, w_gate, w_up, w_down, ffn_all.at[in_one], gate_one, up_one, hidden_all.at[in_one], total_one, CHUNK)
    valid = lax.broadcasted_iota(jnp.int32, (count_one, 1), 0) < length_ref[0]
    scale_one = jnp.where(valid, gating_ref[:, 0:1], 0.0)
    change_one = attn_out_ref[...] + total_one[...]
    d_input_ref[...] = hidden_in[...].astype(wide_type) + scale_one * change_one
    total_one[...] = change_one

    copies[3].wait()
    state_two = pick_exact(pick_two, d_input_ref[...])
    bias_two = causal_bias(count_two, None)
    attn_two, gating_two = attention_forward(
        state_two, gain_attn, small[3:4], cos_two[...], sin_two[...], bias_two, w_attn,
        normed_rest.at[two], qk_two, v_two, att_rest.at[two], log_two,
    )
    after_two = state_two + attn_two
    ffn_forward(
        after_two, gain_ffn, w_gate, w_up, w_down, ffn_all.at[in_two], gate_two, up_two, hidden_all.at[in_two], total_two, CHUNK
    )
    change_two = attn_two + total_two[...]
    delta_two = gating_two * change_two

    state_three = pick_exact(pick_three, state_two + delta_two)
    bias_three = causal_bias(count_three, None)
    attn_three, gating_three = attention_forward(
        state_three, gain_attn, small[4:5], cos_three[...], sin_three[...], bias_three, w_attn,
        normed_rest.at[three], qk_three, v_three, att_rest.at[three], log_three,
    )
    after_three = state_three + attn_three
    ffn_forward(
        after_three, gain_ffn, w_gate, w_up, w_down, ffn_all.at[in_three], gate_three, up_three,
        hidden_all.at[in_three], total_three, CHUNK,
    )
    change_three = attn_three + total_three[...]
    added = delta_two + pick_exact(put_three, gating_three * change_three)
    hidden_out[...] = (d_input_ref[...] + pick_exact(put_two, added)).astype(narrow_dtype)

    incoming_two = rows_dot(pick_two, cotangent[...])
    incoming_three = rows_dot(pick_three, incoming_two.astype(narrow_dtype))
    d_change = gating_three * incoming_three
    d_gating = jnp.sum(change_three * incoming_three, axis=-1, keepdims=True)
    d_ffn_all[in_three] = d_change.astype(narrow_dtype)
    d_after, gain_ffn_three = ffn_backward(
        after_three, gain_ffn, w_gate, w_up, w_down, d_ffn_all.at[in_three], gate_three, up_three,
        d_gate_all.at[in_three], d_up_all.at[in_three], total_three, CHUNK,
    )
    d_attn_all[in_three] = (d_change + d_after).astype(narrow_dtype)
    d_rows, gain_attn_three, router_three = attention_backward(
        state_three, gain_attn, small[4:5], cos_three[...], sin_three[...], bias_three, w_attn, normed_rest.at[three],
        qk_three, v_three, log_three, d_attn_all[in_three], d_gating, gating_three, d_att_three, d_raw_three,
        d_qk_rest.at[three], d_v_rest.at[three],
    )
    back_three = pick_exact(put_three, d_rows + d_after)

    incoming_two = incoming_two + back_three
    d_change = gating_two * incoming_two
    d_gating = jnp.sum(change_two * incoming_two, axis=-1, keepdims=True)
    d_ffn_all[in_two] = d_change.astype(narrow_dtype)
    d_after, gain_ffn_two = ffn_backward(
        after_two, gain_ffn, w_gate, w_up, w_down, d_ffn_all.at[in_two], gate_two, up_two,
        d_gate_all.at[in_two], d_up_all.at[in_two], total_two, CHUNK,
    )
    d_attn_all[in_two] = (d_change + d_after).astype(narrow_dtype)
    d_rows, gain_attn_two, router_two = attention_backward(
        state_two, gain_attn, small[3:4], cos_two[...], sin_two[...], bias_two, w_attn, normed_rest.at[two],
        qk_two, v_two, log_two, d_attn_all[in_two], d_gating, gating_two, d_att_two, d_raw_two,
        d_qk_rest.at[two], d_v_rest.at[two],
    )
    back_two = back_three + d_rows + d_after

    incoming = cotangent[...].astype(wide_type) + pick_exact(put_two, back_two)
    d_input_ref[...] = incoming
    d_change = scale_one * incoming
    d_gating = jnp.where(valid, jnp.sum(total_one[...] * incoming, axis=-1, keepdims=True), 0.0)
    d_gating_ref[...] = jnp.broadcast_to(d_gating, d_gating_ref.shape)
    d_ffn_all[in_one] = d_change.astype(narrow_dtype)
    after_one = hidden_in[...].astype(wide_type) + attn_out_ref[...]
    d_after, gain_ffn_one = ffn_backward(
        after_one, gain_ffn, w_gate, w_up, w_down, d_ffn_all.at[in_one], gate_one, up_one,
        d_gate_all.at[in_one], d_up_all.at[in_one], total_one, CHUNK,
    )
    d_attn_all[in_one] = (scale_one * d_input_ref[...] + d_after).astype(narrow_dtype)
    d_input_ref[...] += d_after
    small_out[...] = jnp.zeros_like(small_out)
    small_out[0:1] = gain_attn_two + gain_attn_three
    small_out[1:2] = gain_ffn_one + gain_ffn_two + gain_ffn_three
    small_out[3:4] = router_two
    small_out[4:5] = router_three
    d_ffn_t_ref[...] = d_ffn_all[...].T
    ffn_t_ref[...] = ffn_all[...].T


def rotary_tables(positions):
    half = HEAD_SIZE // 2
    lanes = jnp.arange(2 * HEAD_SIZE)
    frequency = 10000.0 ** (-(lanes % half).astype(wide_type) / half)
    angles = positions.astype(wide_type)[:, None] * frequency[None, :]
    sign = jnp.where(lanes % HEAD_SIZE < half, -1.0, 1.0)
    return jnp.cos(angles), jnp.sin(angles) * sign[None, :]


def call(kernel, operands, outputs, flops, scratch=(), hbm=(), scalars=1):
    specs = [
        pl.BlockSpec(memory_space=pltpu.SMEM if i < scalars else (pl.ANY if i in hbm else pltpu.VMEM))
        for i in range(len(operands))
    ]
    return pl.pallas_call(
        kernel,
        out_shape=[jax.ShapeDtypeStruct(shape, kind) for shape, kind in outputs],
        in_specs=specs,
        out_specs=[pl.BlockSpec(memory_space=pltpu.VMEM)] * len(outputs),
        scratch_shapes=list(scratch),
        compiler_params=pltpu.CompilerParams(vmem_limit_bytes=VMEM_LIMIT),
        cost_estimate=pl.CostEstimate(flops=flops, bytes_accessed=flops // 400, transcendentals=0),
    )(*operands)


def partner(value, axis, bit):
    count = lax.axis_size(axis)
    return lax.ppermute(value, axis, [(i, i ^ bit) for i in range(count)])


def side(axis, bit):
    return (lax.axis_index(axis) // bit) % 2


def after(value, *others):
    return lax.optimization_barrier((value,) + others)[0]


def bits_of(axis, low):
    found = []
    bit = low
    while bit < lax.axis_size(axis):
        found.append(bit)
        bit = bit * 2
    return found


def piece_of(value, index, size, dim):
    return lax.dynamic_slice_in_dim(value, index * size, size, dim)


def take_half(value, axis, bit, dim):
    size = value.shape[dim] // 2
    which = side(axis, bit)
    return piece_of(value, which, size, dim), piece_of(value, 1 - which, size, dim)


def add(*values):
    total = values[0].astype(wide_type)
    for value in values[1:]:
        total = total + value.astype(wide_type)
    return total.astype(narrow_dtype)


def in_order(parts, index):
    bit = 1
    while bit < len(parts):
        swap = (index // bit) % 2 == 1
        parts = [jnp.where(swap, parts[i ^ bit], parts[i]) for i in range(len(parts))]
        bit = bit * 2
    return parts


def join(parts, index, dim):
    return jnp.concatenate(in_order(parts, index), axis=dim)


def join_half(value, axis, bit, dim):
    return join([value, partner(value, axis, bit)], side(axis, bit), dim)


CORE, ROW, LAYER = 1, 2, 4


class Part:
    def __init__(self, y_dim, z_dim, fsdp_dim, core_dim):
        self.y_dim, self.z_dim, self.fsdp_dim, self.core_dim = y_dim, z_dim, fsdp_dim, core_dim

    def layers(self):
        return lax.axis_size("dp") // LAYER

    def layer(self):
        return lax.axis_index("dp") // LAYER

    def split_x(self, value):
        owners = lax.axis_size("fsdp")
        size = value.shape[self.fsdp_dim] // owners
        mine = lax.axis_index("fsdp")
        return [piece_of(value, mine ^ offset, size, self.fsdp_dim) for offset in range(owners)]

    def send_x(self, parts):
        return [parts[0]] + [partner(part, "fsdp", offset) for offset, part in enumerate(parts) if offset]

    def send_y(self, value):
        keep, send = take_half(value, "dp", ROW, self.y_dim)
        return [keep, partner(send, "dp", ROW)]

    def split_z(self, value):
        size = value.shape[self.z_dim] // self.layers()
        return [piece_of(value, self.layer() ^ offset, size, self.z_dim) for offset in range(self.layers())]

    def send_z(self, parts):
        return [parts[0]] + [partner(part, "dp", offset * LAYER) for offset, part in enumerate(parts) if offset]

    def back_z(self, piece):
        return [piece] + [partner(piece, "dp", offset * LAYER) for offset in range(1, self.layers())]

    def back_y(self, value):
        return [value, partner(value, "dp", ROW)]

    def back_core(self, value):
        return [value, partner(value, "dp", CORE)]

    def join_z(self, parts):
        return join(parts, self.layer(), self.z_dim)

    def join_y(self, parts):
        return join(parts, side("dp", ROW), self.y_dim)

    def join_core(self, parts):
        return join(parts, side("dp", CORE), self.core_dim)


class Order:
    def __init__(self):
        self.last = None

    def hold(self, value):
        return value if self.last is None else after(value, self.last)

    def step(self, work, values):
        result = work([self.hold(values[0])] + list(values[1:]))
        self.last = result
        return result


def reduce_all(parts, makers, order, beside, between, finish):
    core = side("dp", CORE)
    count = len(parts)
    done, halves, joined, pieces, cores = ([None] * count for _ in range(5))

    def produce(k):
        away = makers[k](1 - core, None)
        order.last = away
        value = makers[k](core, partner(away, "dp", CORE))
        order.last = value
        return parts[k].split_x(value)

    def added(values):
        return add(*values)

    waiting = produce(0)
    x_parts = parts[0].send_x(waiting)
    beside()
    waiting = produce(1)
    for k in range(count + 3):
        if k < count:
            halves[k] = order.step(added, x_parts)
            y_parts = parts[k].send_y(halves[k])
        if k + 1 < count:
            x_parts = parts[k + 1].send_x([order.hold(part) for part in waiting])
        if 1 <= k <= count:
            piece = order.step(added, z_parts)
            pieces[k - 1] = parts[k - 1].back_z(piece)
        if 2 <= k <= count + 1:
            value = order.step(parts[k - 2].join_y, back)
            cores[k - 2] = parts[k - 2].back_core(value)
        if k >= 3:
            done[k - 3] = order.step(lambda values: finish[k - 3](parts[k - 3].join_core(values)), cores[k - 3])
        if k + 2 < count:
            waiting = produce(k + 2)
        between(k)
        if k < count:
            z_value = order.step(added, y_parts)
            z_parts = parts[k].send_z(parts[k].split_z(z_value))
        if 1 <= k <= count:
            value = order.step(parts[k - 1].join_z, pieces[k - 1])
            back = parts[k - 1].back_y(value)
    return done


def split_steps(row_steps):
    steps = [("dp", 1, 0), ("dp", 2, 0)]
    return steps + [("dp", bit, 0 if row_steps else 1) for bit in bits_of("dp", 4)]


def place(parts, rows, shape):
    full = jnp.zeros(shape, narrow_dtype)
    for index, part in parts:
        full = lax.dynamic_update_slice_in_dim(full, part, index * rows, 0)
    return full


def gather_near(shard):
    owners = lax.axis_size("fsdp")
    mine = lax.axis_index("fsdp")
    half, _ = take_half(shard, "dp", 1, 0)
    parts = [(mine, shard)]
    for offset in range(1, owners):
        parts.append((mine ^ offset, join_half(partner(half, "fsdp", offset), "dp", 1, 0)))
    return place(parts, shard.shape[0], (shard.shape[0] * owners,) + shard.shape[1:])


def gather_far(shard, row_steps):
    owners = lax.axis_size("fsdp")
    mine = lax.axis_index("fsdp")
    steps = split_steps(row_steps)
    piece = shard
    for axis, bit, dim in steps:
        piece, _ = take_half(piece, axis, bit, dim)
    parts = [(mine, shard)]
    for offset in range(1, owners):
        other = partner(piece, "fsdp", offset)
        for axis, bit, dim in reversed(steps):
            other = join_half(other, axis, bit, dim)
        parts.append((mine ^ offset, other))
    return place(parts, shard.shape[0], (shard.shape[0] * owners,) + shard.shape[1:])


def local(
    hidden_in,
    cotangent,
    norm_attn,
    norm_ffn,
    router,
    w_query,
    key_weight,
    value_weight,
    w_out,
    w_gate,
    w_up,
    w_down,
    lengths,
    chosen_second,
    chosen_third,
):
    owners = lax.axis_size("fsdp")
    mine = lax.axis_index("fsdp")
    small = jnp.concatenate(
        [norm_attn[None, :], norm_ffn[None, :], router.T, jnp.zeros((11, norm_attn.shape[0]), wide_type)]
    ).astype(narrow_dtype)
    small_parts = [(mine, small)] + [
        (mine ^ offset, partner(small, "fsdp", offset)) for offset in range(1, owners)
    ]
    small_rows = jnp.zeros((16, owners * small.shape[1]), narrow_dtype)
    for index, part in small_parts:
        small_rows = lax.dynamic_update_slice_in_dim(small_rows, part, index * small.shape[1], 1)
    width = w_query.shape[1]
    kv_width = key_weight.shape[1]
    attn_shard = jnp.concatenate([w_query, key_weight, w_out, value_weight], axis=1).astype(narrow_dtype)
    attn_full = gather_near(attn_shard)
    gate_full = gather_far(w_gate.astype(narrow_dtype), False)
    up_full = gather_far(w_up.astype(narrow_dtype), False)
    down_full = gather_far(w_down.astype(narrow_dtype), True)
    small_wide = small_rows[:8].astype(wide_type)
    count_one, model = hidden_in.shape
    ff = gate_full.shape[1]
    chosen_two, chosen_three = chosen_second[0], chosen_third[0]
    count_two, count_three = chosen_two.shape[0], chosen_three.shape[0]
    count_rest = count_two + count_three
    cos_one, sin_one = rotary_tables(jnp.arange(count_one))
    cos_two, sin_two = rotary_tables(chosen_two)
    cos_three, sin_three = rotary_tables(chosen_three)
    v_width = attn_full.shape[1] - V_START

    normed_one, qk_one, v_one, att_one, log_one, attn_out_one, gating_one = call(
        first_attention_kernel,
        (lengths, hidden_in, small_wide, cos_one, sin_one, attn_full),
        [
            ((count_one, model), narrow_dtype),
            ((count_one, QK_WIDTH), narrow_dtype),
            ((count_one, v_width), narrow_dtype),
            ((count_one, model), narrow_dtype),
            ((GROUP * count_one, 128), wide_type),
            ((count_one, model), wide_type),
            ((count_one, 128), wide_type),
        ],
        10 * FLOPS_PER_US,
    )
    count_all = count_one + count_rest
    rest = lambda width: ((count_rest, width), narrow_dtype)
    every = lambda width: ((count_all, width), narrow_dtype)
    turned = ((model, count_all), narrow_dtype)
    scratch_for = lambda count: [
        pltpu.VMEM((count, QK_WIDTH), narrow_dtype),
        pltpu.VMEM((count, v_width), narrow_dtype),
        pltpu.VMEM((GROUP * count, 128), wide_type),
    ]
    back_scratch = lambda count: [
        pltpu.VMEM((count, model), narrow_dtype),
        pltpu.VMEM((count, QK_WIDTH), wide_type),
    ]
    wide = lambda count, width: pltpu.VMEM((count, width), wide_type)
    (
        hidden_out, d_input, d_gating_one, small_middle, hidden, d_ffn_t, ffn_t, d_gate, d_up, d_attn,
        att_rest, normed_rest, d_qk_rest, d_v_rest,
    ) = call(
        middle_kernel,
        (
            lengths, hidden_in, cotangent, small_wide, attn_out_one, gating_one, cos_two, sin_two, cos_three, sin_three,
            chosen_two[:, None], chosen_two[None, :], chosen_three[:, None], chosen_three[None, :],
            attn_full, gate_full, up_full, down_full,
        ),
        [
            ((count_one, model), narrow_dtype), ((count_one, model), wide_type), ((count_one, 128), wide_type),
            ((8, model), wide_type), every(ff), turned, turned, every(ff), every(ff), every(model),
            rest(model), rest(model), rest(QK_WIDTH), rest(v_width),
        ],
        57 * FLOPS_PER_US,
        [
            pltpu.VMEM(attn_full.shape, narrow_dtype),
            pltpu.VMEM(gate_full.shape, narrow_dtype),
            pltpu.VMEM(up_full.shape, narrow_dtype),
            pltpu.VMEM(down_full.shape, narrow_dtype),
            pltpu.SemaphoreType.DMA((4,)),
            wide(count_one, ff), wide(count_one, ff), wide(count_two, ff), wide(count_two, ff),
            wide(count_three, ff), wide(count_three, ff),
            wide(count_one, model), wide(count_two, model), wide(count_three, model),
        ]
        + scratch_for(count_two) + scratch_for(count_three) + back_scratch(count_two) + back_scratch(count_three)
        + [pltpu.VMEM((count_all, model), narrow_dtype)] * 2,
        hbm=(14, 15, 16, 17),
    )

    order = Order()
    attention = []

    def last_attention():
        attention.extend(
            call(
                last_attention_kernel,
                (
                    lengths, hidden_in, small_wide, cos_one, sin_one, attn_full, normed_one, qk_one, v_one, att_one,
                    log_one, gating_one, d_gating_one, order.hold(d_attn), d_input, normed_rest, att_rest, d_qk_rest,
                    d_v_rest, small_middle,
                ),
                [
                    every(QK_WIDTH), every(v_width), turned, turned, ((count_one, model), wide_type),
                    ((8, model), wide_type),
                ],
                1000,
                back_scratch(count_one),
            )
        )
        order.last = attention[0]

    def dot(left, right):
        return jnp.dot(left, right, preferred_element_type=wide_type)

    def plus(product, received):
        if received is not None:
            product = product + received.astype(wide_type)
        return product.astype(narrow_dtype)

    def core_rows(left, which):
        rows = left.reshape(owners, 2, model // owners // 2, left.shape[1])
        rows = lax.dynamic_index_in_dim(rows, which, 1, keepdims=False)
        return rows.reshape(model // 2, left.shape[1])

    def make_down(which, received):
        size = ff // owners // 2
        columns = jnp.concatenate([piece_of(hidden, 2 * owner + which, size, 1) for owner in range(owners)], axis=1)
        return plus(dot(order.hold(d_ffn_t), columns), received)

    def make_from(right):
        def make(which, received):
            return plus(dot(core_rows(ffn_t, which), order.hold(right)), received)

        return make

    skip = V_HEAD * HEAD_SIZE
    split = 256

    def make_first(which, received):
        d_qk, _, normed_t, att_t, _, _ = attention
        product = [dot(core_rows(normed_t, which), order.hold(d_qk)), dot(core_rows(att_t, which), d_attn[:, :split])]
        return plus(jnp.concatenate(product, axis=1), received)

    def make_second(which, received):
        _, d_v, normed_t, att_t, _, _ = attention
        left = order.hold(att_t)
        product = [dot(core_rows(left, which), d_attn[:, split:]), dot(core_rows(normed_t, which), d_v[:, skip:])]
        return plus(jnp.concatenate(product, axis=1), received)

    by_rows = lambda: Part(y_dim=0, z_dim=1, fsdp_dim=0, core_dim=0)
    small_state = []
    small_steps = [(axis, bit) for axis in ("fsdp", "dp") for bit in bits_of(axis, 1)]

    def add_small(k):
        if not small_state:
            small_state.extend([attention[5], None])
        value, moved = small_state
        if moved is not None:
            value = order.step(lambda values: values[0] + values[1], [value, moved])
        moved = partner(value, *small_steps[k]) if k < len(small_steps) else None
        small_state[:] = [value, moved]

    widen = lambda value: value.astype(wide_type)
    down_shard, gate_shard, up_shard, first_shard, second_shard = reduce_all(
        [Part(y_dim=0, z_dim=0, fsdp_dim=1, core_dim=1)] + [by_rows() for _ in range(4)],
        [make_down, make_from(d_gate), make_from(d_up), make_first, make_second],
        order,
        last_attention,
        add_small,
        [lambda value: widen(value).T] + [widen] * 4,
    )
    grad_hidden, small_sum = attention[4], small_state[0]
    small_sum = lax.dynamic_slice_in_dim(small_sum, mine * small.shape[1], small.shape[1], 1)
    return (
        hidden_out,
        grad_hidden,
        small_sum[0],
        small_sum[1],
        small_sum[2:5].T,
        first_shard[:, :width],
        first_shard[:, width : width + kv_width],
        second_shard[:, width - split :],
        jnp.concatenate([first_shard[:, width + kv_width :], second_shard[:, : width - split]], axis=1),
        gate_shard,
        up_shard,
        down_shard,
    )


def solution(mesh):
    in_specs = (
        P(("dp", "fsdp"), None),
        P(("dp", "fsdp"), None),
        P("fsdp"),
        P("fsdp"),
        P("fsdp", None),
        P("fsdp", None),
        P("fsdp", None),
        P("fsdp", None),
        P("fsdp", None),
        P("fsdp", None),
        P("fsdp", None),
        P("fsdp", None),
        P(("dp", "fsdp")),
        P(("dp", "fsdp"), None),
        P(("dp", "fsdp"), None),
    )
    out_specs = (
        P(("dp", "fsdp"), None),
        P(("dp", "fsdp"), None),
        P("fsdp"),
        P("fsdp"),
        P("fsdp", None),
        P("fsdp", None),
        P("fsdp", None),
        P("fsdp", None),
        P("fsdp", None),
        P("fsdp", None),
        P("fsdp", None),
        P("fsdp", None),
    )
    return jax.shard_map(local, mesh=mesh, in_specs=in_specs, out_specs=out_specs, check_vma=False)
```

```python
from functools import partial

import jax
import jax.numpy as jnp
from jax import lax
from jax.experimental import pallas as pl
from jax.experimental.pallas import tpu as pltpu
from jax.sharding import PartitionSpec as P

QUERY_HEADS = 15
KEY_VALUE_HEADS = 5
HEAD_SIZE = 64
GROUP = QUERY_HEADS // KEY_VALUE_HEADS
MODEL = QUERY_HEADS * HEAD_SIZE
QK_WIDTH = (QUERY_HEADS + KEY_VALUE_HEADS) * HEAD_SIZE
V_START = QK_WIDTH + MODEL - HEAD_SIZE
V_HEAD = 1
SCALE = HEAD_SIZE ** (-0.5)
CHUNK = 512
STACKED = ()

epsilon = 1e-05
negative = -1e30
narrow_dtype = jnp.bfloat16
wide_type = jnp.float32


def rows_dot(left, right):
    return lax.dot_general(left, right, (((1,), (0,)), ((), ())), preferred_element_type=wide_type)


def rows_dot_t(left, right):
    return lax.dot_general(left, right, (((1,), (1,)), ((), ())), preferred_element_type=wide_type)


def columns_dot(left, right):
    return lax.dot_general(left, right, (((0,), (0,)), ((), ())), preferred_element_type=wide_type)


def inverse_rms(rows):
    return lax.rsqrt(jnp.mean(rows * rows, axis=-1, keepdims=True) + epsilon)


def norm_back(rows, inverse, gain, incoming):
    weighted = incoming * gain
    mean = jnp.mean(weighted * rows, axis=-1, keepdims=True)
    d_rows = inverse * weighted - rows * (inverse * inverse * inverse * mean)
    return d_rows, jnp.sum(incoming * rows * inverse, axis=0, keepdims=True)


def rotate(block, cosines, sines):
    lanes = lax.broadcasted_iota(jnp.int32, block.shape, 1)
    swapped = jnp.where(lanes % HEAD_SIZE < HEAD_SIZE // 2, pltpu.roll(block, 96, 1), pltpu.roll(block, 32, 1))
    return block * cosines + swapped * sines


def causal_bias(count, length):
    row = lax.broadcasted_iota(jnp.int32, (count, count), 0)
    column = lax.broadcasted_iota(jnp.int32, (count, count), 1)
    allowed = column <= row
    if length is not None:
        allowed = allowed & (column < length)
    bias = jnp.where(allowed, 0.0, negative)
    return jnp.concatenate([bias] * GROUP, axis=0)


def head_columns(ref, first, count):
    return jnp.concatenate(
        [ref[:, (first + i) * HEAD_SIZE : (first + i + 1) * HEAD_SIZE] for i in range(count)], axis=0
    )


def attention_forward(rows, gain, router_row, cosines, sines, bias, weight, normed_ref, qk_ref, v_ref, att_ref, log_ref):
    count = rows.shape[0]
    normed_ref[...] = (rows * inverse_rms(rows) * gain).astype(narrow_dtype)
    normed = normed_ref[...]
    gating = jax.nn.sigmoid(jnp.sum(normed.astype(wide_type) * router_row, axis=-1, keepdims=True))
    for block in range(QK_WIDTH // 256):
        product = rows_dot(normed, weight[:, block * 256 : (block + 1) * 256])
        for part in range(2):
            piece = rotate(product[:, part * 128 : (part + 1) * 128], cosines, sines)
            at = block * 256 + part * 128
            qk_ref[:, at : at + 128] = piece.astype(narrow_dtype)
    v_ref[...] = rows_dot(normed, weight[:, V_START:]).astype(narrow_dtype)
    for head in range(KEY_VALUE_HEADS):
        queries = head_columns(qk_ref, head * GROUP, GROUP)
        keys = head_columns(qk_ref, QUERY_HEADS + head, 1)
        values = head_columns(v_ref, V_HEAD + head, 1)
        scores = rows_dot_t(queries, keys) * SCALE + bias
        peak = jnp.max(scores, axis=-1, keepdims=True)
        expanded = jnp.exp(scores - peak)
        total = jnp.sum(expanded, axis=-1, keepdims=True)
        log_ref[:, head : head + 1] = peak + jnp.log(total)
        attended = rows_dot((expanded / total).astype(narrow_dtype), values).astype(narrow_dtype)
        for i in range(GROUP):
            at = (head * GROUP + i) * HEAD_SIZE
            att_ref[:, at : at + HEAD_SIZE] = attended[i * count : (i + 1) * count]
    return rows_dot(att_ref[...], weight[:, QK_WIDTH : QK_WIDTH + MODEL]), gating


def attention_backward(
    rows, gain, router_row, cosines, sines, bias, weight, normed_ref, qk_ref, v_ref, log_ref,
    d_attn_low, d_gating, gating, d_att_ref, d_raw_ref, d_qk_ref, d_v_ref,
):
    count = rows.shape[0]
    d_att_ref[...] = rows_dot_t(d_attn_low, weight[:, QK_WIDTH : QK_WIDTH + MODEL]).astype(narrow_dtype)
    d_v_ref[...] = jnp.zeros_like(d_v_ref)
    for head in range(KEY_VALUE_HEADS):
        queries = head_columns(qk_ref, head * GROUP, GROUP)
        keys = head_columns(qk_ref, QUERY_HEADS + head, 1)
        values = head_columns(v_ref, V_HEAD + head, 1)
        d_attended = head_columns(d_att_ref, head * GROUP, GROUP)
        scores = rows_dot_t(queries, keys) * SCALE + bias
        probabilities = jnp.exp(scores - log_ref[:, head : head + 1])
        d_probs = rows_dot_t(d_attended, values)
        row_dot = jnp.sum(probabilities * d_probs, axis=-1, keepdims=True)
        d_raw = (probabilities * (d_probs - row_dot) * SCALE).astype(narrow_dtype)
        d_queries = rows_dot(d_raw, keys)
        for i in range(GROUP):
            at = (head * GROUP + i) * HEAD_SIZE
            d_raw_ref[:, at : at + HEAD_SIZE] = d_queries[i * count : (i + 1) * count]
        at = (QUERY_HEADS + head) * HEAD_SIZE
        d_raw_ref[:, at : at + HEAD_SIZE] = columns_dot(queries, d_raw).T
        at = (V_HEAD + head) * HEAD_SIZE
        d_values = columns_dot(d_attended, probabilities.astype(narrow_dtype)).T
        d_v_ref[:, at : at + HEAD_SIZE] = d_values.astype(narrow_dtype)
    for block in range(QK_WIDTH // 128):
        at = block * 128
        d_qk_ref[:, at : at + 128] = rotate(d_raw_ref[:, at : at + 128], cosines, -sines).astype(narrow_dtype)
    d_normed = rows_dot_t(d_qk_ref[...], weight[:, :QK_WIDTH]) + rows_dot_t(d_v_ref[...], weight[:, V_START:])
    d_logit = d_gating * gating * (1.0 - gating)
    d_normed = d_normed + d_logit * router_row
    router_gradient = jnp.sum(d_logit * normed_ref[...].astype(wide_type), axis=0, keepdims=True)
    d_rows, gain_gradient = norm_back(rows, inverse_rms(rows), gain, d_normed)
    return d_rows, gain_gradient, router_gradient


def ffn_forward(after, gain, w_gate, w_up, w_down, ffn_ref, gate_ref, up_ref, hidden_ref, total_ref, chunk):
    ffn_ref[...] = (after * inverse_rms(after) * gain).astype(narrow_dtype)
    total_ref[...] = jnp.zeros_like(total_ref)

    def step(index, carry):
        columns = pl.ds(pl.multiple_of(index * chunk, chunk), chunk)
        gate = rows_dot(ffn_ref[...], w_gate[:, columns])
        up = rows_dot(ffn_ref[...], w_up[:, columns])
        gate_ref[:, columns] = gate
        up_ref[:, columns] = up
        hidden = (gate * jax.nn.sigmoid(gate) * up).astype(narrow_dtype)
        hidden_ref[:, columns] = hidden
        total_ref[...] += rows_dot_t(hidden, w_down[:, columns])
        return carry

    lax.fori_loop(0, gate_ref.shape[1] // chunk, step, 0)


def ffn_backward(after, gain, w_gate, w_up, w_down, d_ffn_ref, gate_ref, up_ref, d_gate_ref, d_up_ref, total_ref, chunk):
    total_ref[...] = jnp.zeros_like(total_ref)

    def step(index, carry):
        columns = pl.ds(pl.multiple_of(index * chunk, chunk), chunk)
        d_hidden = rows_dot(d_ffn_ref[...], w_down[:, columns])
        gate = gate_ref[:, columns]
        sig = jax.nn.sigmoid(gate)
        d_gate = (d_hidden * up_ref[:, columns] * sig * (1.0 + gate * (1.0 - sig))).astype(narrow_dtype)
        d_up = (d_hidden * gate * sig).astype(narrow_dtype)
        d_gate_ref[:, columns] = d_gate
        d_up_ref[:, columns] = d_up
        total_ref[...] += rows_dot_t(d_gate, w_gate[:, columns]) + rows_dot_t(d_up, w_up[:, columns])
        return carry

    lax.fori_loop(0, gate_ref.shape[1] // chunk, step, 0)
    return norm_back(after, inverse_rms(after), gain, total_ref[...])


def pick_exact(selector, rows):
    high = rows.astype(narrow_dtype)
    rest = rows - high.astype(wide_type)
    middle = rest.astype(narrow_dtype)
    low = (rest - middle.astype(wide_type)).astype(narrow_dtype)
    return rows_dot(selector, high) + rows_dot(selector, middle) + rows_dot(selector, low)


def first_attention_kernel(
    fetch, length_ref, at_ref, hidden_t, cotangent_t, small, cosines, sines, *refs
):
    sources, refs = refs[: fetch.count], refs[fetch.count :]
    hidden_in, cotangent, normed_ref, qk_ref, v_ref, att_ref, log_ref, out_ref, gating_ref, weight, sems = refs
    hidden_in[...] = hidden_t[...].T
    cotangent[...] = cotangent_t[...].T
    copies = fetch.start(at_ref, sources, {"attn": weight}, sems)
    rows = hidden_in[...].astype(wide_type)
    for copy in copies["attn"]:
        copy.wait()
    bias = causal_bias(rows.shape[0], length_ref[0])
    attn_out, gating = attention_forward(
        rows, small[0:1], small[2:3], cosines[...], sines[...], bias, weight, normed_ref, qk_ref, v_ref, att_ref, log_ref
    )
    out_ref[...] = attn_out
    gating_ref[...] = jnp.broadcast_to(gating, gating_ref.shape)


def last_attention_kernel(
    fetch, length_ref, at_ref, hidden_in, small, cosines, sines, normed_ref, qk_ref, v_ref, att_ref, log_ref, gating_ref,
    d_gating_ref, d_attn_ref, d_input_ref, normed_rest, att_rest, d_qk_rest, d_v_rest, small_middle, *refs,
):
    sources, refs = refs[: fetch.count], refs[fetch.count :]
    d_qk_ref, d_v_ref, normed_t_ref, att_t_ref, grad_hidden_ref, small_out, small_parts, d_att_ref, d_raw_ref, weight, sems = refs
    copies = fetch.start(at_ref, sources, {"attn": weight}, sems)
    for copy in copies["attn"]:
        copy.wait()
    count = hidden_in.shape[0]
    one = pl.ds(0, count)
    rest = pl.ds(count, d_qk_ref.shape[0] - count)
    rows = hidden_in[...].astype(wide_type)
    bias = causal_bias(count, length_ref[0])
    d_rows, gain_gradient, router_gradient = attention_backward(
        rows, small[0:1], small[2:3], cosines[...], sines[...], bias, weight, normed_ref, qk_ref, v_ref, log_ref,
        d_attn_ref[one, :MODEL], d_gating_ref[:, 0:1], gating_ref[:, 0:1], d_att_ref, d_raw_ref, d_qk_ref.at[one], d_v_ref.at[one],
    )
    grad_hidden_ref[...] = d_input_ref[...] + d_rows
    small_out[...] = small_middle[...]
    small_out[0:1] += gain_gradient
    small_out[2:3] = router_gradient
    small_parts[...] = jnp.zeros_like(small_parts)
    size = MODEL // small_parts.shape[0]
    for owner in range(small_parts.shape[0]):
        small_parts[owner, :, 0:size] = small_out[:, owner * size : (owner + 1) * size]
    d_qk_ref[rest] = d_qk_rest[...]
    d_v_ref[rest] = d_v_rest[...]
    normed_t_ref[...] = jnp.concatenate([normed_ref[...], normed_rest[...]], axis=0).T
    att_t_ref[...] = jnp.concatenate([att_ref[...], att_rest[...]], axis=0).T


def middle_kernel(
    fetch, length_ref, at_ref, hidden_in, cotangent, small, attn_out_ref, gating_ref, cos_two, sin_two, cos_three, sin_three,
    column_two, row_two, column_three, row_three, *refs,
):
    sources, refs = refs[: fetch.count], refs[fetch.count :]
    (
        hidden_out, d_input_ref, d_gating_ref, small_out, hidden_all, d_ffn_t_ref, ffn_t_ref, d_gate_all, d_up_all,
        d_attn_all, att_rest, normed_rest, d_qk_rest, d_v_rest,
        w_attn, w_pair, w_down, sems,
        gate_one, up_one, gate_two, up_two, gate_three, up_three, total_one, total_two, total_three,
        qk_two, v_two, log_two, qk_three, v_three, log_three, d_att_two, d_raw_two, d_att_three, d_raw_three,
        ffn_all, d_ffn_all,
    ) = refs
    copies = fetch.start(at_ref, sources, {"pair": w_pair, "down": w_down, "attn": w_attn}, sems)
    w_gate, w_up = w_pair.at[0], w_pair.at[1]
    count_two, count_three = column_two.shape[0], column_three.shape[0]
    count_one = hidden_in.shape[0]
    in_one, in_two = pl.ds(0, count_one), pl.ds(count_one, count_two)
    in_three = pl.ds(count_one + count_two, count_three)
    two = pl.ds(0, count_two)
    three = pl.ds(count_two, count_three)
    gain_attn, gain_ffn = small[0:1], small[1:2]

    def selector(shape, hit):
        return jnp.where(hit, 1.0, 0.0).astype(narrow_dtype)

    pick_two = selector(
        None, lax.broadcasted_iota(jnp.int32, (count_two, count_one), 1) == column_two[...]
    )
    put_two = selector(None, lax.broadcasted_iota(jnp.int32, (count_one, count_two), 0) == row_two[...])
    pick_three = selector(None, column_three[...] == row_two[...])
    put_three = selector(None, column_two[...] == row_three[...])

    after_one = hidden_in[...].astype(wide_type) + attn_out_ref[...]
    for copy in copies["pair"] + copies["down"]:
        copy.wait()
    ffn_forward(after_one, gain_ffn, w_gate, w_up, w_down, ffn_all.at[in_one], gate_one, up_one, hidden_all.at[in_one], total_one, CHUNK)
    valid = lax.broadcasted_iota(jnp.int32, (count_one, 1), 0) < length_ref[0]
    scale_one = jnp.where(valid, gating_ref[:, 0:1], 0.0)
    change_one = attn_out_ref[...] + total_one[...]
    d_input_ref[...] = hidden_in[...].astype(wide_type) + scale_one * change_one
    total_one[...] = change_one

    for copy in copies["attn"]:
        copy.wait()
    d_attn_all[...] = jnp.zeros_like(d_attn_all)
    state_two = pick_exact(pick_two, d_input_ref[...])
    bias_two = causal_bias(count_two, None)
    attn_two, gating_two = attention_forward(
        state_two, gain_attn, small[3:4], cos_two[...], sin_two[...], bias_two, w_attn,
        normed_rest.at[two], qk_two, v_two, att_rest.at[two], log_two,
    )
    after_two = state_two + attn_two
    ffn_forward(
        after_two, gain_ffn, w_gate, w_up, w_down, ffn_all.at[in_two], gate_two, up_two, hidden_all.at[in_two], total_two, CHUNK
    )
    change_two = attn_two + total_two[...]
    delta_two = gating_two * change_two

    state_three = pick_exact(pick_three, state_two + delta_two)
    bias_three = causal_bias(count_three, None)
    attn_three, gating_three = attention_forward(
        state_three, gain_attn, small[4:5], cos_three[...], sin_three[...], bias_three, w_attn,
        normed_rest.at[three], qk_three, v_three, att_rest.at[three], log_three,
    )
    after_three = state_three + attn_three
    ffn_forward(
        after_three, gain_ffn, w_gate, w_up, w_down, ffn_all.at[in_three], gate_three, up_three,
        hidden_all.at[in_three], total_three, CHUNK,
    )
    change_three = attn_three + total_three[...]
    added = delta_two + pick_exact(put_three, gating_three * change_three)
    hidden_out[...] = (d_input_ref[...] + pick_exact(put_two, added)).astype(narrow_dtype)

    incoming_two = rows_dot(pick_two, cotangent[...])
    incoming_three = rows_dot(pick_three, incoming_two.astype(narrow_dtype))
    d_change = gating_three * incoming_three
    d_gating = jnp.sum(change_three * incoming_three, axis=-1, keepdims=True)
    d_ffn_all[in_three] = d_change.astype(narrow_dtype)
    d_after, gain_ffn_three = ffn_backward(
        after_three, gain_ffn, w_gate, w_up, w_down, d_ffn_all.at[in_three], gate_three, up_three,
        d_gate_all.at[in_three], d_up_all.at[in_three], total_three, CHUNK,
    )
    d_attn_all[in_three, :MODEL] = (d_change + d_after).astype(narrow_dtype)
    d_rows, gain_attn_three, router_three = attention_backward(
        state_three, gain_attn, small[4:5], cos_three[...], sin_three[...], bias_three, w_attn, normed_rest.at[three],
        qk_three, v_three, log_three, d_attn_all[in_three, :MODEL], d_gating, gating_three, d_att_three, d_raw_three,
        d_qk_rest.at[three], d_v_rest.at[three],
    )
    back_three = pick_exact(put_three, d_rows + d_after)

    incoming_two = incoming_two + back_three
    d_change = gating_two * incoming_two
    d_gating = jnp.sum(change_two * incoming_two, axis=-1, keepdims=True)
    d_ffn_all[in_two] = d_change.astype(narrow_dtype)
    d_after, gain_ffn_two = ffn_backward(
        after_two, gain_ffn, w_gate, w_up, w_down, d_ffn_all.at[in_two], gate_two, up_two,
        d_gate_all.at[in_two], d_up_all.at[in_two], total_two, CHUNK,
    )
    d_attn_all[in_two, :MODEL] = (d_change + d_after).astype(narrow_dtype)
    d_rows, gain_attn_two, router_two = attention_backward(
        state_two, gain_attn, small[3:4], cos_two[...], sin_two[...], bias_two, w_attn, normed_rest.at[two],
        qk_two, v_two, log_two, d_attn_all[in_two, :MODEL], d_gating, gating_two, d_att_two, d_raw_two,
        d_qk_rest.at[two], d_v_rest.at[two],
    )
    back_two = back_three + d_rows + d_after

    incoming = cotangent[...].astype(wide_type) + pick_exact(put_two, back_two)
    d_input_ref[...] = incoming
    d_change = scale_one * incoming
    d_gating = jnp.where(valid, jnp.sum(total_one[...] * incoming, axis=-1, keepdims=True), 0.0)
    d_gating_ref[...] = jnp.broadcast_to(d_gating, d_gating_ref.shape)
    d_ffn_all[in_one] = d_change.astype(narrow_dtype)
    after_one = hidden_in[...].astype(wide_type) + attn_out_ref[...]
    d_after, gain_ffn_one = ffn_backward(
        after_one, gain_ffn, w_gate, w_up, w_down, d_ffn_all.at[in_one], gate_one, up_one,
        d_gate_all.at[in_one], d_up_all.at[in_one], total_one, CHUNK,
    )
    d_attn_all[in_one, :MODEL] = (scale_one * d_input_ref[...] + d_after).astype(narrow_dtype)
    d_input_ref[...] += d_after
    small_out[...] = jnp.zeros_like(small_out)
    small_out[0:1] = gain_attn_two + gain_attn_three
    small_out[1:2] = gain_ffn_one + gain_ffn_two + gain_ffn_three
    small_out[3:4] = router_two
    small_out[4:5] = router_three
    d_ffn_t_ref[...] = d_ffn_all[...].T
    ffn_t_ref[...] = ffn_all[...].T


def rotary_tables(positions):
    half = HEAD_SIZE // 2
    lanes = jnp.arange(2 * HEAD_SIZE)
    frequency = 10000.0 ** (-(lanes % half).astype(wide_type) / half)
    angles = positions.astype(wide_type)[:, None] * frequency[None, :]
    sign = jnp.where(lanes % HEAD_SIZE < half, -1.0, 1.0)
    return jnp.cos(angles), jnp.sin(angles) * sign[None, :]


def call(kernel, operands, outputs, limit, scratch=(), hbm=0, scalars=1):
    specs = [
        pl.BlockSpec(memory_space=pltpu.SMEM if i < scalars else (pl.ANY if i >= len(operands) - hbm else pltpu.VMEM))
        for i in range(len(operands))
    ]
    return pl.pallas_call(
        kernel,
        out_shape=[jax.ShapeDtypeStruct(shape, kind) for shape, kind in outputs],
        in_specs=specs,
        out_specs=[pl.BlockSpec(memory_space=pltpu.VMEM)] * len(outputs),
        scratch_shapes=list(scratch),
        compiler_params=pltpu.CompilerParams(vmem_limit_bytes=limit * 2**20),
        cost_estimate=pl.CostEstimate(flops=1000, bytes_accessed=1000, transcendentals=0),
    )(*operands)


def partner(value, axis, bit):
    count = lax.axis_size(axis)
    return lax.ppermute(value, axis, [(i, i ^ bit) for i in range(count)])


def after(value, *others):
    return lax.optimization_barrier((value,) + others)[0]


def bits_of(axis, low):
    found = []
    bit = low
    while bit < lax.axis_size(axis):
        found.append(bit)
        bit = bit * 2
    return found


CORE, ROW, LAYER = 1, 2, 4


class Place:
    def __init__(self, model_rows, ff):
        group = lax.axis_index("dp")
        self.owners = lax.axis_size("fsdp")
        self.layers = lax.axis_size("dp") // LAYER
        self.blocks = self.owners == 2 and model_rows % 32 == 0 and ff % (128 * self.layers) == 0
        self.scalars = (lax.axis_index("fsdp"), group % 2, group // ROW % 2, group // LAYER)
        self.vector = jnp.stack(self.scalars).astype(jnp.int32)


def local_step(place, fn, operands, outputs, limit):
    shapes = [((count, rows, columns), kind) for count, rows, columns, kind in outputs]

    def kernel(at_ref, *refs):
        made = fn(tuple(at_ref[i] for i in range(4)), *refs[: len(operands)])
        for blocks, ref in zip(made, refs[len(operands) :]):
            for i, block in enumerate(blocks):
                ref[i] = block.astype(ref.dtype)

    return call(kernel, (place.vector,) + tuple(operands), shapes, limit)


def wide_sum(*blocks):
    total = blocks[0].astype(wide_type)
    for block in blocks[1:]:
        total = total + block.astype(wide_type)
    return total


class Part:
    def __init__(self, place, product, rows, columns, tall=False, extra=None):
        self.place, self.product, self.rows, self.columns, self.tall = place, product, rows, columns, tall
        self.extra, self.tail = extra, 0 if extra is None else 8
        self.count = 2 * place.layers

    def out(self, count):
        return (count, self.rows + self.tail, self.columns, narrow_dtype)

    def step(self, fn, operands, counts, limit=12):
        return local_step(self.place, fn, operands, [self.out(count) for count in counts], limit)

    def blocks(self, value):
        r, c = self.rows, self.columns
        if self.tall:
            return [value[i * r : (i + 1) * r] for i in range(self.count)]
        return [value[y * r : (y + 1) * r, z * c : (z + 1) * c] for y in range(2) for z in range(self.place.layers)]

    def made(self, owner, core, refs):
        found = self.blocks(self.product(owner, core, *refs))
        if self.tail:
            below = self.extra(owner, *refs)
            found = [jnp.concatenate([block, below], axis=0) for block in found]
        return found

    def away(self, *operands):
        def fn(at, *refs):
            made = []
            for offset in range(self.place.owners):
                blocks = self.made(at[0] ^ offset, 1 - at[1], refs)
                made += [blocks[i : i + 2] for i in range(0, len(blocks), 2)]
            return made

        counts = [2] * (self.count // 2)
        return self.step(fn, operands, counts * self.place.owners, 24)

    def keep(self, received, *operands):
        each = len(received) // self.place.owners

        def fn(at, *refs):
            refs, received = refs[: len(operands)], refs[len(operands) :]
            made = []
            for offset in range(self.place.owners):
                blocks = self.made(at[0] ^ offset, at[1], refs)
                made.append([wide_sum(block, received[offset * each + i // 2][i % 2]) for i, block in enumerate(blocks)])
            return made

        return self.step(fn, tuple(operands) + tuple(received), [self.count] * self.place.owners, 24)

    def send_x(self, parts):
        return [parts[0]] + [partner(part, "fsdp", offset) for offset, part in enumerate(parts) if offset]

    def add_x(self, parts):
        def fn(at, *refs):
            layers = self.place.layers
            return [
                [wide_sum(*(ref[row * layers + z] for ref in refs)) for z in range(layers)] for row in (at[2], 1 - at[2])
            ]

        return self.step(fn, parts, [self.place.layers] * 2)

    def send_y(self, parts):
        return [parts[0], partner(parts[1], "dp", ROW)]

    def add_y(self, parts):
        def fn(at, *refs):
            layers = self.place.layers
            return [[wide_sum(*(ref[at[3] ^ offset] for ref in refs))] for offset in range(layers)]

        return self.step(fn, parts, [1] * self.place.layers)

    def send_z(self, parts):
        return [parts[0]] + [partner(part, "dp", offset * LAYER) for offset, part in enumerate(parts) if offset]

    def add_z(self, parts):
        def fn(at, *refs):
            total = wide_sum(*(ref[0] for ref in refs))
            return [[total[: self.rows]], [total[self.rows :]]][: 1 + (self.tail > 0)]

        outputs = [(1, self.rows, self.columns, narrow_dtype), (1, self.tail, self.columns, wide_type)]
        return local_step(self.place, fn, parts, outputs[: 1 + (self.tail > 0)], 12)

    def back_z(self, piece):
        return [piece] + [partner(piece, "dp", offset * LAYER) for offset in range(1, self.place.layers)]

    def join_z(self, parts):
        outputs = [(self.place.layers, self.rows, self.columns, narrow_dtype)]
        return local_step(self.place, lambda at, *refs: [[ref[0] for ref in refs]], parts, outputs, 12)[0]

    def back_y(self, value):
        return [value, partner(value, "dp", ROW)]

    def back_core(self, values):
        return values + [partner(value, "dp", CORE) for value in values]

    def spots(self, at, stacked):
        layers, found = self.place.layers, []
        for core in range(2):
            for row in range(2):
                for z in range(layers):
                    if stacked:
                        source, index = (0, (z * 2 + row) * 2 + core)
                        c, y, layer = core, row, z
                    else:
                        source, index = (core * 2 + row, z)
                        c, y, layer = at[1] ^ core, at[2] ^ row, at[3] ^ z
                    if self.tall:
                        found.append((source, index, (y * layers + layer) * self.rows, c * self.columns))
                    else:
                        found.append((source, index, (c * 2 + y) * self.rows, layer * self.columns))
        return found

    def final(self, values, kind, cuts=None):
        place, stacked = self.place, len(values) == 1
        shape = (self.rows * 4, self.columns * place.layers)
        if self.tall:
            shape = (self.rows * self.count, self.columns * 2)
        def kernel(at_ref, *refs):
            out = refs[-1]
            outs = refs[len(values) : -1]
            for source, index, row, column in self.spots(tuple(at_ref[i] for i in range(4)), stacked):
                if not stacked:
                    row, column = pl.multiple_of(row, 8), pl.multiple_of(column, 128)
                out[pl.ds(row, self.rows), pl.ds(column, self.columns)] = refs[source][index].astype(kind)
            for (start, stop, turned), ref in zip(cuts or (), outs):
                piece = out[:, start:stop]
                ref[...] = piece.T if turned else piece

        if cuts is None:
            return call(kernel, (place.vector,) + tuple(values), [(shape, kind)], 20)[0]
        shapes = [
            ((stop - start, shape[0]) if turned else (shape[0], stop - start), kind) for start, stop, turned in cuts
        ]
        return call(kernel, (place.vector,) + tuple(values), shapes, 28, [pltpu.VMEM(shape, kind)])


class Order:
    def __init__(self):
        self.last = None

    def hold(self, value):
        return value if self.last is None else after(value, self.last)

    def step(self, work, values):
        result = work([self.hold(values[0])] + list(values[1:]))
        self.last = result[0] if isinstance(result, (list, tuple)) else result
        return result


def reduce_all(parts, operands, order, beside, cuts, stacked):
    count = len(parts)
    done, pieces, cores = ([None] * count for _ in range(3))
    extras = []

    def produce(k):
        taken = operands[k]()
        away = order.step(lambda values: parts[k].away(*values), taken)
        received = [partner(value, "dp", CORE) for value in away]
        return order.step(lambda values: parts[k].keep(received, *values), taken)

    waiting = produce(0)
    x_parts = parts[0].send_x(waiting)
    beside()
    waiting = produce(1)
    for k in range(count + 3):
        if k < count:
            y_parts = parts[k].send_y(order.step(parts[k].add_x, x_parts))
        if k + 1 < count:
            x_parts = parts[k + 1].send_x([order.hold(part) for part in waiting])
        if 1 <= k <= count:
            piece, *more = order.step(parts[k - 1].add_z, z_parts)
            extras += more
            if k - 1 in stacked:
                pieces[k - 1] = lax.all_gather(piece[0], "dp", axis=0)
            else:
                pieces[k - 1] = parts[k - 1].back_z(piece)
        if 2 <= k <= count + 1 and k - 2 not in stacked:
            own, moved = back
            cores[k - 2] = parts[k - 2].back_core([order.hold(own), order.hold(moved)])
        if k + 2 < count:
            waiting = produce(k + 2)
        if k >= 3:
            values = [pieces[k - 3]] if k - 3 in stacked else cores[k - 3]
            done[k - 3] = order.step(lambda values: parts[k - 3].final(values, wide_type, cuts[k - 3]), values)
        if k < count:
            z_parts = parts[k].send_z(order.step(parts[k].add_y, y_parts))
        if 1 <= k <= count and k - 1 not in stacked:
            back = parts[k - 1].back_y(order.step(parts[k - 1].join_z, pieces[k - 1]))
    return done, extras


def reduce_plain(matrices):
    return [
        lax.psum(lax.psum_scatter(matrix, "fsdp", scatter_dimension=dim, tiled=True), "dp").astype(wide_type)
        for matrix, dim in matrices
    ]


class Fetch:
    def __init__(self, operands, blocks):
        self.operands, self.blocks, self.count = operands, blocks, len(operands)

    def scratch(self):
        return pltpu.SemaphoreType.DMA((len(self.blocks),))

    def start(self, at_ref, sources, targets, sems):
        at = tuple(at_ref[i] for i in range(4))
        copies = {}
        for number, (target, operand, index, spot, (rows, columns)) in enumerate(self.blocks):
            source = sources[operand] if index is None else sources[operand].at[index]
            lead, row, column = spot(at)
            row = row if isinstance(row, int) else pl.multiple_of(row, 16)
            column = column if isinstance(column, int) else pl.multiple_of(column, 128)
            place = lead + (pl.ds(row, rows), pl.ds(column, columns))
            copy = pltpu.make_async_copy(source, targets[target].at[place], sems.at[number])
            copy.start()
            copies.setdefault(target, []).append(copy)
        return copies


def attention_shard_kernel(at_ref, query, key_t, out, value_t, low_ref, half_ref):
    start = 0
    for block in (query[...], key_t[...].T, out[...], value_t[...].T):
        low_ref[:, start : start + block.shape[1]] = block.astype(narrow_dtype)
        start += block.shape[1]
    rows = half_ref.shape[0]
    half_ref[...] = low_ref[pl.ds(pl.multiple_of(at_ref[1] * rows, 16), rows), :]


def down_shard_kernel(at_ref, down_t, low_ref, half_ref):
    low_ref[...] = down_t[...].astype(narrow_dtype)
    columns = half_ref.shape[1]
    half_ref[...] = low_ref[:, pl.ds(pl.multiple_of(at_ref[1] * columns, 128), columns)]


def narrow_kernel(wide_ref, narrow_ref):
    narrow_ref[...] = wide_ref[...].astype(narrow_dtype)


def narrowed(values):
    rows, columns = values[0].shape
    spec = pl.BlockSpec((rows, CHUNK), lambda i: (0, i))
    return pl.pallas_call(
        narrow_kernel,
        grid=(columns // CHUNK,),
        out_shape=jax.ShapeDtypeStruct((rows, columns), narrow_dtype),
        in_specs=[spec],
        out_specs=spec,
        compiler_params=pltpu.CompilerParams(vmem_limit_bytes=16 * 2**20),
        cost_estimate=pl.CostEstimate(flops=1000, bytes_accessed=1000, transcendentals=0),
    )(values[0])


def gather_weights(place, order, small, attn, pair, down_t, beside):
    mine, core, row, layer = place.scalars
    layers = place.layers
    model_rows, ff = pair[0].shape
    model, down_columns = down_t.shape
    low = lambda value: value.astype(narrow_dtype)
    attn_width = sum(value.shape[1] for value in attn)
    if not place.blocks:
        attn_full, gate, up, down_full = (
            lax.all_gather(low(value), "fsdp", axis=axis, tiled=True)
            for value, axis in ((jnp.concatenate(attn, axis=1), 0), (pair[0], 0), (pair[1], 0), (down_t, 1))
        )
        zero = lambda at: ((), 0, 0)
        first = Fetch([attn_full], [("attn", 0, None, zero, attn_full.shape)])
        every = Fetch(
            [attn_full, gate, up, down_full],
            [
                ("pair", 1, None, lambda at: ((0,), 0, 0), gate.shape),
                ("pair", 2, None, lambda at: ((1,), 0, 0), up.shape),
                ("down", 3, None, zero, down_full.shape),
                ("attn", 0, None, zero, attn_full.shape),
            ],
        )
        beside(first, lax.all_gather(small, "fsdp", axis=1, tiled=True))
        return first, every
    columns = ff // layers
    half = model_rows // 2
    half_columns = down_columns // 2
    own_piece = jnp.where(
        row == 0,
        lax.dynamic_slice(pair[0], (core * half, layer * columns), (half, columns)),
        lax.dynamic_slice(pair[1], (core * half, layer * columns), (half, columns)),
    )
    small_block = jnp.pad(small, ((0, 0), (0, columns - small.shape[1])))
    own_piece = jnp.concatenate([low(own_piece), small_block], axis=0)
    piece = partner(own_piece, "fsdp", 1)
    order.last = own_piece
    attn_low, attn_half = order.step(
        lambda values: call(
            attention_shard_kernel,
            [place.vector] + values,
            [((model_rows, attn_width), narrow_dtype), ((half, attn_width), narrow_dtype)],
            24,
        ),
        [attn[0], attn[1].T, attn[2], attn[3].T],
    )
    piece = order.hold(piece)
    order.last = piece
    pieces = [[piece] + [partner(piece, "dp", offset * LAYER) for offset in range(1, layers)]]
    pieces.append([partner(piece, "dp", ROW)])
    attn_near = partner(after(attn_half, piece), "fsdp", 1)
    down_low, down_half = order.step(
        lambda values: call(
            down_shard_kernel,
            [place.vector] + values,
            [(down_t.shape, narrow_dtype), ((model, half_columns), narrow_dtype)],
            24,
        ),
        [down_t],
    )
    gate_low = order.step(narrowed, [pair[0]])
    up_low = order.step(narrowed, [pair[1]])
    for moved in pieces[0][1:]:
        moved = order.hold(moved)
        pieces[1].append(partner(moved, "dp", ROW))
        order.last = moved
    attn_near = order.hold(attn_near)
    down_near = partner(after(down_half, attn_near), "fsdp", 1)
    attn_other = partner(attn_near, "dp", CORE)

    def halves(target, first):
        size = (half, attn_width)
        return [
            (target, first, None, lambda at: ((), at[0] * model_rows, 0), (model_rows, size[1])),
            (target, first + 1, None, lambda at: ((), (1 - at[0]) * model_rows + at[1] * half, 0), size),
            (target, first + 2, None, lambda at: ((), (1 - at[0]) * model_rows + (1 - at[1]) * half, 0), size),
        ]

    first = Fetch([attn_low, attn_near, attn_other], halves("attn", 0))
    order.last = attn_other
    small_other = piece[half:, : small.shape[1]]
    small_rows = jnp.where(
        mine == 0, jnp.concatenate([small, small_other], axis=1), jnp.concatenate([small_other, small], axis=1)
    )
    beside(first, small_rows)
    pieces[1] = [order.hold(moved) for moved in pieces[1]]
    pieces += [[partner(moved, "dp", CORE) for moved in group] for group in pieces]
    order.last = pieces[1][-1]
    down_near = order.hold(down_near)
    down_other = partner(down_near, "dp", CORE)
    blocks = [
        ("pair", 6, None, lambda at: ((0,), at[0] * model_rows, 0), (model_rows, ff)),
        ("pair", 7, None, lambda at: ((1,), at[0] * model_rows, 0), (model_rows, ff)),
    ]
    for number in range(4):
        for offset in range(layers):

            def spot(at, number=number, offset=offset):
                lead = (at[2] ^ (number % 2),)
                return (lead, (1 - at[0]) * model_rows + (at[1] ^ (number // 2)) * half, (at[3] ^ offset) * columns)

            blocks.append(("pair", 8 + number * layers + offset, (pl.ds(0, half),), spot, (half, columns)))
    near = (model, half_columns)
    blocks += [
        ("down", 3, None, lambda at: ((), 0, at[0] * down_columns), (model, down_columns)),
        ("down", 4, None, lambda at: ((), 0, (1 - at[0]) * down_columns + at[1] * half_columns), near),
        ("down", 5, None, lambda at: ((), 0, (1 - at[0]) * down_columns + (1 - at[1]) * half_columns), near),
    ]
    blocks += halves("attn", 0)
    operands = [attn_low, attn_near, attn_other, down_low, down_near, down_other, gate_low, up_low] + sum(pieces, [])
    return first, Fetch(operands, blocks)


def local(
    hidden_in,
    cotangent,
    norm_attn,
    norm_ffn,
    router,
    w_query,
    key_weight,
    value_weight,
    w_out,
    w_gate,
    w_up,
    w_down,
    lengths,
    chosen_second,
    chosen_third,
):
    place = Place(*w_gate.shape)
    owners, layers = place.owners, place.layers
    mine = place.scalars[0]
    width = w_query.shape[1]
    kv_width = key_weight.shape[1]
    small = jnp.concatenate(
        [norm_attn[None, :], norm_ffn[None, :], router.T, jnp.zeros((11, norm_attn.shape[0]), wide_type)]
    ).astype(narrow_dtype)
    count_one, model = hidden_in.shape
    ff = w_gate.shape[1]
    attn_width = 2 * width + 2 * kv_width
    chosen_two, chosen_three = chosen_second[0], chosen_third[0]
    count_two, count_three = chosen_two.shape[0], chosen_three.shape[0]
    count_rest = count_two + count_three
    count_all = count_one + count_rest
    cos_one, sin_one = rotary_tables(jnp.arange(count_one))
    cos_two, sin_two = rotary_tables(chosen_two)
    cos_three, sin_three = rotary_tables(chosen_three)
    v_width = attn_width - V_START
    first_outputs, small_wide = [], None

    def first_attention(fetch, small_rows):
        nonlocal small_wide
        small_wide = small_rows[:8].astype(wide_type)
        first_outputs.extend(
            call(
                partial(first_attention_kernel, fetch),
                [lengths, place.vector, order.hold(hidden_in.T), cotangent.T, small_wide, cos_one, sin_one] + fetch.operands,
                [
                    ((count_one, model), narrow_dtype),
                    ((count_one, model), narrow_dtype),
                    ((count_one, model), narrow_dtype),
                    ((count_one, QK_WIDTH), narrow_dtype),
                    ((count_one, v_width), narrow_dtype),
                    ((count_one, model), narrow_dtype),
                    ((GROUP * count_one, 128), wide_type),
                    ((count_one, model), wide_type),
                    ((count_one, 128), wide_type),
                ],
                32,
                attn_scratch + [fetch.scratch()],
                hbm=fetch.count,
                scalars=2,
            )
        )
        order.last = first_outputs[0]

    order = Order()
    attn_scratch = [pltpu.VMEM((model, attn_width), narrow_dtype)]
    fetch_attn, fetch_all = gather_weights(
        place, order, small, (w_query, key_weight, w_out, value_weight), (w_gate, w_up), w_down.T, first_attention
    )
    hidden_rows, cotangent_rows, normed_one, qk_one, v_one, att_one, log_one, attn_out_one, gating_one = first_outputs
    rest = lambda width: ((count_rest, width), narrow_dtype)
    every = lambda width: ((count_all, width), narrow_dtype)
    turned = ((model, count_all), narrow_dtype)
    scratch_for = lambda count: [
        pltpu.VMEM((count, QK_WIDTH), narrow_dtype),
        pltpu.VMEM((count, v_width), narrow_dtype),
        pltpu.VMEM((GROUP * count, 128), wide_type),
    ]
    back_scratch = lambda count: [
        pltpu.VMEM((count, model), narrow_dtype),
        pltpu.VMEM((count, QK_WIDTH), wide_type),
    ]
    wide = lambda count, width: pltpu.VMEM((count, width), wide_type)
    attn_tiles = -(-model // 128) * 128
    (
        hidden_out, d_input, d_gating_one, small_middle, hidden, d_ffn_t, ffn_t, d_gate, d_up, d_attn,
        att_rest, normed_rest, d_qk_rest, d_v_rest,
    ) = call(
        partial(middle_kernel, fetch_all),
        [
            lengths, place.vector, hidden_rows, cotangent_rows, small_wide, attn_out_one, gating_one,
            cos_two, sin_two, cos_three, sin_three,
            chosen_two[:, None], chosen_two[None, :], chosen_three[:, None], chosen_three[None, :],
        ]
        + fetch_all.operands,
        [
            ((count_one, model), narrow_dtype), ((count_one, model), wide_type), ((count_one, 128), wide_type),
            ((8, model), wide_type), every(ff), turned, turned, every(ff), every(ff), every(attn_tiles),
            rest(model), rest(model), rest(QK_WIDTH), rest(v_width),
        ],
        60,
        [
            pltpu.VMEM((model, attn_width), narrow_dtype),
            pltpu.VMEM((2, model, ff), narrow_dtype),
            pltpu.VMEM((model, ff), narrow_dtype),
            fetch_all.scratch(),
            wide(count_one, ff), wide(count_one, ff), wide(count_two, ff), wide(count_two, ff),
            wide(count_three, ff), wide(count_three, ff),
            wide(count_one, model), wide(count_two, model), wide(count_three, model),
        ]
        + scratch_for(count_two) + scratch_for(count_three) + back_scratch(count_two) + back_scratch(count_three)
        + [pltpu.VMEM((count_all, model), narrow_dtype)] * 2,
        hbm=fetch_all.count,
        scalars=2,
    )

    small_tile = attn_width // layers
    attention = []

    def last_attention():
        attention.extend(
            call(
                partial(last_attention_kernel, fetch_attn),
                [
                    lengths, place.vector, hidden_rows, small_wide, cos_one, sin_one, normed_one, qk_one, v_one, att_one,
                    log_one, gating_one, d_gating_one, order.hold(d_attn), d_input, normed_rest, att_rest, d_qk_rest,
                    d_v_rest, small_middle,
                ]
                + fetch_attn.operands,
                [
                    every(QK_WIDTH), every(v_width), turned, turned, ((count_one, model), wide_type),
                    ((8, model), wide_type), ((owners, 8, small_tile), wide_type),
                ],
                40,
                back_scratch(count_one) + attn_scratch + [fetch_attn.scratch()],
                hbm=fetch_attn.count,
                scalars=2,
            )
        )
        order.last = attention[0]

    if not place.blocks:
        last_attention()
        d_qk, d_v, normed_t, att_t, grad_hidden, small_all, _ = attention
        narrow_dot = lambda left, right: rows_dot(left, right).astype(narrow_dtype)
        skip = V_HEAD * HEAD_SIZE
        down_t, *reduced = reduce_plain(
            [
                (narrow_dot(d_ffn_t, hidden), 1),
                (narrow_dot(ffn_t, d_gate), 0),
                (narrow_dot(ffn_t, d_up), 0),
                (narrow_dot(normed_t, d_qk), 0),
                (narrow_dot(att_t, d_attn[:, :model]), 0),
                (narrow_dot(normed_t, d_v[:, skip:]), 0),
            ]
        )
        small_all = lax.psum_scatter(lax.psum(small_all, "dp"), "fsdp", scatter_dimension=1, tiled=True)
        return (
            hidden_out, grad_hidden, small_all[0], small_all[1], small_all[2:5].T,
            reduced[2][:, :width], reduced[2][:, width:], reduced[4], reduced[3], reduced[0], reduced[1], down_t.T,
        )
    by_core = lambda left: left.reshape(owners * 2, model // owners // 2, left.shape[1])
    size = ff // owners // 2

    def down_product(owner, core, left, right):
        return rows_dot(left[...], right[:, pl.ds(pl.multiple_of((owner * 2 + core) * size, 128), size)])

    def plain_product(owner, core, left, right):
        return rows_dot(left[owner * 2 + core], right[...])

    def small_block(owner, normed, d_qk, att, d_attn, d_v, small_parts):
        return small_parts[owner]

    def attention_product(owner, core, normed, d_qk, att, d_attn, d_v, small_parts):
        left = normed[owner * 2 + core]
        out = rows_dot(att[owner * 2 + core], d_attn[...])
        value = rows_dot(left, d_v[...])
        shared = attn_tiles - 128
        return jnp.concatenate(
            [rows_dot(left, d_qk[...]), out[:, :shared], out[:, shared:] + value[:, :128], value[:, 128:]], axis=1
        )

    rows = model // owners // 4
    parts = [
        Part(place, down_product, model // 2 // layers, size, tall=True),
        Part(place, plain_product, rows, ff // layers),
        Part(place, plain_product, rows, ff // layers),
        Part(place, attention_product, rows, attn_width // layers, extra=small_block),
    ]
    operands = [
        lambda: [d_ffn_t, hidden],
        lambda: [by_core(ffn_t), d_gate],
        lambda: [by_core(ffn_t), d_up],
        lambda: [by_core(attention[2]), attention[0], by_core(attention[3]), d_attn, attention[1], attention[6]],
    ]
    cuts = [
        (0, width, False),
        (width, width + kv_width, True),
        (width + kv_width, 2 * width + kv_width, False),
        (2 * width + kv_width, attn_width, True),
    ]
    reduced, small_sum = reduce_all(parts, operands, order, last_attention, [None, None, None, cuts], STACKED)
    down_t, gate_shard, up_shard, (query_shard, key_t, out_shard, value_t) = reduced
    grad_hidden, small_sum = attention[4], small_sum[0][0][:, : model // owners]
    return (
        hidden_out,
        grad_hidden,
        small_sum[0],
        small_sum[1],
        small_sum[2:5].T,
        query_shard,
        key_t.T,
        value_t.T,
        out_shard,
        gate_shard,
        up_shard,
        down_t.T,
    )


def solution(mesh):
    in_specs = (
        P(("dp", "fsdp"), None),
        P(("dp", "fsdp"), None),
        P("fsdp"),
        P("fsdp"),
        P("fsdp", None),
        P("fsdp", None),
        P("fsdp", None),
        P("fsdp", None),
        P("fsdp", None),
        P("fsdp", None),
        P("fsdp", None),
        P("fsdp", None),
        P(("dp", "fsdp")),
        P(("dp", "fsdp"), None),
        P(("dp", "fsdp"), None),
    )
    out_specs = (
        P(("dp", "fsdp"), None),
        P(("dp", "fsdp"), None),
        P("fsdp"),
        P("fsdp"),
        P("fsdp", None),
        P("fsdp", None),
        P("fsdp", None),
        P("fsdp", None),
        P("fsdp", None),
        P("fsdp", None),
        P("fsdp", None),
        P("fsdp", None),
    )
    return jax.shard_map(local, mesh=mesh, in_specs=in_specs, out_specs=out_specs, check_vma=False)
```

```python
from functools import partial

import jax
import jax.numpy as jnp
from jax import lax
from jax.experimental import pallas as pl
from jax.experimental.pallas import tpu as pltpu
from jax.sharding import PartitionSpec as P

QUERY_HEADS = 15
KEY_VALUE_HEADS = 5
HEAD_SIZE = 64
GROUP = QUERY_HEADS // KEY_VALUE_HEADS
MODEL = QUERY_HEADS * HEAD_SIZE
QK_WIDTH = (QUERY_HEADS + KEY_VALUE_HEADS) * HEAD_SIZE
V_START = QK_WIDTH + MODEL - HEAD_SIZE
V_HEAD = 1
SCALE = HEAD_SIZE ** (-0.5)

PIECE = 4

epsilon = 1e-05
negative = -1e30
narrow_dtype = jnp.bfloat16
wide_type = jnp.float32


def rows_dot(left, right):
    return lax.dot_general(left, right, (((1,), (0,)), ((), ())), preferred_element_type=wide_type)


def rows_dot_t(left, right):
    return lax.dot_general(left, right, (((1,), (1,)), ((), ())), preferred_element_type=wide_type)


def columns_dot(left, right):
    return lax.dot_general(left, right, (((0,), (0,)), ((), ())), preferred_element_type=wide_type)


def inverse_rms(rows):
    return lax.rsqrt(jnp.mean(rows * rows, axis=-1, keepdims=True) + epsilon)


def norm_back(rows, inverse, gain, incoming):
    weighted = incoming * gain
    mean = jnp.mean(weighted * rows, axis=-1, keepdims=True)
    d_rows = inverse * weighted - rows * (inverse * inverse * inverse * mean)
    return d_rows, jnp.sum(incoming * rows * inverse, axis=0, keepdims=True)


def rotate(block, cosines, sines):
    lanes = lax.broadcasted_iota(jnp.int32, block.shape, 1)
    swapped = jnp.where(lanes % HEAD_SIZE < HEAD_SIZE // 2, pltpu.roll(block, 96, 1), pltpu.roll(block, 32, 1))
    return block * cosines + swapped * sines


def causal_bias(count, length):
    row = lax.broadcasted_iota(jnp.int32, (count, count), 0)
    column = lax.broadcasted_iota(jnp.int32, (count, count), 1)
    allowed = column <= row
    if length is not None:
        allowed = allowed & (column < length)
    bias = jnp.where(allowed, 0.0, negative)
    return jnp.concatenate([bias] * GROUP, axis=0)


def head_columns(ref, first, count):
    return jnp.concatenate(
        [ref[:, (first + i) * HEAD_SIZE : (first + i + 1) * HEAD_SIZE] for i in range(count)], axis=0
    )


def attention_forward(rows, gain, router_row, cosines, sines, bias, weight, normed_ref, qk_ref, v_ref, att_ref, log_ref):
    count = rows.shape[0]
    normed_ref[...] = (rows * inverse_rms(rows) * gain).astype(narrow_dtype)
    normed = normed_ref[...]
    gating = jax.nn.sigmoid(jnp.sum(normed.astype(wide_type) * router_row, axis=-1, keepdims=True))
    for block in range(QK_WIDTH // 256):
        product = rows_dot(normed, weight[:, block * 256 : (block + 1) * 256])
        for part in range(2):
            piece = rotate(product[:, part * 128 : (part + 1) * 128], cosines, sines)
            at = block * 256 + part * 128
            qk_ref[:, at : at + 128] = piece.astype(narrow_dtype)
    v_ref[...] = rows_dot(normed, weight[:, V_START:]).astype(narrow_dtype)
    for head in range(KEY_VALUE_HEADS):
        queries = head_columns(qk_ref, head * GROUP, GROUP)
        keys = head_columns(qk_ref, QUERY_HEADS + head, 1)
        values = head_columns(v_ref, V_HEAD + head, 1)
        scores = rows_dot_t(queries, keys) * SCALE + bias
        peak = jnp.max(scores, axis=-1, keepdims=True)
        expanded = jnp.exp(scores - peak)
        total = jnp.sum(expanded, axis=-1, keepdims=True)
        log_ref[:, head : head + 1] = peak + jnp.log(total)
        attended = rows_dot((expanded / total).astype(narrow_dtype), values).astype(narrow_dtype)
        for i in range(GROUP):
            at = (head * GROUP + i) * HEAD_SIZE
            att_ref[:, at : at + HEAD_SIZE] = attended[i * count : (i + 1) * count]
    return rows_dot(att_ref[...], weight[:, QK_WIDTH : QK_WIDTH + MODEL]), gating


def attention_backward(
    rows, gain, router_row, cosines, sines, bias, weight, normed_ref, qk_ref, v_ref, log_ref,
    d_attn_low, d_gating, gating, d_att_ref, d_raw_ref, d_qk_ref, d_v_ref,
):
    count = rows.shape[0]
    d_att_ref[...] = rows_dot_t(d_attn_low, weight[:, QK_WIDTH : QK_WIDTH + MODEL]).astype(narrow_dtype)
    d_v_ref[...] = jnp.zeros_like(d_v_ref)
    for head in range(KEY_VALUE_HEADS):
        queries = head_columns(qk_ref, head * GROUP, GROUP)
        keys = head_columns(qk_ref, QUERY_HEADS + head, 1)
        values = head_columns(v_ref, V_HEAD + head, 1)
        d_attended = head_columns(d_att_ref, head * GROUP, GROUP)
        scores = rows_dot_t(queries, keys) * SCALE + bias
        probabilities = jnp.exp(scores - log_ref[:, head : head + 1])
        d_probs = rows_dot_t(d_attended, values)
        row_dot = jnp.sum(probabilities * d_probs, axis=-1, keepdims=True)
        d_raw = (probabilities * (d_probs - row_dot) * SCALE).astype(narrow_dtype)
        d_queries = rows_dot(d_raw, keys)
        for i in range(GROUP):
            at = (head * GROUP + i) * HEAD_SIZE
            d_raw_ref[:, at : at + HEAD_SIZE] = d_queries[i * count : (i + 1) * count]
        at = (QUERY_HEADS + head) * HEAD_SIZE
        d_raw_ref[:, at : at + HEAD_SIZE] = columns_dot(queries, d_raw).T
        at = (V_HEAD + head) * HEAD_SIZE
        d_values = columns_dot(d_attended, probabilities.astype(narrow_dtype)).T
        d_v_ref[:, at : at + HEAD_SIZE] = d_values.astype(narrow_dtype)
    for block in range(QK_WIDTH // 128):
        at = block * 128
        d_qk_ref[:, at : at + 128] = rotate(d_raw_ref[:, at : at + 128], cosines, -sines).astype(narrow_dtype)
    d_normed = rows_dot_t(d_qk_ref[...], weight[:, :QK_WIDTH]) + rows_dot_t(d_v_ref[...], weight[:, V_START:])
    d_logit = d_gating * gating * (1.0 - gating)
    d_normed = d_normed + d_logit * router_row
    router_gradient = jnp.sum(d_logit * normed_ref[...].astype(wide_type), axis=0, keepdims=True)
    d_rows, gain_gradient = norm_back(rows, inverse_rms(rows), gain, d_normed)
    return d_rows, gain_gradient, router_gradient


def ffn_forward(after, gain, w_gate, w_up, w_down, ffn_ref, hidden_ref, gate_ref=None, up_ref=None, ready=()):
    ffn_ref[...] = (after * inverse_rms(after) * gain).astype(narrow_dtype)
    gate = rows_dot(ffn_ref[...], w_gate[...])
    up = rows_dot(ffn_ref[...], w_up[...])
    if gate_ref is not None:
        gate_ref[...] = gate
        up_ref[...] = up
    hidden_ref[...] = (gate * jax.nn.sigmoid(gate) * up).astype(narrow_dtype)
    for copy in ready:
        copy.wait()
    return rows_dot_t(hidden_ref[...], w_down[...])


def ffn_backward(after, gain, w_gate, w_up, w_down, d_ffn_ref, gate, up, d_gate_ref, d_up_ref):
    d_hidden = rows_dot(d_ffn_ref[...], w_down[...])
    sig = jax.nn.sigmoid(gate)
    d_gate_ref[...] = (d_hidden * up * sig * (1.0 + gate * (1.0 - sig))).astype(narrow_dtype)
    d_up_ref[...] = (d_hidden * gate * sig).astype(narrow_dtype)
    total = rows_dot_t(d_gate_ref[...], w_gate[...]) + rows_dot_t(d_up_ref[...], w_up[...])
    return norm_back(after, inverse_rms(after), gain, total)


def pick_exact(selector, rows):
    high = rows.astype(narrow_dtype)
    rest = rows - high.astype(wide_type)
    middle = rest.astype(narrow_dtype)
    low = (rest - middle.astype(wide_type)).astype(narrow_dtype)
    return rows_dot(selector, high) + rows_dot(selector, middle) + rows_dot(selector, low)


def first_attention_kernel(
    fetch, length_ref, at_ref, hidden_t, cotangent_t, small, cosines, sines, *refs
):
    sources, refs = refs[: fetch.count], refs[fetch.count :]
    hidden_in, cotangent, normed_ref, qk_ref, v_ref, att_ref, log_ref, out_ref, gating_ref, weight, sems = refs
    hidden_in[...] = hidden_t[...].T
    cotangent[...] = cotangent_t[...].T
    copies = fetch.start(at_ref, sources, {"attn": weight}, sems)
    rows = hidden_in[...].astype(wide_type)
    for copy in copies["attn"]:
        copy.wait()
    bias = causal_bias(rows.shape[0], length_ref[0])
    attn_out, gating = attention_forward(
        rows, small[0:1], small[2:3], cosines[...], sines[...], bias, weight, normed_ref, qk_ref, v_ref, att_ref, log_ref
    )
    out_ref[...] = attn_out
    gating_ref[...] = jnp.broadcast_to(gating, gating_ref.shape)


def last_attention_kernel(
    fetch, length_ref, at_ref, hidden_in, small, cosines, sines, normed_ref, qk_ref, v_ref, att_ref, log_ref, gating_ref,
    d_gating_ref, d_attn_ref, d_input_ref, normed_rest, att_rest, d_qk_rest, d_v_rest, small_middle, *refs,
):
    sources, refs = refs[: fetch.count], refs[fetch.count :]
    d_qk_ref, d_v_ref, normed_t_ref, att_t_ref, grad_hidden_ref, small_out, small_parts, d_att_ref, d_raw_ref, weight, sems = refs
    copies = fetch.start(at_ref, sources, {"attn": weight}, sems)
    for copy in copies["attn"]:
        copy.wait()
    count = hidden_in.shape[0]
    one = pl.ds(0, count)
    rest = pl.ds(count, d_qk_ref.shape[0] - count)
    rows = hidden_in[...].astype(wide_type)
    bias = causal_bias(count, length_ref[0])
    d_rows, gain_gradient, router_gradient = attention_backward(
        rows, small[0:1], small[2:3], cosines[...], sines[...], bias, weight, normed_ref, qk_ref, v_ref, log_ref,
        d_attn_ref[one, :MODEL], d_gating_ref[:, 0:1], gating_ref[:, 0:1], d_att_ref, d_raw_ref, d_qk_ref.at[one], d_v_ref.at[one],
    )
    grad_hidden_ref[...] = d_input_ref[...] + d_rows
    small_out[...] = small_middle[...]
    small_out[0:1] += gain_gradient
    small_out[2:3] = router_gradient
    small_parts[...] = jnp.zeros_like(small_parts)
    size = MODEL // small_parts.shape[0]
    for owner in range(small_parts.shape[0]):
        small_parts[owner, :, 0:size] = small_out[:, owner * size : (owner + 1) * size]
    d_qk_ref[rest] = d_qk_rest[...]
    d_v_ref[rest] = d_v_rest[...]
    normed_t_ref[...] = jnp.concatenate([normed_ref[...], normed_rest[...]], axis=0).T
    att_t_ref[...] = jnp.concatenate([att_ref[...], att_rest[...]], axis=0).T


def middle_kernel(
    fetch, length_ref, at_ref, hidden_in, cotangent, small, attn_out_ref, gating_ref, cos_two, sin_two, cos_three, sin_three,
    row_two, row_three, *refs,
):
    sources, refs = refs[: fetch.count], refs[fetch.count :]
    (
        hidden_out, d_input_ref, d_gating_ref, small_out, hidden_all, d_ffn_t_ref, d_gate_rest, d_up_rest, d_attn_rest,
        att_rest, normed_rest, d_qk_rest, d_v_rest, ffn_one, ffn_rest, d_ffn_one,
        w_attn, w_pair, w_down, sems,
        gate_two, up_two, gate_three, up_three, change_one, change_two, change_three,
        qk_two, v_two, log_two, qk_three, v_three, log_three, d_att_two, d_raw_two, d_att_three, d_raw_three, d_ffn_rest,
    ) = refs
    copies = fetch.start(at_ref, sources, {"pair": w_pair, "down": w_down, "attn": w_attn}, sems)
    w_gate, w_up = w_pair.at[0], w_pair.at[1]
    count_two, count_three = row_two.shape[1], row_three.shape[1]
    count_one = hidden_in.shape[0]
    in_one, in_two = pl.ds(0, count_one), pl.ds(count_one, count_two)
    in_three = pl.ds(count_one + count_two, count_three)
    two = pl.ds(0, count_two)
    three = pl.ds(count_two, count_three)
    gain_attn, gain_ffn = small[0:1], small[1:2]

    def spread(row_ref):
        hit = lax.broadcasted_iota(jnp.int32, (count_one, row_ref.shape[1]), 0) == row_ref[...]
        return jnp.where(hit, 1.0, 0.0)

    put_two = spread(row_two)
    pick_two = put_two.T.astype(narrow_dtype)
    put_two = put_two.astype(narrow_dtype)
    put_three = rows_dot(pick_two, spread(row_three).astype(narrow_dtype))
    pick_three = put_three.T.astype(narrow_dtype)
    put_three = put_three.astype(narrow_dtype)

    after_one = hidden_in[...].astype(wide_type) + attn_out_ref[...]
    for copy in copies["pair"]:
        copy.wait()
    ffn_out = ffn_forward(
        after_one, gain_ffn, w_gate, w_up, w_down, ffn_one, hidden_all.at[in_one], ready=copies["down"]
    )
    valid = lax.broadcasted_iota(jnp.int32, (count_one, 1), 0) < length_ref[0]
    scale_one = jnp.where(valid, gating_ref[:, 0:1], 0.0)
    change_one[...] = attn_out_ref[...] + ffn_out
    d_input_ref[...] = hidden_in[...].astype(wide_type) + scale_one * change_one[...]

    for copy in copies["attn"]:
        copy.wait()
    d_attn_rest[...] = jnp.zeros_like(d_attn_rest)
    state_two = pick_exact(pick_two, d_input_ref[...])
    bias_two = causal_bias(count_two, None)
    attn_two, gating_two = attention_forward(
        state_two, gain_attn, small[3:4], cos_two[...], sin_two[...], bias_two, w_attn,
        normed_rest.at[two], qk_two, v_two, att_rest.at[two], log_two,
    )
    after_two = state_two + attn_two
    change_two[...] = attn_two + ffn_forward(
        after_two, gain_ffn, w_gate, w_up, w_down, ffn_rest.at[two], hidden_all.at[in_two], gate_two, up_two
    )
    delta_two = gating_two * change_two[...]

    state_three = pick_exact(pick_three, state_two + delta_two)
    bias_three = causal_bias(count_three, None)
    attn_three, gating_three = attention_forward(
        state_three, gain_attn, small[4:5], cos_three[...], sin_three[...], bias_three, w_attn,
        normed_rest.at[three], qk_three, v_three, att_rest.at[three], log_three,
    )
    after_three = state_three + attn_three
    change_three[...] = attn_three + ffn_forward(
        after_three, gain_ffn, w_gate, w_up, w_down, ffn_rest.at[three], hidden_all.at[in_three], gate_three, up_three
    )
    added = delta_two + pick_exact(put_three, gating_three * change_three[...])
    hidden_out[...] = (d_input_ref[...] + pick_exact(put_two, added)).astype(narrow_dtype)

    incoming_two = rows_dot(pick_two, cotangent[...])
    incoming_three = rows_dot(pick_three, incoming_two.astype(narrow_dtype))
    d_change = gating_three * incoming_three
    d_gating = jnp.sum(change_three[...] * incoming_three, axis=-1, keepdims=True)
    d_ffn_rest[three] = d_change.astype(narrow_dtype)
    d_after, gain_ffn_three = ffn_backward(
        after_three, gain_ffn, w_gate, w_up, w_down, d_ffn_rest.at[three], gate_three[...], up_three[...],
        d_gate_rest.at[three], d_up_rest.at[three],
    )
    d_attn_rest[three, :MODEL] = (d_change + d_after).astype(narrow_dtype)
    d_rows, gain_attn_three, router_three = attention_backward(
        state_three, gain_attn, small[4:5], cos_three[...], sin_three[...], bias_three, w_attn, normed_rest.at[three],
        qk_three, v_three, log_three, d_attn_rest[three, :MODEL], d_gating, gating_three, d_att_three, d_raw_three,
        d_qk_rest.at[three], d_v_rest.at[three],
    )
    back_three = pick_exact(put_three, d_rows + d_after)

    incoming_two = incoming_two + back_three
    d_change = gating_two * incoming_two
    d_gating = jnp.sum(change_two[...] * incoming_two, axis=-1, keepdims=True)
    d_ffn_rest[two] = d_change.astype(narrow_dtype)
    d_after, gain_ffn_two = ffn_backward(
        after_two, gain_ffn, w_gate, w_up, w_down, d_ffn_rest.at[two], gate_two[...], up_two[...],
        d_gate_rest.at[two], d_up_rest.at[two],
    )
    d_attn_rest[two, :MODEL] = (d_change + d_after).astype(narrow_dtype)
    d_rows, gain_attn_two, router_two = attention_backward(
        state_two, gain_attn, small[3:4], cos_two[...], sin_two[...], bias_two, w_attn, normed_rest.at[two],
        qk_two, v_two, log_two, d_attn_rest[two, :MODEL], d_gating, gating_two, d_att_two, d_raw_two,
        d_qk_rest.at[two], d_v_rest.at[two],
    )
    back_two = back_three + d_rows + d_after

    incoming = cotangent[...].astype(wide_type) + pick_exact(put_two, back_two)
    d_input_ref[...] = incoming
    d_gating = jnp.where(valid, jnp.sum(change_one[...] * incoming, axis=-1, keepdims=True), 0.0)
    d_gating_ref[...] = jnp.broadcast_to(d_gating, d_gating_ref.shape)
    d_ffn_one[...] = (scale_one * incoming).astype(narrow_dtype)
    small_out[...] = jnp.zeros_like(small_out)
    small_out[0:1] = gain_attn_two + gain_attn_three
    small_out[1:2] = gain_ffn_two + gain_ffn_three
    small_out[3:4] = router_two
    small_out[4:5] = router_three
    d_ffn_t_ref[...] = jnp.concatenate([d_ffn_one[...], d_ffn_rest[...]], axis=0).T


def last_ffn_kernel(
    fetch, length_ref, at_ref, hidden_in, small, attn_out_ref, gating_ref, d_input_in, d_ffn_one,
    ffn_one, ffn_rest, d_gate_rest, d_up_rest, d_attn_rest, small_middle, *refs,
):
    sources, refs = refs[: fetch.count], refs[fetch.count :]
    d_gate_all, d_up_all, d_attn_all, ffn_t_ref, d_input_ref, small_out, w_pair, w_down, sems = refs
    copies = fetch.start(at_ref, sources, {"pair": w_pair, "down": w_down}, sems)
    count = hidden_in.shape[0]
    one, rest = pl.ds(0, count), pl.ds(count, d_gate_all.shape[0] - count)
    d_gate_all[rest] = d_gate_rest[...]
    d_up_all[rest] = d_up_rest[...]
    d_attn_all[rest] = d_attn_rest[...]
    d_attn_all[one] = jnp.zeros((count, d_attn_all.shape[1]), narrow_dtype)
    ffn_t_ref[...] = jnp.concatenate([ffn_one[...], ffn_rest[...]], axis=0).T
    valid = lax.broadcasted_iota(jnp.int32, (count, 1), 0) < length_ref[0]
    scale = jnp.where(valid, gating_ref[:, 0:1], 0.0)
    after_one = hidden_in[...].astype(wide_type) + attn_out_ref[...]
    for copy in copies["pair"]:
        copy.wait()
    gate = rows_dot(ffn_one[...], w_pair[0])
    up = rows_dot(ffn_one[...], w_pair[1])
    for copy in copies["down"]:
        copy.wait()
    d_after, gain_gradient = ffn_backward(
        after_one, small[1:2], w_pair.at[0], w_pair.at[1], w_down, d_ffn_one, gate, up,
        d_gate_all.at[one], d_up_all.at[one],
    )
    d_attn_all[one, :MODEL] = (scale * d_input_in[...] + d_after).astype(narrow_dtype)
    d_input_ref[...] = d_input_in[...] + d_after
    small_out[...] = small_middle[...]
    small_out[1:2] += gain_gradient


def rotary_tables(positions):
    half = HEAD_SIZE // 2
    lanes = jnp.arange(2 * HEAD_SIZE)
    frequency = 10000.0 ** (-(lanes % half).astype(wide_type) / half)
    angles = positions.astype(wide_type)[:, None] * frequency[None, :]
    sign = jnp.where(lanes % HEAD_SIZE < half, -1.0, 1.0)
    return jnp.cos(angles), jnp.sin(angles) * sign[None, :]


def call(kernel, operands, outputs, limit, scratch=(), hbm=0, scalars=1):
    specs = [
        pl.BlockSpec(memory_space=pltpu.SMEM if i < scalars else (pl.ANY if i >= len(operands) - hbm else pltpu.VMEM))
        for i in range(len(operands))
    ]
    return pl.pallas_call(
        kernel,
        out_shape=[jax.ShapeDtypeStruct(shape, kind) for shape, kind in outputs],
        in_specs=specs,
        out_specs=[pl.BlockSpec(memory_space=pltpu.VMEM)] * len(outputs),
        scratch_shapes=list(scratch),
        compiler_params=pltpu.CompilerParams(vmem_limit_bytes=limit * 2**20),
        cost_estimate=pl.CostEstimate(flops=1000, bytes_accessed=1000, transcendentals=0),
    )(*operands)


def partner(value, axis, bit):
    count = lax.axis_size(axis)
    return lax.ppermute(value, axis, [(i, i ^ bit) for i in range(count)])


def after(value, *others):
    return lax.optimization_barrier((value,) + others)[0]


def bits_of(axis, low):
    found = []
    bit = low
    while bit < lax.axis_size(axis):
        found.append(bit)
        bit = bit * 2
    return found


CORE, ROW, LAYER = 1, 2, 4


class Place:
    def __init__(self, model_rows, ff):
        group = lax.axis_index("dp")
        self.owners = lax.axis_size("fsdp")
        self.layers = lax.axis_size("dp") // LAYER
        self.blocks = self.owners == 2 and self.layers == 4 and model_rows % 32 == 0 and ff % (128 * self.layers) == 0
        self.scalars = (lax.axis_index("fsdp"), group % 2, group // ROW % 2, group // LAYER)
        self.vector = jnp.stack(self.scalars).astype(jnp.int32)


def local_step(place, fn, operands, outputs, limit):
    shapes = [((count, rows, columns), kind) for count, rows, columns, kind in outputs]

    def kernel(at_ref, *refs):
        made = fn(tuple(at_ref[i] for i in range(4)), *refs[: len(operands)])
        for blocks, ref in zip(made, refs[len(operands) :]):
            for i, block in enumerate(blocks):
                ref[i] = block.astype(ref.dtype)

    return call(kernel, (place.vector,) + tuple(operands), shapes, limit)


def wide_sum(*blocks):
    total = blocks[0].astype(wide_type)
    for block in blocks[1:]:
        total = total + block.astype(wide_type)
    return total


class Part:
    def __init__(self, place, product, rows, columns, tall=False, extra=None):
        self.place, self.product, self.rows, self.columns, self.tall = place, product, rows, columns, tall
        self.extra, self.tail = extra, 0 if extra is None else 8
        self.count = 2 * place.layers

    def out(self, count):
        return (count, self.rows + self.tail, self.columns, narrow_dtype)

    def step(self, fn, operands, counts, limit=12):
        return local_step(self.place, fn, operands, [self.out(count) for count in counts], limit)

    def blocks(self, value):
        r, c = self.rows, self.columns
        if self.tall:
            return [value[i * r : (i + 1) * r] for i in range(self.count)]
        return [value[y * r : (y + 1) * r, z * c : (z + 1) * c] for y in range(2) for z in range(self.place.layers)]

    def made(self, owner, core, refs):
        found = self.blocks(self.product(owner, core, *refs))
        if self.tail:
            below = self.extra(owner, *refs)
            found = [jnp.concatenate([block, below], axis=0) for block in found]
        return found

    def away(self, operands, sides):
        def fn(at, *refs):
            blocks = sum((self.made(at[0] ^ offset, 1 - at[1], refs) for offset in sides), [])
            return [blocks[i : i + PIECE] for i in range(0, len(blocks), PIECE)]

        return self.step(fn, operands, [PIECE] * (len(sides) * self.count // PIECE), 24)

    def keep(self, received, operands, sides):
        def fn(at, *refs):
            received, refs = refs[: -len(operands)], refs[-len(operands) :]
            return [
                [
                    wide_sum(block, received[(number * self.count + i) // PIECE][i % PIECE])
                    for i, block in enumerate(self.made(at[0] ^ offset, at[1], refs))
                ]
                for number, offset in enumerate(sides)
            ]

        return self.step(fn, tuple(received) + tuple(operands), [self.count] * len(sides), 24)

    def add_x(self, values):
        def fn(at, keep, received):
            layers = self.place.layers
            return [
                [wide_sum(keep[row * layers + z], received[row * layers + z]) for z in range(layers)]
                for row in (at[2], 1 - at[2])
            ]

        return self.step(fn, values, [self.place.layers] * 2)

    def add_y(self, values):
        def fn(at, keep, received):
            odd = at[3] % 2
            return [[wide_sum(keep[2 * j + side], received[2 * j + side]) for j in range(2)] for side in (odd, 1 - odd)]

        return self.step(fn, values, [2, 2])

    def add_z(self, values):
        return self.step(lambda at, keep, received: [[wide_sum(keep[j], received[j]) for j in range(2)]], values, [2])[0]

    def add_last(self, values):
        def fn(at, keep, received):
            totals = [wide_sum(keep[j], received[j]) for j in range(2)]
            return [[total[: self.rows] for total in totals], [totals[0][self.rows :]]][: 1 + (self.tail > 0)]

        outputs = [(2, self.rows, self.columns, narrow_dtype), (1, self.tail, self.columns, wide_type)]
        return local_step(self.place, fn, values, outputs[: 1 + (self.tail > 0)], 12)

    def join_z(self, values):
        def fn(at, own, received):
            odd = at[3] % 2
            return [[jnp.where(odd == i % 2, own[i // 2], received[i // 2]) for i in range(4)]]

        return local_step(self.place, fn, values, [(4, self.rows, self.columns, narrow_dtype)], 12)[0]

    def final(self, values, kind, cuts=None):
        place = self.place
        shape = (self.rows * 4, self.columns * place.layers)
        if self.tall:
            shape = (self.rows * self.count, self.columns * 2)

        def kernel(at_ref, *refs):
            out = refs[-1]
            outs = refs[len(values) : -1]
            for source in range(4):
                core, y = at_ref[1] ^ (source // 2), at_ref[2] ^ (source % 2)
                for z in range(place.layers):
                    if self.tall:
                        row, column = (y * place.layers + z) * self.rows, pl.multiple_of(core * self.columns, 128)
                    else:
                        row, column = (core * 2 + y) * self.rows, z * self.columns
                    spot = (pl.ds(pl.multiple_of(row, 8), self.rows), pl.ds(column, self.columns))
                    out[spot] = refs[source][z].astype(kind)
            for (start, stop, turned), ref in zip(cuts or (), outs):
                piece = out[:, start:stop]
                ref[...] = piece.T if turned else piece

        if cuts is None:
            return call(kernel, (place.vector,) + tuple(values), [(shape, kind)], 20)[0]
        shapes = [
            ((stop - start, shape[0]) if turned else (shape[0], stop - start), kind) for start, stop, turned in cuts
        ]
        return call(kernel, (place.vector,) + tuple(values), shapes, 28, [pltpu.VMEM(shape, kind)])


class Order:
    def __init__(self):
        self.last = None

    def hold(self, value):
        return value if self.last is None else after(value, self.last)

    def step(self, work, values):
        result = work([self.hold(values[0])] + list(values[1:]))
        self.last = result[0] if isinstance(result, (list, tuple)) else result
        return result


def reduce_all(parts, operands, order, beside, cuts):
    count = len(parts)
    state = [{} for _ in parts]
    done, extras = [None] * count, []

    def step(k, work, *names):
        return order.step(work, [state[k][name] for name in names])

    def away(k, sides=(0, 1)):
        made = order.step(lambda values: parts[k].away(values, sides), operands[k]())
        state[k]["core"] = [partner(piece, "dp", CORE) for piece in made]

    def keep(k, sides=(0, 1)):
        taken = operands[k]()
        taken[0] = order.hold(taken[0])
        made = parts[k].keep(state[k]["core"], taken, sides)
        order.last = made[0]
        for side, value in zip(sides, made):
            state[k][("keep", "go")[side]] = value

    def start_x(k):
        state[k]["moved"] = partner(order.hold(state[k]["go"]), "fsdp", 1)

    away(0, (1,))
    going = state[0]["core"]
    away(0, (0,))
    staying, state[0]["core"] = state[0]["core"], going
    keep(0, (1,))
    start_x(0)
    state[0]["core"] = staying
    keep(0, (0,))
    beside[0]()
    away(1)
    keep(1)
    for k in range(count + 3):
        now, last, before = k < count, 1 <= k <= count, 2 <= k <= count + 1
        if now:
            state[k]["y"], moved = step(k, parts[k].add_x, "keep", "moved")
            state[k]["y moved"] = partner(moved, "dp", ROW)
        if k + 1 < count:
            start_x(k + 1)
        if 3 <= k:
            done[k - 3] = order.step(lambda values: parts[k - 3].final(values, wide_type, cuts[k - 3]), state[k - 3]["cores"])
        if k == 0:
            beside[1]()
        if last:
            state[k - 1]["sum"], *more = step(k - 1, parts[k - 1].add_last, "half", "half moved")
            extras += more
            state[k - 1]["sum moved"] = partner(state[k - 1]["sum"], "dp", LAYER)
        if before:
            own, moved = order.hold(state[k - 2]["four"]), order.hold(state[k - 2]["four moved"])
            order.last = moved
            state[k - 2]["cores"] = [own, moved] + [partner(value, "dp", CORE) for value in (own, moved)]
        if now:
            state[k]["z"], moved = step(k, parts[k].add_y, "y", "y moved")
            state[k]["z moved"] = partner(moved, "dp", LAYER)
        if k + 2 < count:
            away(k + 2)
            keep(k + 2)
        if last:
            state[k - 1]["four"] = step(k - 1, parts[k - 1].join_z, "sum", "sum moved")
            state[k - 1]["four moved"] = partner(state[k - 1]["four"], "dp", ROW)
        if now:
            state[k]["half"] = step(k, parts[k].add_z, "z", "z moved")
            state[k]["half moved"] = partner(state[k]["half"], "dp", 2 * LAYER)
    return done, extras


def reduce_plain(matrices):
    return [
        lax.psum(lax.psum_scatter(matrix, "fsdp", scatter_dimension=dim, tiled=True), "dp").astype(wide_type)
        for matrix, dim in matrices
    ]


class Fetch:
    def __init__(self, operands, blocks):
        self.operands, self.blocks, self.count = operands, blocks, len(operands)

    def scratch(self):
        return pltpu.SemaphoreType.DMA((len(self.blocks),))

    def start(self, at_ref, sources, targets, sems):
        at = tuple(at_ref[i] for i in range(4))
        copies = {}
        for number, (target, operand, index, spot, (rows, columns)) in enumerate(self.blocks):
            source = sources[operand] if index is None else sources[operand].at[index]
            lead, row, column = spot(at)
            row = row if isinstance(row, int) else pl.multiple_of(row, 16)
            column = column if isinstance(column, int) else pl.multiple_of(column, 128)
            place = lead + (pl.ds(row, rows), pl.ds(column, columns))
            copy = pltpu.make_async_copy(source, targets[target].at[place], sems.at[number])
            copy.start()
            copies.setdefault(target, []).append(copy)
        return copies


def attention_shard_kernel(at_ref, query, key_t, out, value_t, low_ref, half_ref):
    start = 0
    for block in (query[...], key_t[...].T, out[...], value_t[...].T):
        low_ref[:, start : start + block.shape[1]] = block.astype(narrow_dtype)
        start += block.shape[1]
    rows = half_ref.shape[0]
    half_ref[...] = low_ref[pl.ds(pl.multiple_of(at_ref[1] * rows, 16), rows), :]


def down_shard_kernel(at_ref, down_t, low_ref, half_ref):
    low_ref[...] = down_t[...].astype(narrow_dtype)
    columns = half_ref.shape[1]
    half_ref[...] = low_ref[:, pl.ds(pl.multiple_of(at_ref[1] * columns, 128), columns)]


def narrow_kernel(wide_ref, narrow_ref):
    narrow_ref[...] = wide_ref[...].astype(narrow_dtype)


def narrowed(values):
    rows, columns = values[0].shape
    width = 512
    spec = pl.BlockSpec((rows, width), lambda i: (0, i))
    return pl.pallas_call(
        narrow_kernel,
        grid=(columns // width,),
        out_shape=jax.ShapeDtypeStruct((rows, columns), narrow_dtype),
        in_specs=[spec],
        out_specs=spec,
        compiler_params=pltpu.CompilerParams(vmem_limit_bytes=16 * 2**20),
        cost_estimate=pl.CostEstimate(flops=1000, bytes_accessed=1000, transcendentals=0),
    )(values[0])


def gather_weights(place, order, small, attn, pair, down_t, beside):
    mine, core, row, layer = place.scalars
    layers = place.layers
    model_rows, ff = pair[0].shape
    model, down_columns = down_t.shape
    low = lambda value: value.astype(narrow_dtype)
    attn_width = sum(value.shape[1] for value in attn)
    if not place.blocks:
        attn_full, gate, up, down_full = (
            lax.all_gather(low(value), "fsdp", axis=axis, tiled=True)
            for value, axis in ((jnp.concatenate(attn, axis=1), 0), (pair[0], 0), (pair[1], 0), (down_t, 1))
        )
        zero = lambda at: ((), 0, 0)
        first = Fetch([attn_full], [("attn", 0, None, zero, attn_full.shape)])
        every = Fetch(
            [attn_full, gate, up, down_full],
            [
                ("pair", 1, None, lambda at: ((0,), 0, 0), gate.shape),
                ("pair", 2, None, lambda at: ((1,), 0, 0), up.shape),
                ("down", 3, None, zero, down_full.shape),
                ("attn", 0, None, zero, attn_full.shape),
            ],
        )
        beside(first, lax.all_gather(small, "fsdp", axis=1, tiled=True))
        return first, every, Fetch(every.operands, every.blocks[:3])
    columns = ff // layers
    half = model_rows // 2
    half_columns = down_columns // 2
    own_piece = jnp.where(
        row == 0,
        lax.dynamic_slice(pair[0], (core * half, layer * columns), (half, columns)),
        lax.dynamic_slice(pair[1], (core * half, layer * columns), (half, columns)),
    )
    small_block = jnp.pad(small, ((0, 0), (0, columns - small.shape[1])))
    own_piece = jnp.concatenate([low(own_piece), small_block], axis=0)
    piece = partner(own_piece, "fsdp", 1)
    order.last = own_piece
    attn_low, attn_half = order.step(
        lambda values: call(
            attention_shard_kernel,
            [place.vector] + values,
            [((model_rows, attn_width), narrow_dtype), ((half, attn_width), narrow_dtype)],
            24,
        ),
        [attn[0], attn[1].T, attn[2], attn[3].T],
    )
    piece = order.hold(piece)
    order.last = piece
    pieces = [[piece] + [partner(piece, "dp", offset * LAYER) for offset in range(1, layers)]]
    pieces.append([partner(piece, "dp", ROW)])
    attn_near = partner(after(attn_half, piece), "fsdp", 1)
    down_low, down_half = order.step(
        lambda values: call(
            down_shard_kernel,
            [place.vector] + values,
            [(down_t.shape, narrow_dtype), ((model, half_columns), narrow_dtype)],
            24,
        ),
        [down_t],
    )
    gate_low = order.step(narrowed, [pair[0]])
    up_low = order.step(narrowed, [pair[1]])
    def over_y(index):
        moved = order.last = order.hold(pieces[0][index])
        pieces[0][index] = moved
        pieces[1].append(partner(moved, "dp", ROW))

    def arrived(index):
        pieces[1][index] = order.last = order.hold(pieces[1][index])

    over_y(1)
    over_y(2)
    arrived(0)
    over_y(3)
    attn_near = order.last = order.hold(attn_near)
    down_near = partner(after(down_half, attn_near), "fsdp", 1)
    attn_other = partner(attn_near, "dp", CORE)

    def halves(target, first):
        size = (half, attn_width)
        return [
            (target, first, None, lambda at: ((), at[0] * model_rows, 0), (model_rows, size[1])),
            (target, first + 1, None, lambda at: ((), (1 - at[0]) * model_rows + at[1] * half, 0), size),
            (target, first + 2, None, lambda at: ((), (1 - at[0]) * model_rows + (1 - at[1]) * half, 0), size),
        ]

    first = Fetch([attn_low, attn_near, attn_other], halves("attn", 0))
    order.last = attn_other
    small_other = piece[half:, : small.shape[1]]
    small_rows = jnp.where(
        mine == 0, jnp.concatenate([small, small_other], axis=1), jnp.concatenate([small_other, small], axis=1)
    )
    beside(first, small_rows)
    arrived(1)
    arrived(2)
    arrived(3)
    pieces += [[partner(moved, "dp", CORE) for moved in group] for group in pieces]
    down_near = order.hold(down_near)
    down_other = partner(down_near, "dp", CORE)
    blocks = [
        ("pair", 6, None, lambda at: ((0,), at[0] * model_rows, 0), (model_rows, ff)),
        ("pair", 7, None, lambda at: ((1,), at[0] * model_rows, 0), (model_rows, ff)),
    ]
    for number in range(4):
        for offset in range(layers):

            def spot(at, number=number, offset=offset):
                lead = (at[2] ^ (number % 2),)
                return (lead, (1 - at[0]) * model_rows + (at[1] ^ (number // 2)) * half, (at[3] ^ offset) * columns)

            blocks.append(("pair", 8 + number * layers + offset, (pl.ds(0, half),), spot, (half, columns)))
    near = (model, half_columns)
    blocks += [
        ("down", 3, None, lambda at: ((), 0, at[0] * down_columns), (model, down_columns)),
        ("down", 4, None, lambda at: ((), 0, (1 - at[0]) * down_columns + at[1] * half_columns), near),
        ("down", 5, None, lambda at: ((), 0, (1 - at[0]) * down_columns + (1 - at[1]) * half_columns), near),
    ]
    blocks += halves("attn", 0)
    operands = [attn_low, attn_near, attn_other, down_low, down_near, down_other, gate_low, up_low] + sum(pieces, [])
    ffn_blocks = [(block[0], block[1] - 3) + block[2:] for block in blocks if block[0] != "attn"]
    return first, Fetch(operands, blocks), Fetch(operands[3:], ffn_blocks)


def local(
    hidden_in,
    cotangent,
    norm_attn,
    norm_ffn,
    router,
    w_query,
    key_weight,
    value_weight,
    w_out,
    w_gate,
    w_up,
    w_down,
    lengths,
    chosen_second,
    chosen_third,
):
    place = Place(*w_gate.shape)
    owners, layers = place.owners, place.layers
    mine = place.scalars[0]
    width = w_query.shape[1]
    kv_width = key_weight.shape[1]
    small = jnp.concatenate(
        [norm_attn[None, :], norm_ffn[None, :], router.T, jnp.zeros((11, norm_attn.shape[0]), wide_type)]
    ).astype(narrow_dtype)
    count_one, model = hidden_in.shape
    ff = w_gate.shape[1]
    attn_width = 2 * width + 2 * kv_width
    chosen_two, chosen_three = chosen_second[0], chosen_third[0]
    count_two, count_three = chosen_two.shape[0], chosen_three.shape[0]
    count_rest = count_two + count_three
    count_all = count_one + count_rest
    cos_one, sin_one = rotary_tables(jnp.arange(count_one))
    cos_two, sin_two = rotary_tables(chosen_two)
    cos_three, sin_three = rotary_tables(chosen_three)
    v_width = attn_width - V_START
    first_outputs, small_wide = [], None

    def first_attention(fetch, small_rows):
        nonlocal small_wide
        small_wide = small_rows[:8].astype(wide_type)
        first_outputs.extend(
            call(
                partial(first_attention_kernel, fetch),
                [lengths, place.vector, after(order.hold(hidden_in.T), cos_two, sin_two, cos_three, sin_three), cotangent.T, small_wide, cos_one, sin_one]
                + fetch.operands,
                [
                    ((count_one, model), narrow_dtype),
                    ((count_one, model), narrow_dtype),
                    ((count_one, model), narrow_dtype),
                    ((count_one, QK_WIDTH), narrow_dtype),
                    ((count_one, v_width), narrow_dtype),
                    ((count_one, model), narrow_dtype),
                    ((GROUP * count_one, 128), wide_type),
                    ((count_one, model), wide_type),
                    ((count_one, 128), wide_type),
                ],
                32,
                attn_scratch + [fetch.scratch()],
                hbm=fetch.count,
                scalars=2,
            )
        )
        order.last = first_outputs[0]

    order = Order()
    attn_scratch = [pltpu.VMEM((model, attn_width), narrow_dtype)]
    fetch_attn, fetch_all, fetch_ffn = gather_weights(
        place, order, small, (w_query, key_weight, w_out, value_weight), (w_gate, w_up), w_down.T, first_attention
    )
    hidden_rows, cotangent_rows, normed_one, qk_one, v_one, att_one, log_one, attn_out_one, gating_one = first_outputs
    rest = lambda width: ((count_rest, width), narrow_dtype)
    every = lambda width: ((count_all, width), narrow_dtype)
    turned = ((model, count_all), narrow_dtype)
    scratch_for = lambda count: [
        pltpu.VMEM((count, QK_WIDTH), narrow_dtype),
        pltpu.VMEM((count, v_width), narrow_dtype),
        pltpu.VMEM((GROUP * count, 128), wide_type),
    ]
    back_scratch = lambda count: [
        pltpu.VMEM((count, model), narrow_dtype),
        pltpu.VMEM((count, QK_WIDTH), wide_type),
    ]
    wide = lambda count, width: pltpu.VMEM((count, width), wide_type)
    attn_tiles = -(-model // 128) * 128
    (
        hidden_out, d_input, d_gating_one, small_middle, hidden, d_ffn_t, d_gate_rest, d_up_rest, d_attn_rest,
        att_rest, normed_rest, d_qk_rest, d_v_rest, ffn_one, ffn_rest, d_ffn_one,
    ) = call(
        partial(middle_kernel, fetch_all),
        [
            lengths, place.vector, hidden_rows, cotangent_rows, small_wide, attn_out_one, gating_one,
            cos_two, sin_two, cos_three, sin_three,
            chosen_two[None, :], chosen_three[None, :],
        ]
        + fetch_all.operands,
        [
            ((count_one, model), narrow_dtype), ((count_one, model), wide_type), ((count_one, 128), wide_type),
            ((8, model), wide_type), every(ff), turned, rest(ff), rest(ff), rest(attn_tiles),
            rest(model), rest(model), rest(QK_WIDTH), rest(v_width),
            ((count_one, model), narrow_dtype), rest(model), ((count_one, model), narrow_dtype),
        ],
        46,
        [
            pltpu.VMEM((model, attn_width), narrow_dtype),
            pltpu.VMEM((2, model, ff), narrow_dtype),
            pltpu.VMEM((model, ff), narrow_dtype),
            fetch_all.scratch(),
            wide(count_two, ff), wide(count_two, ff), wide(count_three, ff), wide(count_three, ff),
            wide(count_one, model), wide(count_two, model), wide(count_three, model),
        ]
        + scratch_for(count_two) + scratch_for(count_three) + back_scratch(count_two) + back_scratch(count_three)
        + [pltpu.VMEM((count_rest, model), narrow_dtype)],
        hbm=fetch_all.count,
        scalars=2,
    )

    small_tile = attn_width // layers
    attention, feed = [], []

    def last_ffn():
        feed.extend(
            call(
                partial(last_ffn_kernel, fetch_ffn),
                [
                    lengths, place.vector, hidden_rows, small_wide, attn_out_one, gating_one, d_input,
                    order.hold(d_ffn_one), ffn_one, ffn_rest, d_gate_rest, d_up_rest, d_attn_rest,
                    small_middle,
                ]
                + fetch_ffn.operands,
                [
                    every(ff), every(ff), every(attn_tiles), turned, ((count_one, model), wide_type),
                    ((8, model), wide_type),
                ],
                48,
                [
                    pltpu.VMEM((2, model, ff), narrow_dtype),
                    pltpu.VMEM((model, ff), narrow_dtype),
                    fetch_ffn.scratch(),
                ],
                hbm=fetch_ffn.count,
                scalars=2,
            )
        )
        order.last = feed[0]

    def last_attention():
        d_attn, d_input_last, small_feed = feed[2], feed[4], feed[5]
        attention.extend(
            call(
                partial(last_attention_kernel, fetch_attn),
                [
                    lengths, place.vector, hidden_rows, small_wide, cos_one, sin_one, normed_one, qk_one, v_one, att_one,
                    log_one, gating_one, d_gating_one, order.hold(d_attn), d_input_last, normed_rest, att_rest, d_qk_rest,
                    d_v_rest, small_feed,
                ]
                + fetch_attn.operands,
                [
                    every(QK_WIDTH), every(v_width), turned, turned, ((count_one, model), wide_type),
                    ((8, model), wide_type), ((owners, 8, small_tile), wide_type),
                ],
                40,
                back_scratch(count_one) + attn_scratch + [fetch_attn.scratch()],
                hbm=fetch_attn.count,
                scalars=2,
            )
        )
        order.last = attention[0]

    if not place.blocks:
        last_ffn()
        last_attention()
        d_gate, d_up, d_attn, ffn_t, _, _ = feed
        d_qk, d_v, normed_t, att_t, grad_hidden, small_all, _ = attention
        narrow_dot = lambda left, right: rows_dot(left, right).astype(narrow_dtype)
        skip = V_HEAD * HEAD_SIZE
        down_t, *reduced = reduce_plain(
            [
                (narrow_dot(d_ffn_t, hidden), 1),
                (narrow_dot(ffn_t, d_gate), 0),
                (narrow_dot(ffn_t, d_up), 0),
                (narrow_dot(normed_t, d_qk), 0),
                (narrow_dot(att_t, d_attn[:, :model]), 0),
                (narrow_dot(normed_t, d_v[:, skip:]), 0),
            ]
        )
        small_all = lax.psum_scatter(lax.psum(small_all, "dp"), "fsdp", scatter_dimension=1, tiled=True)
        return (
            hidden_out, grad_hidden, small_all[0], small_all[1], small_all[2:5].T,
            reduced[2][:, :width], reduced[2][:, width:], reduced[4], reduced[3], reduced[0], reduced[1], down_t.T,
        )
    by_core = lambda left: left.reshape(owners * 2, model // owners // 2, left.shape[1])
    size = ff // owners // 2

    def down_product(owner, core, left, right):
        return rows_dot(left[...], right[:, pl.ds(pl.multiple_of((owner * 2 + core) * size, 128), size)])

    def plain_product(owner, core, left, right):
        return rows_dot(left[owner * 2 + core], right[...])

    def small_block(owner, normed, d_qk, att, d_attn, d_v, small_parts):
        return small_parts[owner]

    def attention_product(owner, core, normed, d_qk, att, d_attn, d_v, small_parts):
        left = normed[owner * 2 + core]
        out = rows_dot(att[owner * 2 + core], d_attn[...])
        value = rows_dot(left, d_v[...])
        shared = attn_tiles - 128
        return jnp.concatenate(
            [rows_dot(left, d_qk[...]), out[:, :shared], out[:, shared:] + value[:, :128], value[:, 128:]], axis=1
        )

    rows = model // owners // 4
    parts = [
        Part(place, down_product, model // 2 // layers, size, tall=True),
        Part(place, plain_product, rows, ff // layers),
        Part(place, plain_product, rows, ff // layers),
        Part(place, attention_product, rows, attn_width // layers, extra=small_block),
    ]
    operands = [
        lambda: [d_ffn_t, hidden],
        lambda: [by_core(feed[3]), feed[0]],
        lambda: [by_core(feed[3]), feed[1]],
        lambda: [by_core(attention[2]), attention[0], by_core(attention[3]), feed[2], attention[1], attention[6]],
    ]
    cuts = [
        (0, width, False),
        (width, width + kv_width, True),
        (width + kv_width, 2 * width + kv_width, False),
        (2 * width + kv_width, attn_width, True),
    ]
    reduced, small_sum = reduce_all(parts, operands, order, (last_ffn, last_attention), [None, None, None, cuts])
    down_t, gate_shard, up_shard, (query_shard, key_t, out_shard, value_t) = reduced
    grad_hidden, small_sum = attention[4], small_sum[0][0][:, : model // owners]
    return (
        hidden_out,
        grad_hidden,
        small_sum[0],
        small_sum[1],
        small_sum[2:5].T,
        query_shard,
        key_t.T,
        value_t.T,
        out_shard,
        gate_shard,
        up_shard,
        down_t.T,
    )


def solution(mesh):
    in_specs = (
        P(("dp", "fsdp"), None),
        P(("dp", "fsdp"), None),
        P("fsdp"),
        P("fsdp"),
        P("fsdp", None),
        P("fsdp", None),
        P("fsdp", None),
        P("fsdp", None),
        P("fsdp", None),
        P("fsdp", None),
        P("fsdp", None),
        P("fsdp", None),
        P(("dp", "fsdp")),
        P(("dp", "fsdp"), None),
        P(("dp", "fsdp"), None),
    )
    out_specs = (
        P(("dp", "fsdp"), None),
        P(("dp", "fsdp"), None),
        P("fsdp"),
        P("fsdp"),
        P("fsdp", None),
        P("fsdp", None),
        P("fsdp", None),
        P("fsdp", None),
        P("fsdp", None),
        P("fsdp", None),
        P("fsdp", None),
        P("fsdp", None),
    )
    return jax.shard_map(local, mesh=mesh, in_specs=in_specs, out_specs=out_specs, check_vma=False)
```

```python
from functools import partial

import jax
import jax.numpy as jnp
from jax import lax
from jax.experimental import pallas as pl
from jax.experimental.pallas import tpu as pltpu
from jax.sharding import PartitionSpec as P

QUERY_HEADS = 15
KEY_VALUE_HEADS = 5
HEAD_SIZE = 64
GROUP = QUERY_HEADS // KEY_VALUE_HEADS
MODEL = QUERY_HEADS * HEAD_SIZE
QK_WIDTH = (QUERY_HEADS + KEY_VALUE_HEADS) * HEAD_SIZE
V_START = QK_WIDTH + MODEL - HEAD_SIZE
V_HEAD = 1
SCALE = HEAD_SIZE ** (-0.5)

PIECE = 4

epsilon = 1e-05
negative = -1e30
narrow_dtype = jnp.bfloat16
wide_type = jnp.float32


def rows_dot(left, right):
    return lax.dot_general(left, right, (((1,), (0,)), ((), ())), preferred_element_type=wide_type)


def rows_dot_t(left, right):
    return lax.dot_general(left, right, (((1,), (1,)), ((), ())), preferred_element_type=wide_type)


def columns_dot(left, right):
    return lax.dot_general(left, right, (((0,), (0,)), ((), ())), preferred_element_type=wide_type)


def inverse_rms(rows):
    return lax.rsqrt(jnp.mean(rows * rows, axis=-1, keepdims=True) + epsilon)


def norm_back(rows, inverse, gain, incoming):
    weighted = incoming * gain
    mean = jnp.mean(weighted * rows, axis=-1, keepdims=True)
    d_rows = inverse * weighted - rows * (inverse * inverse * inverse * mean)
    return d_rows, jnp.sum(incoming * rows * inverse, axis=0, keepdims=True)


def rotate(block, cosines, sines):
    lanes = lax.broadcasted_iota(jnp.int32, block.shape, 1)
    swapped = jnp.where(lanes % HEAD_SIZE < HEAD_SIZE // 2, pltpu.roll(block, 96, 1), pltpu.roll(block, 32, 1))
    return block * cosines + swapped * sines


def causal_bias(count, length):
    row = lax.broadcasted_iota(jnp.int32, (count, count), 0)
    column = lax.broadcasted_iota(jnp.int32, (count, count), 1)
    allowed = column <= row
    if length is not None:
        allowed = allowed & (column < length)
    bias = jnp.where(allowed, 0.0, negative)
    return jnp.concatenate([bias] * GROUP, axis=0)


def head_columns(ref, first, count):
    return jnp.concatenate(
        [ref[:, (first + i) * HEAD_SIZE : (first + i + 1) * HEAD_SIZE] for i in range(count)], axis=0
    )


def attention_forward(rows, gain, router_row, cosines, sines, bias, weight, normed_ref, qk_ref, v_ref, att_ref, log_ref):
    count = rows.shape[0]
    normed_ref[...] = (rows * inverse_rms(rows) * gain).astype(narrow_dtype)
    normed = normed_ref[...]
    gating = jax.nn.sigmoid(jnp.sum(normed.astype(wide_type) * router_row, axis=-1, keepdims=True))
    for block in range(QK_WIDTH // 256):
        product = rows_dot(normed, weight[:, block * 256 : (block + 1) * 256])
        for part in range(2):
            piece = rotate(product[:, part * 128 : (part + 1) * 128], cosines, sines)
            at = block * 256 + part * 128
            qk_ref[:, at : at + 128] = piece.astype(narrow_dtype)
    v_ref[...] = rows_dot(normed, weight[:, V_START:]).astype(narrow_dtype)
    for head in range(KEY_VALUE_HEADS):
        queries = head_columns(qk_ref, head * GROUP, GROUP)
        keys = head_columns(qk_ref, QUERY_HEADS + head, 1)
        values = head_columns(v_ref, V_HEAD + head, 1)
        scores = rows_dot_t(queries, keys) * SCALE + bias
        peak = jnp.max(scores, axis=-1, keepdims=True)
        expanded = jnp.exp(scores - peak)
        total = jnp.sum(expanded, axis=-1, keepdims=True)
        log_ref[:, head : head + 1] = peak + jnp.log(total)
        attended = rows_dot((expanded / total).astype(narrow_dtype), values).astype(narrow_dtype)
        for i in range(GROUP):
            at = (head * GROUP + i) * HEAD_SIZE
            att_ref[:, at : at + HEAD_SIZE] = attended[i * count : (i + 1) * count]
    return rows_dot(att_ref[...], weight[:, QK_WIDTH : QK_WIDTH + MODEL]), gating


def attention_backward(
    rows, gain, router_row, cosines, sines, bias, weight, normed_ref, qk_ref, v_ref, log_ref,
    d_attn_low, d_gating, gating, d_att_ref, d_raw_ref, d_qk_ref, d_v_ref,
):
    count = rows.shape[0]
    d_att_ref[...] = rows_dot_t(d_attn_low, weight[:, QK_WIDTH : QK_WIDTH + MODEL]).astype(narrow_dtype)
    d_v_ref[...] = jnp.zeros_like(d_v_ref)
    for head in range(KEY_VALUE_HEADS):
        queries = head_columns(qk_ref, head * GROUP, GROUP)
        keys = head_columns(qk_ref, QUERY_HEADS + head, 1)
        values = head_columns(v_ref, V_HEAD + head, 1)
        d_attended = head_columns(d_att_ref, head * GROUP, GROUP)
        scores = rows_dot_t(queries, keys) * SCALE + bias
        probabilities = jnp.exp(scores - log_ref[:, head : head + 1])
        d_probs = rows_dot_t(d_attended, values)
        row_dot = jnp.sum(probabilities * d_probs, axis=-1, keepdims=True)
        d_raw = (probabilities * (d_probs - row_dot) * SCALE).astype(narrow_dtype)
        d_queries = rows_dot(d_raw, keys)
        for i in range(GROUP):
            at = (head * GROUP + i) * HEAD_SIZE
            d_raw_ref[:, at : at + HEAD_SIZE] = d_queries[i * count : (i + 1) * count]
        at = (QUERY_HEADS + head) * HEAD_SIZE
        d_raw_ref[:, at : at + HEAD_SIZE] = columns_dot(queries, d_raw).T
        at = (V_HEAD + head) * HEAD_SIZE
        d_values = columns_dot(d_attended, probabilities.astype(narrow_dtype)).T
        d_v_ref[:, at : at + HEAD_SIZE] = d_values.astype(narrow_dtype)
    for block in range(QK_WIDTH // 128):
        at = block * 128
        d_qk_ref[:, at : at + 128] = rotate(d_raw_ref[:, at : at + 128], cosines, -sines).astype(narrow_dtype)
    d_normed = rows_dot_t(d_qk_ref[...], weight[:, :QK_WIDTH]) + rows_dot_t(d_v_ref[...], weight[:, V_START:])
    d_logit = d_gating * gating * (1.0 - gating)
    d_normed = d_normed + d_logit * router_row
    router_gradient = jnp.sum(d_logit * normed_ref[...].astype(wide_type), axis=0, keepdims=True)
    d_rows, gain_gradient = norm_back(rows, inverse_rms(rows), gain, d_normed)
    return d_rows, gain_gradient, router_gradient


def ffn_forward(after, gain, w_gate, w_up, w_down, ffn_ref, hidden_ref, gate_ref=None, up_ref=None, ready=()):
    ffn_ref[...] = (after * inverse_rms(after) * gain).astype(narrow_dtype)
    gate = rows_dot(ffn_ref[...], w_gate[...])
    up = rows_dot(ffn_ref[...], w_up[...])
    if gate_ref is not None:
        gate_ref[...] = gate
        up_ref[...] = up
    hidden_ref[...] = (gate * jax.nn.sigmoid(gate) * up).astype(narrow_dtype)
    for copy in ready:
        copy.wait()
    return rows_dot_t(hidden_ref[...], w_down[...])


def ffn_backward(after, gain, w_gate, w_up, w_down, d_ffn_ref, gate, up, d_gate_ref, d_up_ref):
    d_hidden = rows_dot(d_ffn_ref[...], w_down[...])
    sig = jax.nn.sigmoid(gate)
    d_gate_ref[...] = (d_hidden * up * sig * (1.0 + gate * (1.0 - sig))).astype(narrow_dtype)
    d_up_ref[...] = (d_hidden * gate * sig).astype(narrow_dtype)
    total = rows_dot_t(d_gate_ref[...], w_gate[...]) + rows_dot_t(d_up_ref[...], w_up[...])
    return norm_back(after, inverse_rms(after), gain, total)


def pick_exact(selector, rows):
    high = rows.astype(narrow_dtype)
    rest = rows - high.astype(wide_type)
    middle = rest.astype(narrow_dtype)
    low = (rest - middle.astype(wide_type)).astype(narrow_dtype)
    return rows_dot(selector, high) + rows_dot(selector, middle) + rows_dot(selector, low)


def first_attention_kernel(
    fetch, length_ref, at_ref, hidden_t, cotangent_t, small, cosines, sines, *refs
):
    sources, refs = refs[: fetch.count], refs[fetch.count :]
    hidden_in, cotangent, normed_ref, qk_ref, v_ref, att_ref, log_ref, out_ref, gating_ref, weight, sems = refs
    hidden_in[...] = hidden_t[...].T
    cotangent[...] = cotangent_t[...].T
    copies = fetch.start(at_ref, sources, {"attn": weight}, sems)
    rows = hidden_in[...].astype(wide_type)
    for copy in copies["attn"]:
        copy.wait()
    bias = causal_bias(rows.shape[0], length_ref[0])
    attn_out, gating = attention_forward(
        rows, small[0:1], small[2:3], cosines[...], sines[...], bias, weight, normed_ref, qk_ref, v_ref, att_ref, log_ref
    )
    out_ref[...] = attn_out
    gating_ref[...] = jnp.broadcast_to(gating, gating_ref.shape)


def last_attention_kernel(
    fetch, length_ref, at_ref, hidden_in, small, cosines, sines, normed_ref, qk_ref, v_ref, att_ref, log_ref, gating_ref,
    d_gating_ref, d_attn_ref, d_input_ref, normed_rest, att_rest, d_qk_rest, d_v_rest, small_middle, *refs,
):
    sources, refs = refs[: fetch.count], refs[fetch.count :]
    d_qk_ref, d_v_ref, normed_t_ref, att_t_ref, grad_hidden_ref, small_out, small_parts, d_att_ref, d_raw_ref, weight, sems = refs
    copies = fetch.start(at_ref, sources, {"attn": weight}, sems)
    for copy in copies["attn"]:
        copy.wait()
    count = hidden_in.shape[0]
    one = pl.ds(0, count)
    rest = pl.ds(count, d_qk_ref.shape[0] - count)
    rows = hidden_in[...].astype(wide_type)
    bias = causal_bias(count, length_ref[0])
    d_rows, gain_gradient, router_gradient = attention_backward(
        rows, small[0:1], small[2:3], cosines[...], sines[...], bias, weight, normed_ref, qk_ref, v_ref, log_ref,
        d_attn_ref[one, :MODEL], d_gating_ref[:, 0:1], gating_ref[:, 0:1], d_att_ref, d_raw_ref, d_qk_ref.at[one], d_v_ref.at[one],
    )
    grad_hidden_ref[...] = d_input_ref[...] + d_rows
    small_out[...] = small_middle[...]
    small_out[0:1] += gain_gradient
    small_out[2:3] = router_gradient
    small_parts[...] = jnp.zeros_like(small_parts)
    size = MODEL // small_parts.shape[0]
    for owner in range(small_parts.shape[0]):
        small_parts[owner, :, 0:size] = small_out[:, owner * size : (owner + 1) * size]
    d_qk_ref[rest] = d_qk_rest[...]
    d_v_ref[rest] = d_v_rest[...]
    normed_t_ref[...] = jnp.concatenate([normed_ref[...], normed_rest[...]], axis=0).T
    att_t_ref[...] = jnp.concatenate([att_ref[...], att_rest[...]], axis=0).T


def middle_kernel(
    fetch, length_ref, at_ref, hidden_in, cotangent, small, attn_out_ref, gating_ref, cos_two, sin_two, cos_three, sin_three,
    row_two, row_three, *refs,
):
    sources, refs = refs[: fetch.count], refs[fetch.count :]
    (
        hidden_out, d_input_ref, d_gating_ref, small_out, hidden_all, d_ffn_t_ref, d_gate_rest, d_up_rest, d_attn_rest,
        att_rest, normed_rest, d_qk_rest, d_v_rest, ffn_one, ffn_rest, d_ffn_one,
        w_attn, w_pair, w_down, sems,
        gate_two, up_two, gate_three, up_three, change_one, change_two, change_three,
        qk_two, v_two, log_two, qk_three, v_three, log_three, d_att_two, d_raw_two, d_att_three, d_raw_three, d_ffn_rest,
    ) = refs
    copies = fetch.start(at_ref, sources, {"pair": w_pair, "down": w_down, "attn": w_attn}, sems)
    w_gate, w_up = w_pair.at[0], w_pair.at[1]
    count_two, count_three = row_two.shape[1], row_three.shape[1]
    count_one = hidden_in.shape[0]
    in_one, in_two = pl.ds(0, count_one), pl.ds(count_one, count_two)
    in_three = pl.ds(count_one + count_two, count_three)
    two = pl.ds(0, count_two)
    three = pl.ds(count_two, count_three)
    gain_attn, gain_ffn = small[0:1], small[1:2]

    def spread(row_ref):
        hit = lax.broadcasted_iota(jnp.int32, (count_one, row_ref.shape[1]), 0) == row_ref[...]
        return jnp.where(hit, 1.0, 0.0)

    put_two = spread(row_two)
    pick_two = put_two.T.astype(narrow_dtype)
    put_two = put_two.astype(narrow_dtype)
    put_three = rows_dot(pick_two, spread(row_three).astype(narrow_dtype))
    pick_three = put_three.T.astype(narrow_dtype)
    put_three = put_three.astype(narrow_dtype)

    after_one = hidden_in[...].astype(wide_type) + attn_out_ref[...]
    for copy in copies["pair"]:
        copy.wait()
    ffn_out = ffn_forward(
        after_one, gain_ffn, w_gate, w_up, w_down, ffn_one, hidden_all.at[in_one], ready=copies["down"]
    )
    valid = lax.broadcasted_iota(jnp.int32, (count_one, 1), 0) < length_ref[0]
    scale_one = jnp.where(valid, gating_ref[:, 0:1], 0.0)
    change_one[...] = attn_out_ref[...] + ffn_out
    d_input_ref[...] = hidden_in[...].astype(wide_type) + scale_one * change_one[...]

    for copy in copies["attn"]:
        copy.wait()
    d_attn_rest[...] = jnp.zeros_like(d_attn_rest)
    state_two = pick_exact(pick_two, d_input_ref[...])
    bias_two = causal_bias(count_two, None)
    attn_two, gating_two = attention_forward(
        state_two, gain_attn, small[3:4], cos_two[...], sin_two[...], bias_two, w_attn,
        normed_rest.at[two], qk_two, v_two, att_rest.at[two], log_two,
    )
    after_two = state_two + attn_two
    change_two[...] = attn_two + ffn_forward(
        after_two, gain_ffn, w_gate, w_up, w_down, ffn_rest.at[two], hidden_all.at[in_two], gate_two, up_two
    )
    delta_two = gating_two * change_two[...]

    state_three = pick_exact(pick_three, state_two + delta_two)
    bias_three = causal_bias(count_three, None)
    attn_three, gating_three = attention_forward(
        state_three, gain_attn, small[4:5], cos_three[...], sin_three[...], bias_three, w_attn,
        normed_rest.at[three], qk_three, v_three, att_rest.at[three], log_three,
    )
    after_three = state_three + attn_three
    change_three[...] = attn_three + ffn_forward(
        after_three, gain_ffn, w_gate, w_up, w_down, ffn_rest.at[three], hidden_all.at[in_three], gate_three, up_three
    )
    added = delta_two + pick_exact(put_three, gating_three * change_three[...])
    hidden_out[...] = (d_input_ref[...] + pick_exact(put_two, added)).astype(narrow_dtype)

    incoming_two = rows_dot(pick_two, cotangent[...])
    incoming_three = rows_dot(pick_three, incoming_two.astype(narrow_dtype))
    d_change = gating_three * incoming_three
    d_gating = jnp.sum(change_three[...] * incoming_three, axis=-1, keepdims=True)
    d_ffn_rest[three] = d_change.astype(narrow_dtype)
    d_after, gain_ffn_three = ffn_backward(
        after_three, gain_ffn, w_gate, w_up, w_down, d_ffn_rest.at[three], gate_three[...], up_three[...],
        d_gate_rest.at[three], d_up_rest.at[three],
    )
    d_attn_rest[three, :MODEL] = (d_change + d_after).astype(narrow_dtype)
    d_rows, gain_attn_three, router_three = attention_backward(
        state_three, gain_attn, small[4:5], cos_three[...], sin_three[...], bias_three, w_attn, normed_rest.at[three],
        qk_three, v_three, log_three, d_attn_rest[three, :MODEL], d_gating, gating_three, d_att_three, d_raw_three,
        d_qk_rest.at[three], d_v_rest.at[three],
    )
    back_three = pick_exact(put_three, d_rows + d_after)

    incoming_two = incoming_two + back_three
    d_change = gating_two * incoming_two
    d_gating = jnp.sum(change_two[...] * incoming_two, axis=-1, keepdims=True)
    d_ffn_rest[two] = d_change.astype(narrow_dtype)
    d_after, gain_ffn_two = ffn_backward(
        after_two, gain_ffn, w_gate, w_up, w_down, d_ffn_rest.at[two], gate_two[...], up_two[...],
        d_gate_rest.at[two], d_up_rest.at[two],
    )
    d_attn_rest[two, :MODEL] = (d_change + d_after).astype(narrow_dtype)
    d_rows, gain_attn_two, router_two = attention_backward(
        state_two, gain_attn, small[3:4], cos_two[...], sin_two[...], bias_two, w_attn, normed_rest.at[two],
        qk_two, v_two, log_two, d_attn_rest[two, :MODEL], d_gating, gating_two, d_att_two, d_raw_two,
        d_qk_rest.at[two], d_v_rest.at[two],
    )
    back_two = back_three + d_rows + d_after

    incoming = cotangent[...].astype(wide_type) + pick_exact(put_two, back_two)
    d_input_ref[...] = incoming
    d_gating = jnp.where(valid, jnp.sum(change_one[...] * incoming, axis=-1, keepdims=True), 0.0)
    d_gating_ref[...] = jnp.broadcast_to(d_gating, d_gating_ref.shape)
    d_ffn_one[...] = (scale_one * incoming).astype(narrow_dtype)
    small_out[...] = jnp.zeros_like(small_out)
    small_out[0:1] = gain_attn_two + gain_attn_three
    small_out[1:2] = gain_ffn_two + gain_ffn_three
    small_out[3:4] = router_two
    small_out[4:5] = router_three
    d_ffn_t_ref[...] = jnp.concatenate([d_ffn_one[...], d_ffn_rest[...]], axis=0).T


def last_ffn_kernel(
    fetch, length_ref, at_ref, hidden_in, small, attn_out_ref, gating_ref, d_input_in, d_ffn_one,
    ffn_one, ffn_rest, d_gate_rest, d_up_rest, d_attn_rest, small_middle, *refs,
):
    sources, refs = refs[: fetch.count], refs[fetch.count :]
    d_gate_all, d_up_all, d_attn_all, ffn_t_ref, d_input_ref, small_out, w_pair, w_down, sems = refs
    copies = fetch.start(at_ref, sources, {"pair": w_pair, "down": w_down}, sems)
    count = hidden_in.shape[0]
    one, rest = pl.ds(0, count), pl.ds(count, d_gate_all.shape[0] - count)
    d_gate_all[rest] = d_gate_rest[...]
    d_up_all[rest] = d_up_rest[...]
    d_attn_all[rest] = d_attn_rest[...]
    d_attn_all[one] = jnp.zeros((count, d_attn_all.shape[1]), narrow_dtype)
    ffn_t_ref[...] = jnp.concatenate([ffn_one[...], ffn_rest[...]], axis=0).T
    valid = lax.broadcasted_iota(jnp.int32, (count, 1), 0) < length_ref[0]
    scale = jnp.where(valid, gating_ref[:, 0:1], 0.0)
    after_one = hidden_in[...].astype(wide_type) + attn_out_ref[...]
    for copy in copies["pair"]:
        copy.wait()
    gate = rows_dot(ffn_one[...], w_pair[0])
    up = rows_dot(ffn_one[...], w_pair[1])
    for copy in copies["down"]:
        copy.wait()
    d_after, gain_gradient = ffn_backward(
        after_one, small[1:2], w_pair.at[0], w_pair.at[1], w_down, d_ffn_one, gate, up,
        d_gate_all.at[one], d_up_all.at[one],
    )
    d_attn_all[one, :MODEL] = (scale * d_input_in[...] + d_after).astype(narrow_dtype)
    d_input_ref[...] = d_input_in[...] + d_after
    small_out[...] = small_middle[...]
    small_out[1:2] += gain_gradient


def rotary_tables(positions):
    half = HEAD_SIZE // 2
    lanes = jnp.arange(2 * HEAD_SIZE)
    frequency = 10000.0 ** (-(lanes % half).astype(wide_type) / half)
    angles = positions.astype(wide_type)[:, None] * frequency[None, :]
    sign = jnp.where(lanes % HEAD_SIZE < half, -1.0, 1.0)
    return jnp.cos(angles), jnp.sin(angles) * sign[None, :]


def call(kernel, operands, outputs, limit, scratch=(), hbm=0, scalars=1):
    specs = [
        pl.BlockSpec(memory_space=pltpu.SMEM if i < scalars else (pl.ANY if i >= len(operands) - hbm else pltpu.VMEM))
        for i in range(len(operands))
    ]
    return pl.pallas_call(
        kernel,
        out_shape=[jax.ShapeDtypeStruct(shape, kind) for shape, kind in outputs],
        in_specs=specs,
        out_specs=[pl.BlockSpec(memory_space=pltpu.VMEM)] * len(outputs),
        scratch_shapes=list(scratch),
        compiler_params=pltpu.CompilerParams(vmem_limit_bytes=limit * 2**20),
        cost_estimate=pl.CostEstimate(flops=1000, bytes_accessed=1000, transcendentals=0),
    )(*operands)


def partner(value, axis, bit):
    count = lax.axis_size(axis)
    return lax.ppermute(value, axis, [(i, i ^ bit) for i in range(count)])


def after(value, *others):
    return lax.optimization_barrier((value,) + others)[0]


def bits_of(axis, low):
    found = []
    bit = low
    while bit < lax.axis_size(axis):
        found.append(bit)
        bit = bit * 2
    return found


CORE, ROW, LAYER = 1, 2, 4


class Place:
    def __init__(self, model_rows, ff):
        group = lax.axis_index("dp")
        self.owners = lax.axis_size("fsdp")
        self.layers = lax.axis_size("dp") // LAYER
        self.blocks = self.owners == 2 and self.layers == 4 and model_rows % 32 == 0 and ff % (128 * self.layers) == 0
        self.scalars = (lax.axis_index("fsdp"), group % 2, group // ROW % 2, group // LAYER)
        self.vector = jnp.stack(self.scalars).astype(jnp.int32)


def local_step(place, fn, operands, outputs, limit):
    shapes = [((count, rows, columns), kind) for count, rows, columns, kind in outputs]

    def kernel(at_ref, *refs):
        made = fn(tuple(at_ref[i] for i in range(4)), *refs[: len(operands)])
        for blocks, ref in zip(made, refs[len(operands) :]):
            for i, block in enumerate(blocks):
                ref[i] = block.astype(ref.dtype)

    return call(kernel, (place.vector,) + tuple(operands), shapes, limit)


def wide_sum(*blocks):
    total = blocks[0].astype(wide_type)
    for block in blocks[1:]:
        total = total + block.astype(wide_type)
    return total


class Part:
    def __init__(self, place, product, rows, columns, tall=False, extra=None):
        self.place, self.product, self.rows, self.columns, self.tall = place, product, rows, columns, tall
        self.extra, self.tail = extra, 0 if extra is None else 8
        self.count = 2 * place.layers

    def out(self, count):
        return (count, self.rows + self.tail, self.columns, narrow_dtype)

    def step(self, fn, operands, counts, limit=12):
        return local_step(self.place, fn, operands, [self.out(count) for count in counts], limit)

    def blocks(self, value):
        r, c = self.rows, self.columns
        if self.tall:
            return [value[i * r : (i + 1) * r] for i in range(self.count)]
        return [value[y * r : (y + 1) * r, z * c : (z + 1) * c] for y in range(2) for z in range(self.place.layers)]

    def made(self, owner, core, refs):
        found = self.blocks(self.product(owner, core, *refs))
        if self.tail:
            below = self.extra(owner, *refs)
            found = [jnp.concatenate([block, below], axis=0) for block in found]
        return found

    def away(self, operands, sides):
        def fn(at, *refs):
            blocks = sum((self.made(at[0] ^ offset, 1 - at[1], refs) for offset in sides), [])
            return [blocks[i : i + PIECE] for i in range(0, len(blocks), PIECE)]

        return self.step(fn, operands, [PIECE] * (len(sides) * self.count // PIECE), 24)

    def keep(self, received, operands, sides):
        def fn(at, *refs):
            received, refs = refs[: -len(operands)], refs[-len(operands) :]
            return [
                [
                    wide_sum(block, received[(number * self.count + i) // PIECE][i % PIECE])
                    for i, block in enumerate(self.made(at[0] ^ offset, at[1], refs))
                ]
                for number, offset in enumerate(sides)
            ]

        return self.step(fn, tuple(received) + tuple(operands), [self.count] * len(sides), 24)

    def add_x(self, values):
        def fn(at, keep, received):
            layers = self.place.layers
            return [
                [wide_sum(keep[row * layers + z], received[row * layers + z]) for z in range(layers)]
                for row in (at[2], 1 - at[2])
            ]

        return self.step(fn, values, [self.place.layers] * 2)

    def add_y(self, values):
        def fn(at, keep, received):
            odd = at[3] % 2
            return [[wide_sum(keep[2 * j + side], received[2 * j + side]) for j in range(2)] for side in (odd, 1 - odd)]

        return self.step(fn, values, [2, 2])

    def add_z(self, values):
        return self.step(lambda at, keep, received: [[wide_sum(keep[j], received[j]) for j in range(2)]], values, [2])[0]

    def add_last(self, values):
        def fn(at, keep, received):
            totals = [wide_sum(keep[j], received[j]) for j in range(2)]
            return [[total[: self.rows] for total in totals], [totals[0][self.rows :]]][: 1 + (self.tail > 0)]

        outputs = [(2, self.rows, self.columns, narrow_dtype), (1, self.tail, self.columns, wide_type)]
        return local_step(self.place, fn, values, outputs[: 1 + (self.tail > 0)], 12)

    def join_z(self, values):
        def fn(at, own, received):
            odd = at[3] % 2
            return [[jnp.where(odd == i % 2, own[i // 2], received[i // 2]) for i in range(4)]]

        return local_step(self.place, fn, values, [(4, self.rows, self.columns, narrow_dtype)], 12)[0]

    def final(self, values, kind, cuts=None):
        place = self.place
        shape = (self.rows * 4, self.columns * place.layers)
        if self.tall:
            shape = (self.rows * self.count, self.columns * 2)

        def kernel(at_ref, *refs):
            out = refs[-1]
            outs = refs[len(values) : -1]
            for source in range(4):
                core, y = at_ref[1] ^ (source // 2), at_ref[2] ^ (source % 2)
                for z in range(place.layers):
                    if self.tall:
                        row, column = (y * place.layers + z) * self.rows, pl.multiple_of(core * self.columns, 128)
                    else:
                        row, column = (core * 2 + y) * self.rows, z * self.columns
                    spot = (pl.ds(pl.multiple_of(row, 8), self.rows), pl.ds(column, self.columns))
                    out[spot] = refs[source][z].astype(kind)
            for (start, stop, turned), ref in zip(cuts or (), outs):
                piece = out[:, start:stop]
                ref[...] = piece.T if turned else piece

        if cuts is None:
            return call(kernel, (place.vector,) + tuple(values), [(shape, kind)], 20)[0]
        shapes = [
            ((stop - start, shape[0]) if turned else (shape[0], stop - start), kind) for start, stop, turned in cuts
        ]
        return call(kernel, (place.vector,) + tuple(values), shapes, 28, [pltpu.VMEM(shape, kind)])


class Order:
    def __init__(self):
        self.last = None

    def hold(self, value):
        return value if self.last is None else after(value, self.last)

    def step(self, work, values):
        result = work([self.hold(values[0])] + list(values[1:]))
        self.last = result[0] if isinstance(result, (list, tuple)) else result
        return result


def reduce_all(parts, operands, order, beside, cuts):
    count = len(parts)
    state = [{} for _ in parts]
    done, extras = [None] * count, []

    def step(k, work, *names):
        return order.step(work, [state[k][name] for name in names])

    def away(k, sides=(0, 1)):
        made = order.step(lambda values: parts[k].away(values, sides), operands[k]())
        state[k]["core"] = [partner(piece, "dp", CORE) for piece in made]

    def keep(k, sides=(0, 1)):
        taken = operands[k]()
        taken[0] = order.hold(taken[0])
        made = parts[k].keep(state[k]["core"], taken, sides)
        order.last = made[0]
        for side, value in zip(sides, made):
            state[k][("keep", "go")[side]] = value

    def start_x(k):
        state[k]["moved"] = partner(order.hold(state[k]["go"]), "fsdp", 1)

    away(0, (1,))
    going = state[0]["core"]
    away(0, (0,))
    staying, state[0]["core"] = state[0]["core"], going
    keep(0, (1,))
    start_x(0)
    state[0]["core"] = staying
    keep(0, (0,))
    beside[0]()
    away(1)
    keep(1)
    for k in range(count + 3):
        now, last, before = k < count, 1 <= k <= count, 2 <= k <= count + 1
        if now:
            state[k]["y"], moved = step(k, parts[k].add_x, "keep", "moved")
            state[k]["y moved"] = partner(moved, "dp", ROW)
        if k + 1 < count:
            start_x(k + 1)
        if 3 <= k:
            done[k - 3] = order.step(lambda values: parts[k - 3].final(values, wide_type, cuts[k - 3]), state[k - 3]["cores"])
        if k == 0:
            beside[1]()
        if now:
            state[k]["z"], moved = step(k, parts[k].add_y, "y", "y moved")
            state[k]["z moved"] = partner(moved, "dp", LAYER)
        if last:
            state[k - 1]["sum"], *more = step(k - 1, parts[k - 1].add_last, "half", "half moved")
            extras += more
            state[k - 1]["sum moved"] = partner(state[k - 1]["sum"], "dp", LAYER)
        if before:
            own, moved = order.hold(state[k - 2]["four"]), order.hold(state[k - 2]["four moved"])
            order.last = moved
            state[k - 2]["cores"] = [own, moved] + [partner(value, "dp", CORE) for value in (own, moved)]
        if k + 2 < count:
            away(k + 2)
            keep(k + 2)
        if now:
            state[k]["half"] = step(k, parts[k].add_z, "z", "z moved")
            state[k]["half moved"] = partner(state[k]["half"], "dp", 2 * LAYER)
        if last:
            state[k - 1]["four"] = step(k - 1, parts[k - 1].join_z, "sum", "sum moved")
            state[k - 1]["four moved"] = partner(state[k - 1]["four"], "dp", ROW)
    return done, extras


def reduce_plain(matrices):
    return [
        lax.psum(lax.psum_scatter(matrix, "fsdp", scatter_dimension=dim, tiled=True), "dp").astype(wide_type)
        for matrix, dim in matrices
    ]


class Fetch:
    def __init__(self, operands, blocks):
        self.operands, self.blocks, self.count = operands, blocks, len(operands)

    def scratch(self):
        return pltpu.SemaphoreType.DMA((len(self.blocks),))

    def start(self, at_ref, sources, targets, sems):
        at = tuple(at_ref[i] for i in range(4))
        copies = {}
        for number, (target, operand, index, spot, (rows, columns)) in enumerate(self.blocks):
            source = sources[operand] if index is None else sources[operand].at[index]
            lead, row, column = spot(at)
            row = row if isinstance(row, int) else pl.multiple_of(row, 16)
            column = column if isinstance(column, int) else pl.multiple_of(column, 128)
            place = lead + (pl.ds(row, rows), pl.ds(column, columns))
            copy = pltpu.make_async_copy(source, targets[target].at[place], sems.at[number])
            copy.start()
            copies.setdefault(target, []).append(copy)
        return copies


def attention_shard_kernel(at_ref, query, key_t, out, value_t, low_ref, half_ref):
    start = 0
    for block in (query[...], key_t[...].T, out[...], value_t[...].T):
        low_ref[:, start : start + block.shape[1]] = block.astype(narrow_dtype)
        start += block.shape[1]
    rows = half_ref.shape[0]
    half_ref[...] = low_ref[pl.ds(pl.multiple_of(at_ref[1] * rows, 16), rows), :]


def down_shard_kernel(at_ref, down_t, low_ref, half_ref):
    low_ref[...] = down_t[...].astype(narrow_dtype)
    columns = half_ref.shape[1]
    half_ref[...] = low_ref[:, pl.ds(pl.multiple_of(at_ref[1] * columns, 128), columns)]


def narrow_kernel(wide_ref, narrow_ref):
    narrow_ref[...] = wide_ref[...].astype(narrow_dtype)


def narrowed(values):
    rows, columns = values[0].shape
    width = 512
    spec = pl.BlockSpec((rows, width), lambda i: (0, i))
    return pl.pallas_call(
        narrow_kernel,
        grid=(columns // width,),
        out_shape=jax.ShapeDtypeStruct((rows, columns), narrow_dtype),
        in_specs=[spec],
        out_specs=spec,
        compiler_params=pltpu.CompilerParams(vmem_limit_bytes=16 * 2**20),
        cost_estimate=pl.CostEstimate(flops=1000, bytes_accessed=1000, transcendentals=0),
    )(values[0])


def gather_weights(place, order, small, attn, pair, down_t, beside):
    mine, core, row, layer = place.scalars
    layers = place.layers
    model_rows, ff = pair[0].shape
    model, down_columns = down_t.shape
    low = lambda value: value.astype(narrow_dtype)
    attn_width = sum(value.shape[1] for value in attn)
    if not place.blocks:
        attn_full, gate, up, down_full = (
            lax.all_gather(low(value), "fsdp", axis=axis, tiled=True)
            for value, axis in ((jnp.concatenate(attn, axis=1), 0), (pair[0], 0), (pair[1], 0), (down_t, 1))
        )
        zero = lambda at: ((), 0, 0)
        first = Fetch([attn_full], [("attn", 0, None, zero, attn_full.shape)])
        every = Fetch(
            [attn_full, gate, up, down_full],
            [
                ("pair", 1, None, lambda at: ((0,), 0, 0), gate.shape),
                ("pair", 2, None, lambda at: ((1,), 0, 0), up.shape),
                ("down", 3, None, zero, down_full.shape),
                ("attn", 0, None, zero, attn_full.shape),
            ],
        )
        beside(first, lax.all_gather(small, "fsdp", axis=1, tiled=True))
        return first, every, Fetch(every.operands, every.blocks[:3])
    columns = ff // layers
    half = model_rows // 2
    half_columns = down_columns // 2
    own_piece = jnp.where(
        row == 0,
        lax.dynamic_slice(pair[0], (core * half, layer * columns), (half, columns)),
        lax.dynamic_slice(pair[1], (core * half, layer * columns), (half, columns)),
    )
    small_block = jnp.pad(small, ((0, 0), (0, columns - small.shape[1])))
    own_piece = jnp.concatenate([low(own_piece), small_block], axis=0)
    piece = partner(own_piece, "fsdp", 1)
    order.last = own_piece
    attn_low, attn_half = order.step(
        lambda values: call(
            attention_shard_kernel,
            [place.vector] + values,
            [((model_rows, attn_width), narrow_dtype), ((half, attn_width), narrow_dtype)],
            24,
        ),
        [attn[0], attn[1].T, attn[2], attn[3].T],
    )
    piece = order.hold(piece)
    order.last = piece
    pieces = [[piece] + [partner(piece, "dp", offset * LAYER) for offset in range(1, layers)]]
    pieces.append([partner(piece, "dp", ROW)])
    attn_near = partner(after(attn_half, piece), "fsdp", 1)
    down_low, down_half = order.step(
        lambda values: call(
            down_shard_kernel,
            [place.vector] + values,
            [(down_t.shape, narrow_dtype), ((model, half_columns), narrow_dtype)],
            24,
        ),
        [down_t],
    )
    gate_low = order.step(narrowed, [pair[0]])
    up_low = order.step(narrowed, [pair[1]])
    def over_y(index):
        moved = order.last = order.hold(pieces[0][index])
        pieces[0][index] = moved
        pieces[1].append(partner(moved, "dp", ROW))

    def arrived(index):
        pieces[1][index] = order.last = order.hold(pieces[1][index])

    over_y(1)
    over_y(2)
    arrived(0)
    over_y(3)
    attn_near = order.last = order.hold(attn_near)
    down_near = partner(after(down_half, attn_near), "fsdp", 1)
    attn_other = partner(attn_near, "dp", CORE)

    def halves(target, first):
        size = (half, attn_width)
        return [
            (target, first, None, lambda at: ((), at[0] * model_rows, 0), (model_rows, size[1])),
            (target, first + 1, None, lambda at: ((), (1 - at[0]) * model_rows + at[1] * half, 0), size),
            (target, first + 2, None, lambda at: ((), (1 - at[0]) * model_rows + (1 - at[1]) * half, 0), size),
        ]

    first = Fetch([attn_low, attn_near, attn_other], halves("attn", 0))
    order.last = attn_other
    small_other = piece[half:, : small.shape[1]]
    small_rows = jnp.where(
        mine == 0, jnp.concatenate([small, small_other], axis=1), jnp.concatenate([small_other, small], axis=1)
    )
    beside(first, small_rows)
    arrived(1)
    arrived(2)
    arrived(3)
    pieces += [[partner(moved, "dp", CORE) for moved in group] for group in pieces]
    down_near = order.hold(down_near)
    down_other = partner(down_near, "dp", CORE)
    blocks = [
        ("pair", 6, None, lambda at: ((0,), at[0] * model_rows, 0), (model_rows, ff)),
        ("pair", 7, None, lambda at: ((1,), at[0] * model_rows, 0), (model_rows, ff)),
    ]
    for number in range(4):
        for offset in range(layers):

            def spot(at, number=number, offset=offset):
                lead = (at[2] ^ (number % 2),)
                return (lead, (1 - at[0]) * model_rows + (at[1] ^ (number // 2)) * half, (at[3] ^ offset) * columns)

            blocks.append(("pair", 8 + number * layers + offset, (pl.ds(0, half),), spot, (half, columns)))
    near = (model, half_columns)
    blocks += [
        ("down", 3, None, lambda at: ((), 0, at[0] * down_columns), (model, down_columns)),
        ("down", 4, None, lambda at: ((), 0, (1 - at[0]) * down_columns + at[1] * half_columns), near),
        ("down", 5, None, lambda at: ((), 0, (1 - at[0]) * down_columns + (1 - at[1]) * half_columns), near),
    ]
    blocks += halves("attn", 0)
    operands = [attn_low, attn_near, attn_other, down_low, down_near, down_other, gate_low, up_low] + sum(pieces, [])
    ffn_blocks = [(block[0], block[1] - 3) + block[2:] for block in blocks if block[0] != "attn"]
    return first, Fetch(operands, blocks), Fetch(operands[3:], ffn_blocks)


def local(
    hidden_in,
    cotangent,
    norm_attn,
    norm_ffn,
    router,
    w_query,
    key_weight,
    value_weight,
    w_out,
    w_gate,
    w_up,
    w_down,
    lengths,
    chosen_second,
    chosen_third,
):
    place = Place(*w_gate.shape)
    owners, layers = place.owners, place.layers
    mine = place.scalars[0]
    width = w_query.shape[1]
    kv_width = key_weight.shape[1]
    small = jnp.concatenate(
        [norm_attn[None, :], norm_ffn[None, :], router.T, jnp.zeros((11, norm_attn.shape[0]), wide_type)]
    ).astype(narrow_dtype)
    count_one, model = hidden_in.shape
    ff = w_gate.shape[1]
    attn_width = 2 * width + 2 * kv_width
    chosen_two, chosen_three = chosen_second[0], chosen_third[0]
    count_two, count_three = chosen_two.shape[0], chosen_three.shape[0]
    count_rest = count_two + count_three
    count_all = count_one + count_rest
    cos_one, sin_one = rotary_tables(jnp.arange(count_one))
    cos_two, sin_two = rotary_tables(chosen_two)
    cos_three, sin_three = rotary_tables(chosen_three)
    v_width = attn_width - V_START
    first_outputs, small_wide = [], None

    def first_attention(fetch, small_rows):
        nonlocal small_wide
        small_wide = small_rows[:8].astype(wide_type)
        first_outputs.extend(
            call(
                partial(first_attention_kernel, fetch),
                [lengths, place.vector, after(order.hold(hidden_in.T), cos_two, sin_two, cos_three, sin_three), cotangent.T, small_wide, cos_one, sin_one]
                + fetch.operands,
                [
                    ((count_one, model), narrow_dtype),
                    ((count_one, model), narrow_dtype),
                    ((count_one, model), narrow_dtype),
                    ((count_one, QK_WIDTH), narrow_dtype),
                    ((count_one, v_width), narrow_dtype),
                    ((count_one, model), narrow_dtype),
                    ((GROUP * count_one, 128), wide_type),
                    ((count_one, model), wide_type),
                    ((count_one, 128), wide_type),
                ],
                32,
                attn_scratch + [fetch.scratch()],
                hbm=fetch.count,
                scalars=2,
            )
        )
        order.last = first_outputs[0]

    order = Order()
    attn_scratch = [pltpu.VMEM((model, attn_width), narrow_dtype)]
    fetch_attn, fetch_all, fetch_ffn = gather_weights(
        place, order, small, (w_query, key_weight, w_out, value_weight), (w_gate, w_up), w_down.T, first_attention
    )
    hidden_rows, cotangent_rows, normed_one, qk_one, v_one, att_one, log_one, attn_out_one, gating_one = first_outputs
    rest = lambda width: ((count_rest, width), narrow_dtype)
    every = lambda width: ((count_all, width), narrow_dtype)
    turned = ((model, count_all), narrow_dtype)
    scratch_for = lambda count: [
        pltpu.VMEM((count, QK_WIDTH), narrow_dtype),
        pltpu.VMEM((count, v_width), narrow_dtype),
        pltpu.VMEM((GROUP * count, 128), wide_type),
    ]
    back_scratch = lambda count: [
        pltpu.VMEM((count, model), narrow_dtype),
        pltpu.VMEM((count, QK_WIDTH), wide_type),
    ]
    wide = lambda count, width: pltpu.VMEM((count, width), wide_type)
    attn_tiles = -(-model // 128) * 128
    (
        hidden_out, d_input, d_gating_one, small_middle, hidden, d_ffn_t, d_gate_rest, d_up_rest, d_attn_rest,
        att_rest, normed_rest, d_qk_rest, d_v_rest, ffn_one, ffn_rest, d_ffn_one,
    ) = call(
        partial(middle_kernel, fetch_all),
        [
            lengths, place.vector, hidden_rows, cotangent_rows, small_wide, attn_out_one, gating_one,
            cos_two, sin_two, cos_three, sin_three,
            chosen_two[None, :], chosen_three[None, :],
        ]
        + fetch_all.operands,
        [
            ((count_one, model), narrow_dtype), ((count_one, model), wide_type), ((count_one, 128), wide_type),
            ((8, model), wide_type), every(ff), turned, rest(ff), rest(ff), rest(attn_tiles),
            rest(model), rest(model), rest(QK_WIDTH), rest(v_width),
            ((count_one, model), narrow_dtype), rest(model), ((count_one, model), narrow_dtype),
        ],
        46,
        [
            pltpu.VMEM((model, attn_width), narrow_dtype),
            pltpu.VMEM((2, model, ff), narrow_dtype),
            pltpu.VMEM((model, ff), narrow_dtype),
            fetch_all.scratch(),
            wide(count_two, ff), wide(count_two, ff), wide(count_three, ff), wide(count_three, ff),
            wide(count_one, model), wide(count_two, model), wide(count_three, model),
        ]
        + scratch_for(count_two) + scratch_for(count_three) + back_scratch(count_two) + back_scratch(count_three)
        + [pltpu.VMEM((count_rest, model), narrow_dtype)],
        hbm=fetch_all.count,
        scalars=2,
    )

    small_tile = attn_width // layers
    attention, feed = [], []

    def last_ffn():
        feed.extend(
            call(
                partial(last_ffn_kernel, fetch_ffn),
                [
                    lengths, place.vector, hidden_rows, small_wide, attn_out_one, gating_one, d_input,
                    order.hold(d_ffn_one), ffn_one, ffn_rest, d_gate_rest, d_up_rest, d_attn_rest,
                    small_middle,
                ]
                + fetch_ffn.operands,
                [
                    every(ff), every(ff), every(attn_tiles), turned, ((count_one, model), wide_type),
                    ((8, model), wide_type),
                ],
                48,
                [
                    pltpu.VMEM((2, model, ff), narrow_dtype),
                    pltpu.VMEM((model, ff), narrow_dtype),
                    fetch_ffn.scratch(),
                ],
                hbm=fetch_ffn.count,
                scalars=2,
            )
        )
        order.last = feed[0]

    def last_attention():
        d_attn, d_input_last, small_feed = feed[2], feed[4], feed[5]
        attention.extend(
            call(
                partial(last_attention_kernel, fetch_attn),
                [
                    lengths, place.vector, hidden_rows, small_wide, cos_one, sin_one, normed_one, qk_one, v_one, att_one,
                    log_one, gating_one, d_gating_one, order.hold(d_attn), d_input_last, normed_rest, att_rest, d_qk_rest,
                    d_v_rest, small_feed,
                ]
                + fetch_attn.operands,
                [
                    every(QK_WIDTH), every(v_width), turned, turned, ((count_one, model), wide_type),
                    ((8, model), wide_type), ((owners, 8, small_tile), wide_type),
                ],
                40,
                back_scratch(count_one) + attn_scratch + [fetch_attn.scratch()],
                hbm=fetch_attn.count,
                scalars=2,
            )
        )
        order.last = attention[0]

    if not place.blocks:
        last_ffn()
        last_attention()
        d_gate, d_up, d_attn, ffn_t, _, _ = feed
        d_qk, d_v, normed_t, att_t, grad_hidden, small_all, _ = attention
        narrow_dot = lambda left, right: rows_dot(left, right).astype(narrow_dtype)
        skip = V_HEAD * HEAD_SIZE
        down_t, *reduced = reduce_plain(
            [
                (narrow_dot(d_ffn_t, hidden), 1),
                (narrow_dot(ffn_t, d_gate), 0),
                (narrow_dot(ffn_t, d_up), 0),
                (narrow_dot(normed_t, d_qk), 0),
                (narrow_dot(att_t, d_attn[:, :model]), 0),
                (narrow_dot(normed_t, d_v[:, skip:]), 0),
            ]
        )
        small_all = lax.psum_scatter(lax.psum(small_all, "dp"), "fsdp", scatter_dimension=1, tiled=True)
        return (
            hidden_out, grad_hidden, small_all[0], small_all[1], small_all[2:5].T,
            reduced[2][:, :width], reduced[2][:, width:], reduced[4], reduced[3], reduced[0], reduced[1], down_t.T,
        )
    by_core = lambda left: left.reshape(owners * 2, model // owners // 2, left.shape[1])
    size = ff // owners // 2

    def down_product(owner, core, left, right):
        return rows_dot(left[...], right[:, pl.ds(pl.multiple_of((owner * 2 + core) * size, 128), size)])

    def plain_product(owner, core, left, right):
        return rows_dot(left[owner * 2 + core], right[...])

    def small_block(owner, normed, d_qk, att, d_attn, d_v, small_parts):
        return small_parts[owner]

    def attention_product(owner, core, normed, d_qk, att, d_attn, d_v, small_parts):
        left = normed[owner * 2 + core]
        out = rows_dot(att[owner * 2 + core], d_attn[...])
        value = rows_dot(left, d_v[...])
        shared = attn_tiles - 128
        return jnp.concatenate(
            [rows_dot(left, d_qk[...]), out[:, :shared], out[:, shared:] + value[:, :128], value[:, 128:]], axis=1
        )

    rows = model // owners // 4
    parts = [
        Part(place, down_product, model // 2 // layers, size, tall=True),
        Part(place, plain_product, rows, ff // layers),
        Part(place, plain_product, rows, ff // layers),
        Part(place, attention_product, rows, attn_width // layers, extra=small_block),
    ]
    operands = [
        lambda: [d_ffn_t, hidden],
        lambda: [by_core(feed[3]), feed[0]],
        lambda: [by_core(feed[3]), feed[1]],
        lambda: [by_core(attention[2]), attention[0], by_core(attention[3]), feed[2], attention[1], attention[6]],
    ]
    cuts = [
        (0, width, False),
        (width, width + kv_width, True),
        (width + kv_width, 2 * width + kv_width, False),
        (2 * width + kv_width, attn_width, True),
    ]
    reduced, small_sum = reduce_all(parts, operands, order, (last_ffn, last_attention), [None, None, None, cuts])
    down_t, gate_shard, up_shard, (query_shard, key_t, out_shard, value_t) = reduced
    grad_hidden, small_sum = attention[4], small_sum[0][0][:, : model // owners]
    return (
        hidden_out,
        grad_hidden,
        small_sum[0],
        small_sum[1],
        small_sum[2:5].T,
        query_shard,
        key_t.T,
        value_t.T,
        out_shard,
        gate_shard,
        up_shard,
        down_t.T,
    )


def solution(mesh):
    in_specs = (
        P(("dp", "fsdp"), None),
        P(("dp", "fsdp"), None),
        P("fsdp"),
        P("fsdp"),
        P("fsdp", None),
        P("fsdp", None),
        P("fsdp", None),
        P("fsdp", None),
        P("fsdp", None),
        P("fsdp", None),
        P("fsdp", None),
        P("fsdp", None),
        P(("dp", "fsdp")),
        P(("dp", "fsdp"), None),
        P(("dp", "fsdp"), None),
    )
    out_specs = (
        P(("dp", "fsdp"), None),
        P(("dp", "fsdp"), None),
        P("fsdp"),
        P("fsdp"),
        P("fsdp", None),
        P("fsdp", None),
        P("fsdp", None),
        P("fsdp", None),
        P("fsdp", None),
        P("fsdp", None),
        P("fsdp", None),
        P("fsdp", None),
    )
    return jax.shard_map(local, mesh=mesh, in_specs=in_specs, out_specs=out_specs, check_vma=False)
```

```python
from functools import partial

import jax
import jax.numpy as jnp
from jax import lax
from jax.experimental import pallas as pl
from jax.experimental.pallas import tpu as pltpu
from jax.sharding import PartitionSpec as P

QUERY_HEADS = 15
KEY_VALUE_HEADS = 5
HEAD_SIZE = 64
GROUP = QUERY_HEADS // KEY_VALUE_HEADS
MODEL = QUERY_HEADS * HEAD_SIZE
QK_WIDTH = (QUERY_HEADS + KEY_VALUE_HEADS) * HEAD_SIZE
V_START = QK_WIDTH + MODEL - HEAD_SIZE
V_HEAD = 1
SCALE = HEAD_SIZE ** (-0.5)

PIECE = 4

epsilon = 1e-05
negative = -1e30
narrow_dtype = jnp.bfloat16
wide_type = jnp.float32


def rows_dot(left, right):
    return lax.dot_general(left, right, (((1,), (0,)), ((), ())), preferred_element_type=wide_type)


def rows_dot_t(left, right):
    return lax.dot_general(left, right, (((1,), (1,)), ((), ())), preferred_element_type=wide_type)


def columns_dot(left, right):
    return lax.dot_general(left, right, (((0,), (0,)), ((), ())), preferred_element_type=wide_type)


def inverse_rms(rows):
    return lax.rsqrt(jnp.mean(rows * rows, axis=-1, keepdims=True) + epsilon)


def norm_back(rows, inverse, gain, incoming):
    weighted = incoming * gain
    mean = jnp.mean(weighted * rows, axis=-1, keepdims=True)
    d_rows = inverse * weighted - rows * (inverse * inverse * inverse * mean)
    return d_rows, jnp.sum(incoming * rows * inverse, axis=0, keepdims=True)


def rotate(block, cosines, sines):
    lanes = lax.broadcasted_iota(jnp.int32, block.shape, 1)
    swapped = jnp.where(lanes % HEAD_SIZE < HEAD_SIZE // 2, pltpu.roll(block, 96, 1), pltpu.roll(block, 32, 1))
    return block * cosines + swapped * sines


def causal_bias(count, length):
    row = lax.broadcasted_iota(jnp.int32, (count, count), 0)
    column = lax.broadcasted_iota(jnp.int32, (count, count), 1)
    allowed = column <= row
    if length is not None:
        allowed = allowed & (column < length)
    bias = jnp.where(allowed, 0.0, negative)
    return jnp.concatenate([bias] * GROUP, axis=0)


def head_columns(ref, first, count):
    return jnp.concatenate(
        [ref[:, (first + i) * HEAD_SIZE : (first + i + 1) * HEAD_SIZE] for i in range(count)], axis=0
    )


def attention_forward(rows, gain, router_row, cosines, sines, bias, weight, normed_ref, qk_ref, v_ref, att_ref, log_ref):
    count = rows.shape[0]
    normed_ref[...] = (rows * inverse_rms(rows) * gain).astype(narrow_dtype)
    normed = normed_ref[...]
    gating = jax.nn.sigmoid(jnp.sum(normed.astype(wide_type) * router_row, axis=-1, keepdims=True))
    for block in range(QK_WIDTH // 256):
        product = rows_dot(normed, weight[:, block * 256 : (block + 1) * 256])
        for part in range(2):
            piece = rotate(product[:, part * 128 : (part + 1) * 128], cosines, sines)
            at = block * 256 + part * 128
            qk_ref[:, at : at + 128] = piece.astype(narrow_dtype)
    v_ref[...] = rows_dot(normed, weight[:, V_START:]).astype(narrow_dtype)
    for head in range(KEY_VALUE_HEADS):
        queries = head_columns(qk_ref, head * GROUP, GROUP)
        keys = head_columns(qk_ref, QUERY_HEADS + head, 1)
        values = head_columns(v_ref, V_HEAD + head, 1)
        scores = rows_dot_t(queries, keys) * SCALE + bias
        peak = jnp.max(scores, axis=-1, keepdims=True)
        expanded = jnp.exp(scores - peak)
        total = jnp.sum(expanded, axis=-1, keepdims=True)
        log_ref[:, head : head + 1] = peak + jnp.log(total)
        attended = rows_dot((expanded / total).astype(narrow_dtype), values).astype(narrow_dtype)
        for i in range(GROUP):
            at = (head * GROUP + i) * HEAD_SIZE
            att_ref[:, at : at + HEAD_SIZE] = attended[i * count : (i + 1) * count]
    return rows_dot(att_ref[...], weight[:, QK_WIDTH : QK_WIDTH + MODEL]), gating


def attention_backward(
    rows, gain, router_row, cosines, sines, bias, weight, normed_ref, qk_ref, v_ref, log_ref,
    d_attn_low, d_gating, gating, d_att_ref, d_raw_ref, d_qk_ref, d_v_ref,
):
    count = rows.shape[0]
    d_att_ref[...] = rows_dot_t(d_attn_low, weight[:, QK_WIDTH : QK_WIDTH + MODEL]).astype(narrow_dtype)
    d_v_ref[...] = jnp.zeros_like(d_v_ref)
    for head in range(KEY_VALUE_HEADS):
        queries = head_columns(qk_ref, head * GROUP, GROUP)
        keys = head_columns(qk_ref, QUERY_HEADS + head, 1)
        values = head_columns(v_ref, V_HEAD + head, 1)
        d_attended = head_columns(d_att_ref, head * GROUP, GROUP)
        scores = rows_dot_t(queries, keys) * SCALE + bias
        probabilities = jnp.exp(scores - log_ref[:, head : head + 1])
        d_probs = rows_dot_t(d_attended, values)
        row_dot = jnp.sum(probabilities * d_probs, axis=-1, keepdims=True)
        d_raw = (probabilities * (d_probs - row_dot) * SCALE).astype(narrow_dtype)
        d_queries = rows_dot(d_raw, keys)
        for i in range(GROUP):
            at = (head * GROUP + i) * HEAD_SIZE
            d_raw_ref[:, at : at + HEAD_SIZE] = d_queries[i * count : (i + 1) * count]
        at = (QUERY_HEADS + head) * HEAD_SIZE
        d_raw_ref[:, at : at + HEAD_SIZE] = columns_dot(queries, d_raw).T
        at = (V_HEAD + head) * HEAD_SIZE
        d_values = columns_dot(d_attended, probabilities.astype(narrow_dtype)).T
        d_v_ref[:, at : at + HEAD_SIZE] = d_values.astype(narrow_dtype)
    for block in range(QK_WIDTH // 128):
        at = block * 128
        d_qk_ref[:, at : at + 128] = rotate(d_raw_ref[:, at : at + 128], cosines, -sines).astype(narrow_dtype)
    d_normed = rows_dot_t(d_qk_ref[...], weight[:, :QK_WIDTH]) + rows_dot_t(d_v_ref[...], weight[:, V_START:])
    d_logit = d_gating * gating * (1.0 - gating)
    d_normed = d_normed + d_logit * router_row
    router_gradient = jnp.sum(d_logit * normed_ref[...].astype(wide_type), axis=0, keepdims=True)
    d_rows, gain_gradient = norm_back(rows, inverse_rms(rows), gain, d_normed)
    return d_rows, gain_gradient, router_gradient


def ffn_forward(after, gain, w_gate, w_up, w_down, ffn_ref, hidden_ref, gate_ref=None, up_ref=None, ready=()):
    ffn_ref[...] = (after * inverse_rms(after) * gain).astype(narrow_dtype)
    gate = rows_dot(ffn_ref[...], w_gate[...])
    up = rows_dot(ffn_ref[...], w_up[...])
    if gate_ref is not None:
        gate_ref[...] = gate
        up_ref[...] = up
    hidden_ref[...] = (gate * jax.nn.sigmoid(gate) * up).astype(narrow_dtype)
    for copy in ready:
        copy.wait()
    return rows_dot_t(hidden_ref[...], w_down[...])


def ffn_backward(after, gain, w_gate, w_up, w_down, d_ffn_ref, gate, up, d_gate_ref, d_up_ref):
    d_hidden = rows_dot(d_ffn_ref[...], w_down[...])
    sig = jax.nn.sigmoid(gate)
    d_gate_ref[...] = (d_hidden * up * sig * (1.0 + gate * (1.0 - sig))).astype(narrow_dtype)
    d_up_ref[...] = (d_hidden * gate * sig).astype(narrow_dtype)
    total = rows_dot_t(d_gate_ref[...], w_gate[...]) + rows_dot_t(d_up_ref[...], w_up[...])
    return norm_back(after, inverse_rms(after), gain, total)


def pick_exact(selector, rows):
    high = rows.astype(narrow_dtype)
    rest = rows - high.astype(wide_type)
    middle = rest.astype(narrow_dtype)
    low = (rest - middle.astype(wide_type)).astype(narrow_dtype)
    return rows_dot(selector, high) + rows_dot(selector, middle) + rows_dot(selector, low)


def first_attention_kernel(
    fetch, length_ref, at_ref, hidden_t, cotangent_t, small, cosines, sines, *refs
):
    sources, refs = refs[: fetch.count], refs[fetch.count :]
    hidden_in, cotangent, normed_ref, qk_ref, v_ref, att_ref, log_ref, out_ref, gating_ref, weight, sems = refs
    hidden_in[...] = hidden_t[...].T
    cotangent[...] = cotangent_t[...].T
    copies = fetch.start(at_ref, sources, {"attn": weight}, sems)
    rows = hidden_in[...].astype(wide_type)
    for copy in copies["attn"]:
        copy.wait()
    bias = causal_bias(rows.shape[0], length_ref[0])
    attn_out, gating = attention_forward(
        rows, small[0:1], small[2:3], cosines[...], sines[...], bias, weight, normed_ref, qk_ref, v_ref, att_ref, log_ref
    )
    out_ref[...] = attn_out
    gating_ref[...] = jnp.broadcast_to(gating, gating_ref.shape)


def last_attention_kernel(
    fetch, length_ref, at_ref, hidden_in, small, cosines, sines, normed_ref, qk_ref, v_ref, att_ref, log_ref, gating_ref,
    d_gating_ref, d_attn_ref, d_input_ref, normed_rest, att_rest, d_qk_rest, d_v_rest, small_middle, hidden_out, *refs,
):
    sources, refs = refs[: fetch.count], refs[fetch.count :]
    (
        d_qk_ref, d_v_ref, normed_t_ref, att_t_ref, grad_hidden_t, small_out, small_parts, hidden_out_t,
        d_att_ref, d_raw_ref, weight, sems,
    ) = refs
    copies = fetch.start(at_ref, sources, {"attn": weight}, sems)
    for copy in copies["attn"]:
        copy.wait()
    count = hidden_in.shape[0]
    one = pl.ds(0, count)
    rest = pl.ds(count, d_qk_ref.shape[0] - count)
    rows = hidden_in[...].astype(wide_type)
    bias = causal_bias(count, length_ref[0])
    d_rows, gain_gradient, router_gradient = attention_backward(
        rows, small[0:1], small[2:3], cosines[...], sines[...], bias, weight, normed_ref, qk_ref, v_ref, log_ref,
        d_attn_ref[one, :MODEL], d_gating_ref[:, 0:1], gating_ref[:, 0:1], d_att_ref, d_raw_ref, d_qk_ref.at[one], d_v_ref.at[one],
    )
    grad_hidden_t[...] = (d_input_ref[...] + d_rows).T
    hidden_out_t[...] = hidden_out[...].T
    small_out[...] = small_middle[...]
    small_out[0:1] += gain_gradient
    small_out[2:3] = router_gradient
    small_parts[...] = jnp.zeros_like(small_parts)
    size = MODEL // small_parts.shape[0]
    for owner in range(small_parts.shape[0]):
        small_parts[owner, :, 0:size] = small_out[:, owner * size : (owner + 1) * size]
    d_qk_ref[rest] = d_qk_rest[...]
    d_v_ref[rest] = d_v_rest[...]
    normed_t_ref[...] = jnp.concatenate([normed_ref[...], normed_rest[...]], axis=0).T
    att_t_ref[...] = jnp.concatenate([att_ref[...], att_rest[...]], axis=0).T


def middle_kernel(
    fetch, length_ref, at_ref, hidden_in, cotangent, small, attn_out_ref, gating_ref, cos_two, sin_two, cos_three, sin_three,
    row_two, row_three, *refs,
):
    sources, refs = refs[: fetch.count], refs[fetch.count :]
    (
        hidden_out, d_input_ref, d_gating_ref, small_out, hidden_all, d_ffn_t_ref, d_gate_rest, d_up_rest, d_attn_rest,
        att_rest, normed_rest, d_qk_rest, d_v_rest, ffn_one, ffn_rest, d_ffn_one,
        w_attn, w_pair, w_down, sems,
        gate_two, up_two, gate_three, up_three, change_one, change_two, change_three,
        qk_two, v_two, log_two, qk_three, v_three, log_three, d_att_two, d_raw_two, d_att_three, d_raw_three, d_ffn_rest,
    ) = refs
    copies = fetch.start(at_ref, sources, {"pair": w_pair, "down": w_down, "attn": w_attn}, sems)
    w_gate, w_up = w_pair.at[0], w_pair.at[1]
    count_two, count_three = row_two.shape[1], row_three.shape[1]
    count_one = hidden_in.shape[0]
    in_one, in_two = pl.ds(0, count_one), pl.ds(count_one, count_two)
    in_three = pl.ds(count_one + count_two, count_three)
    two = pl.ds(0, count_two)
    three = pl.ds(count_two, count_three)
    gain_attn, gain_ffn = small[0:1], small[1:2]

    def spread(row_ref):
        hit = lax.broadcasted_iota(jnp.int32, (count_one, row_ref.shape[1]), 0) == row_ref[...]
        return jnp.where(hit, 1.0, 0.0)

    put_two = spread(row_two)
    pick_two = put_two.T.astype(narrow_dtype)
    put_two = put_two.astype(narrow_dtype)
    put_three = rows_dot(pick_two, spread(row_three).astype(narrow_dtype))
    pick_three = put_three.T.astype(narrow_dtype)
    put_three = put_three.astype(narrow_dtype)

    after_one = hidden_in[...].astype(wide_type) + attn_out_ref[...]
    for copy in copies["pair"]:
        copy.wait()
    ffn_out = ffn_forward(
        after_one, gain_ffn, w_gate, w_up, w_down, ffn_one, hidden_all.at[in_one], ready=copies["down"]
    )
    valid = lax.broadcasted_iota(jnp.int32, (count_one, 1), 0) < length_ref[0]
    scale_one = jnp.where(valid, gating_ref[:, 0:1], 0.0)
    change_one[...] = attn_out_ref[...] + ffn_out
    d_input_ref[...] = hidden_in[...].astype(wide_type) + scale_one * change_one[...]

    for copy in copies["attn"]:
        copy.wait()
    d_attn_rest[...] = jnp.zeros_like(d_attn_rest)
    state_two = pick_exact(pick_two, d_input_ref[...])
    bias_two = causal_bias(count_two, None)
    attn_two, gating_two = attention_forward(
        state_two, gain_attn, small[3:4], cos_two[...], sin_two[...], bias_two, w_attn,
        normed_rest.at[two], qk_two, v_two, att_rest.at[two], log_two,
    )
    after_two = state_two + attn_two
    change_two[...] = attn_two + ffn_forward(
        after_two, gain_ffn, w_gate, w_up, w_down, ffn_rest.at[two], hidden_all.at[in_two], gate_two, up_two
    )
    delta_two = gating_two * change_two[...]

    state_three = pick_exact(pick_three, state_two + delta_two)
    bias_three = causal_bias(count_three, None)
    attn_three, gating_three = attention_forward(
        state_three, gain_attn, small[4:5], cos_three[...], sin_three[...], bias_three, w_attn,
        normed_rest.at[three], qk_three, v_three, att_rest.at[three], log_three,
    )
    after_three = state_three + attn_three
    change_three[...] = attn_three + ffn_forward(
        after_three, gain_ffn, w_gate, w_up, w_down, ffn_rest.at[three], hidden_all.at[in_three], gate_three, up_three
    )
    added = delta_two + pick_exact(put_three, gating_three * change_three[...])
    hidden_out[...] = (d_input_ref[...] + pick_exact(put_two, added)).astype(narrow_dtype)

    incoming_two = rows_dot(pick_two, cotangent[...])
    incoming_three = rows_dot(pick_three, incoming_two.astype(narrow_dtype))
    d_change = gating_three * incoming_three
    d_gating = jnp.sum(change_three[...] * incoming_three, axis=-1, keepdims=True)
    d_ffn_rest[three] = d_change.astype(narrow_dtype)
    d_after, gain_ffn_three = ffn_backward(
        after_three, gain_ffn, w_gate, w_up, w_down, d_ffn_rest.at[three], gate_three[...], up_three[...],
        d_gate_rest.at[three], d_up_rest.at[three],
    )
    d_attn_rest[three, :MODEL] = (d_change + d_after).astype(narrow_dtype)
    d_rows, gain_attn_three, router_three = attention_backward(
        state_three, gain_attn, small[4:5], cos_three[...], sin_three[...], bias_three, w_attn, normed_rest.at[three],
        qk_three, v_three, log_three, d_attn_rest[three, :MODEL], d_gating, gating_three, d_att_three, d_raw_three,
        d_qk_rest.at[three], d_v_rest.at[three],
    )
    back_three = pick_exact(put_three, d_rows + d_after)

    incoming_two = incoming_two + back_three
    d_change = gating_two * incoming_two
    d_gating = jnp.sum(change_two[...] * incoming_two, axis=-1, keepdims=True)
    d_ffn_rest[two] = d_change.astype(narrow_dtype)
    d_after, gain_ffn_two = ffn_backward(
        after_two, gain_ffn, w_gate, w_up, w_down, d_ffn_rest.at[two], gate_two[...], up_two[...],
        d_gate_rest.at[two], d_up_rest.at[two],
    )
    d_attn_rest[two, :MODEL] = (d_change + d_after).astype(narrow_dtype)
    d_rows, gain_attn_two, router_two = attention_backward(
        state_two, gain_attn, small[3:4], cos_two[...], sin_two[...], bias_two, w_attn, normed_rest.at[two],
        qk_two, v_two, log_two, d_attn_rest[two, :MODEL], d_gating, gating_two, d_att_two, d_raw_two,
        d_qk_rest.at[two], d_v_rest.at[two],
    )
    back_two = back_three + d_rows + d_after

    incoming = cotangent[...].astype(wide_type) + pick_exact(put_two, back_two)
    d_input_ref[...] = incoming
    d_gating = jnp.where(valid, jnp.sum(change_one[...] * incoming, axis=-1, keepdims=True), 0.0)
    d_gating_ref[...] = jnp.broadcast_to(d_gating, d_gating_ref.shape)
    d_ffn_one[...] = (scale_one * incoming).astype(narrow_dtype)
    small_out[...] = jnp.zeros_like(small_out)
    small_out[0:1] = gain_attn_two + gain_attn_three
    small_out[1:2] = gain_ffn_two + gain_ffn_three
    small_out[3:4] = router_two
    small_out[4:5] = router_three
    d_ffn_t_ref[...] = jnp.concatenate([d_ffn_one[...], d_ffn_rest[...]], axis=0).T


def last_ffn_kernel(
    fetch, length_ref, at_ref, hidden_in, small, attn_out_ref, gating_ref, d_input_in, d_ffn_one,
    ffn_one, ffn_rest, d_gate_rest, d_up_rest, d_attn_rest, small_middle, *refs,
):
    sources, refs = refs[: fetch.count], refs[fetch.count :]
    d_gate_all, d_up_all, d_attn_all, ffn_t_ref, d_input_ref, small_out, w_pair, w_down, sems = refs
    copies = fetch.start(at_ref, sources, {"pair": w_pair, "down": w_down}, sems)
    count = hidden_in.shape[0]
    one, rest = pl.ds(0, count), pl.ds(count, d_gate_all.shape[0] - count)
    d_gate_all[rest] = d_gate_rest[...]
    d_up_all[rest] = d_up_rest[...]
    d_attn_all[rest] = d_attn_rest[...]
    d_attn_all[one] = jnp.zeros((count, d_attn_all.shape[1]), narrow_dtype)
    ffn_t_ref[...] = jnp.concatenate([ffn_one[...], ffn_rest[...]], axis=0).T
    valid = lax.broadcasted_iota(jnp.int32, (count, 1), 0) < length_ref[0]
    scale = jnp.where(valid, gating_ref[:, 0:1], 0.0)
    after_one = hidden_in[...].astype(wide_type) + attn_out_ref[...]
    for copy in copies["pair"]:
        copy.wait()
    gate = rows_dot(ffn_one[...], w_pair[0])
    up = rows_dot(ffn_one[...], w_pair[1])
    for copy in copies["down"]:
        copy.wait()
    d_after, gain_gradient = ffn_backward(
        after_one, small[1:2], w_pair.at[0], w_pair.at[1], w_down, d_ffn_one, gate, up,
        d_gate_all.at[one], d_up_all.at[one],
    )
    d_attn_all[one, :MODEL] = (scale * d_input_in[...] + d_after).astype(narrow_dtype)
    d_input_ref[...] = d_input_in[...] + d_after
    small_out[...] = small_middle[...]
    small_out[1:2] += gain_gradient


def rotary_tables(positions):
    half = HEAD_SIZE // 2
    lanes = jnp.arange(2 * HEAD_SIZE)
    frequency = 10000.0 ** (-(lanes % half).astype(wide_type) / half)
    angles = positions.astype(wide_type)[:, None] * frequency[None, :]
    sign = jnp.where(lanes % HEAD_SIZE < half, -1.0, 1.0)
    return jnp.cos(angles), jnp.sin(angles) * sign[None, :]


def call(kernel, operands, outputs, limit, scratch=(), hbm=0, scalars=1):
    specs = [
        pl.BlockSpec(memory_space=pltpu.SMEM if i < scalars else (pl.ANY if i >= len(operands) - hbm else pltpu.VMEM))
        for i in range(len(operands))
    ]
    return pl.pallas_call(
        kernel,
        out_shape=[jax.ShapeDtypeStruct(shape, kind) for shape, kind in outputs],
        in_specs=specs,
        out_specs=[pl.BlockSpec(memory_space=pltpu.VMEM)] * len(outputs),
        scratch_shapes=list(scratch),
        compiler_params=pltpu.CompilerParams(vmem_limit_bytes=limit * 2**20),
        cost_estimate=pl.CostEstimate(flops=1000, bytes_accessed=1000, transcendentals=0),
    )(*operands)


def partner(value, axis, bit):
    count = lax.axis_size(axis)
    return lax.ppermute(value, axis, [(i, i ^ bit) for i in range(count)])


def after(value, *others):
    return lax.optimization_barrier((value,) + others)[0]


def bits_of(axis, low):
    found = []
    bit = low
    while bit < lax.axis_size(axis):
        found.append(bit)
        bit = bit * 2
    return found


CORE, ROW, LAYER = 1, 2, 4


class Place:
    def __init__(self, model_rows, ff):
        group = lax.axis_index("dp")
        self.owners = lax.axis_size("fsdp")
        self.layers = lax.axis_size("dp") // LAYER
        self.blocks = self.owners == 2 and self.layers == 4 and model_rows % 32 == 0 and ff % (128 * self.layers) == 0
        self.scalars = (lax.axis_index("fsdp"), group % 2, group // ROW % 2, group // LAYER)
        self.vector = jnp.stack(self.scalars).astype(jnp.int32)


def local_step(place, fn, operands, outputs, limit):
    shapes = [((count, rows, columns), kind) for count, rows, columns, kind in outputs]

    def kernel(at_ref, *refs):
        made = fn(tuple(at_ref[i] for i in range(4)), *refs[: len(operands)])
        for blocks, ref in zip(made, refs[len(operands) :]):
            for i, block in enumerate(blocks):
                ref[i] = block.astype(ref.dtype)

    return call(kernel, (place.vector,) + tuple(operands), shapes, limit)


def wide_sum(*blocks):
    total = blocks[0].astype(wide_type)
    for block in blocks[1:]:
        total = total + block.astype(wide_type)
    return total


class Part:
    def __init__(self, place, product, rows, columns, tall=False, extra=None):
        self.place, self.product, self.rows, self.columns, self.tall = place, product, rows, columns, tall
        self.extra, self.tail = extra, 0 if extra is None else 8
        self.count = 2 * place.layers

    def out(self, count):
        return (count, self.rows + self.tail, self.columns, narrow_dtype)

    def step(self, fn, operands, counts, limit=12):
        return local_step(self.place, fn, operands, [self.out(count) for count in counts], limit)

    def blocks(self, value):
        r, c = self.rows, self.columns
        if self.tall:
            return [value[i * r : (i + 1) * r] for i in range(self.count)]
        return [value[y * r : (y + 1) * r, z * c : (z + 1) * c] for y in range(2) for z in range(self.place.layers)]

    def made(self, owner, core, refs):
        found = self.blocks(self.product(owner, core, *refs))
        if self.tail:
            below = self.extra(owner, *refs)
            found = [jnp.concatenate([block, below], axis=0) for block in found]
        return found

    def away(self, operands, sides):
        def fn(at, *refs):
            blocks = sum((self.made(at[0] ^ offset, 1 - at[1], refs) for offset in sides), [])
            return [blocks[i : i + PIECE] for i in range(0, len(blocks), PIECE)]

        return self.step(fn, operands, [PIECE] * (len(sides) * self.count // PIECE), 18)

    def keep(self, received, operands, sides):
        def fn(at, *refs):
            received, refs = refs[: -len(operands)], refs[-len(operands) :]
            return [
                [
                    wide_sum(block, received[(number * self.count + i) // PIECE][i % PIECE])
                    for i, block in enumerate(self.made(at[0] ^ offset, at[1], refs))
                ]
                for number, offset in enumerate(sides)
            ]

        return self.step(fn, tuple(received) + tuple(operands), [self.count] * len(sides), 18)

    def add_x(self, values):
        def fn(at, keep, received):
            layers = self.place.layers
            return [
                [wide_sum(keep[row * layers + z], received[row * layers + z]) for z in range(layers)]
                for row in (at[2], 1 - at[2])
            ]

        return self.step(fn, values, [self.place.layers] * 2)

    def add_y(self, values):
        def fn(at, keep, received):
            odd = at[3] % 2
            return [[wide_sum(keep[2 * j + side], received[2 * j + side]) for j in range(2)] for side in (odd, 1 - odd)]

        return self.step(fn, values, [2, 2])

    def add_z(self, values):
        return self.step(lambda at, keep, received: [[wide_sum(keep[j], received[j]) for j in range(2)]], values, [2])[0]

    def add_last(self, values):
        def fn(at, keep, received):
            totals = [wide_sum(keep[j], received[j]) for j in range(2)]
            return [[total[: self.rows] for total in totals], [totals[0][self.rows :]]][: 1 + (self.tail > 0)]

        outputs = [(2, self.rows, self.columns, narrow_dtype), (1, self.tail, self.columns, wide_type)]
        return local_step(self.place, fn, values, outputs[: 1 + (self.tail > 0)], 12)

    def join_z(self, values):
        def fn(at, own, received):
            odd = at[3] % 2
            return [[jnp.where(odd == i % 2, own[i // 2], received[i // 2]) for i in range(4)]]

        return local_step(self.place, fn, values, [(4, self.rows, self.columns, narrow_dtype)], 12)[0]

    def final(self, values, kind, cuts=None):
        place = self.place
        shape = (self.rows * 4, self.columns * place.layers)
        if self.tall:
            shape = (self.rows * self.count, self.columns * 2)

        def kernel(at_ref, *refs):
            out = refs[-1]
            outs = refs[len(values) : -1]
            for source in range(4):
                core, y = at_ref[1] ^ (source // 2), at_ref[2] ^ (source % 2)
                for z in range(place.layers):
                    if self.tall:
                        row, column = (y * place.layers + z) * self.rows, pl.multiple_of(core * self.columns, 128)
                    else:
                        row, column = (core * 2 + y) * self.rows, z * self.columns
                    spot = (pl.ds(pl.multiple_of(row, 8), self.rows), pl.ds(column, self.columns))
                    out[spot] = refs[source][z].astype(kind)
            for (start, stop, turned), ref in zip(cuts or (), outs):
                piece = out[:, start:stop]
                ref[...] = piece.T if turned else piece

        if cuts is None:
            return call(kernel, (place.vector,) + tuple(values), [(shape, kind)], 20)[0]
        shapes = [
            ((stop - start, shape[0]) if turned else (shape[0], stop - start), kind) for start, stop, turned in cuts
        ]
        return call(kernel, (place.vector,) + tuple(values), shapes, 28, [pltpu.VMEM(shape, kind)])


class Order:
    def __init__(self):
        self.last = None

    def hold(self, value):
        return value if self.last is None else after(value, self.last)

    def step(self, work, values):
        result = work([self.hold(values[0])] + list(values[1:]))
        self.last = result[0] if isinstance(result, (list, tuple)) else result
        return result


def reduce_all(parts, operands, order, beside, cuts):
    count = len(parts)
    state = [{} for _ in parts]
    done, extras = [None] * count, []

    def step(k, work, *names):
        return order.step(work, [state[k][name] for name in names])

    def away(k, sides=(0, 1)):
        made = order.step(lambda values: parts[k].away(values, sides), operands[k]())
        state[k]["core"] = [partner(piece, "dp", CORE) for piece in made]

    def keep(k, sides=(0, 1)):
        taken = operands[k]()
        taken[0] = order.hold(taken[0])
        made = parts[k].keep(state[k]["core"], taken, sides)
        order.last = made[0]
        for side, value in zip(sides, made):
            state[k][("keep", "go")[side]] = value

    def start_x(k):
        state[k]["moved"] = partner(order.hold(state[k]["go"]), "fsdp", 1)

    away(0, (1,))
    going = state[0]["core"]
    away(0, (0,))
    staying, state[0]["core"] = state[0]["core"], going
    keep(0, (1,))
    start_x(0)
    state[0]["core"] = staying
    keep(0, (0,))
    beside[0]()
    away(1)
    keep(1)
    for k in range(count + 3):
        now, last, before = k < count, 1 <= k <= count, 2 <= k <= count + 1
        if now:
            state[k]["y"], moved = step(k, parts[k].add_x, "keep", "moved")
            state[k]["y moved"] = partner(moved, "dp", ROW)
        if k + 1 < count:
            start_x(k + 1)
        if 3 <= k:
            done[k - 3] = order.step(lambda values: parts[k - 3].final(values, wide_type, cuts[k - 3]), state[k - 3]["cores"])
        if k == 0:
            beside[1]()
        if now:
            state[k]["z"], moved = step(k, parts[k].add_y, "y", "y moved")
            state[k]["z moved"] = partner(moved, "dp", LAYER)
        if last:
            state[k - 1]["sum"], *more = step(k - 1, parts[k - 1].add_last, "half", "half moved")
            extras += more
            state[k - 1]["sum moved"] = partner(state[k - 1]["sum"], "dp", LAYER)
        if before:
            own, moved = order.hold(state[k - 2]["four"]), order.hold(state[k - 2]["four moved"])
            order.last = moved
            state[k - 2]["cores"] = [own, moved] + [partner(value, "dp", CORE) for value in (own, moved)]
        if k + 2 < count:
            away(k + 2)
            keep(k + 2)
        if now:
            state[k]["half"] = step(k, parts[k].add_z, "z", "z moved")
            state[k]["half moved"] = partner(state[k]["half"], "dp", 2 * LAYER)
        if last:
            state[k - 1]["four"] = step(k - 1, parts[k - 1].join_z, "sum", "sum moved")
            state[k - 1]["four moved"] = partner(state[k - 1]["four"], "dp", ROW)
    return done, extras


def reduce_plain(matrices):
    return [
        lax.psum(lax.psum_scatter(matrix, "fsdp", scatter_dimension=dim, tiled=True), "dp").astype(wide_type)
        for matrix, dim in matrices
    ]


class Fetch:
    def __init__(self, operands, blocks):
        self.operands, self.blocks, self.count = operands, blocks, len(operands)

    def scratch(self):
        return pltpu.SemaphoreType.DMA((len(self.blocks),))

    def start(self, at_ref, sources, targets, sems):
        at = tuple(at_ref[i] for i in range(4))
        copies = {}
        for number, (target, operand, index, spot, (rows, columns)) in enumerate(self.blocks):
            source = sources[operand] if index is None else sources[operand].at[index]
            lead, row, column = spot(at)
            row = row if isinstance(row, int) else pl.multiple_of(row, 16)
            column = column if isinstance(column, int) else pl.multiple_of(column, 128)
            place = lead + (pl.ds(row, rows), pl.ds(column, columns))
            copy = pltpu.make_async_copy(source, targets[target].at[place], sems.at[number])
            copy.start()
            copies.setdefault(target, []).append(copy)
        return copies


def attention_shard_kernel(at_ref, query, key_t, out, value_t, low_ref, half_ref):
    start = 0
    for block in (query[...], key_t[...].T, out[...], value_t[...].T):
        low_ref[:, start : start + block.shape[1]] = block.astype(narrow_dtype)
        start += block.shape[1]
    rows = half_ref.shape[0]
    half_ref[...] = low_ref[pl.ds(pl.multiple_of(at_ref[1] * rows, 16), rows), :]


def down_shard_kernel(at_ref, down_t, low_ref, half_ref):
    low_ref[...] = down_t[...].astype(narrow_dtype)
    columns = half_ref.shape[1]
    half_ref[...] = low_ref[:, pl.ds(pl.multiple_of(at_ref[1] * columns, 128), columns)]


def narrow_kernel(wide_ref, narrow_ref):
    narrow_ref[...] = wide_ref[...].astype(narrow_dtype)


def narrowed(values):
    rows, columns = values[0].shape
    width = 512
    spec = pl.BlockSpec((rows, width), lambda i: (0, i))
    return pl.pallas_call(
        narrow_kernel,
        grid=(columns // width,),
        out_shape=jax.ShapeDtypeStruct((rows, columns), narrow_dtype),
        in_specs=[spec],
        out_specs=spec,
        compiler_params=pltpu.CompilerParams(vmem_limit_bytes=16 * 2**20),
        cost_estimate=pl.CostEstimate(flops=1000, bytes_accessed=1000, transcendentals=0),
    )(values[0])


def gather_weights(place, order, small, attn, pair, down_t, beside):
    mine, core, row, layer = place.scalars
    layers = place.layers
    model_rows, ff = pair[0].shape
    model, down_columns = down_t.shape
    low = lambda value: value.astype(narrow_dtype)
    attn_width = sum(value.shape[1] for value in attn)
    if not place.blocks:
        attn_full, gate, up, down_full = (
            lax.all_gather(low(value), "fsdp", axis=axis, tiled=True)
            for value, axis in ((jnp.concatenate(attn, axis=1), 0), (pair[0], 0), (pair[1], 0), (down_t, 1))
        )
        zero = lambda at: ((), 0, 0)
        first = Fetch([attn_full], [("attn", 0, None, zero, attn_full.shape)])
        every = Fetch(
            [attn_full, gate, up, down_full],
            [
                ("pair", 1, None, lambda at: ((0,), 0, 0), gate.shape),
                ("pair", 2, None, lambda at: ((1,), 0, 0), up.shape),
                ("down", 3, None, zero, down_full.shape),
                ("attn", 0, None, zero, attn_full.shape),
            ],
        )
        beside(first, lax.all_gather(small, "fsdp", axis=1, tiled=True))
        return first, every, Fetch(every.operands, every.blocks[:3])
    columns = ff // layers
    half = model_rows // 2
    half_columns = down_columns // 2
    own_piece = jnp.where(
        row == 0,
        lax.dynamic_slice(pair[0], (core * half, layer * columns), (half, columns)),
        lax.dynamic_slice(pair[1], (core * half, layer * columns), (half, columns)),
    )
    small_block = jnp.pad(small, ((0, 0), (0, columns - small.shape[1])))
    own_piece = jnp.concatenate([low(own_piece), small_block], axis=0)
    piece = partner(own_piece, "fsdp", 1)
    order.last = own_piece
    attn_low, attn_half = order.step(
        lambda values: call(
            attention_shard_kernel,
            [place.vector] + values,
            [((model_rows, attn_width), narrow_dtype), ((half, attn_width), narrow_dtype)],
            24,
        ),
        [attn[0], attn[1].T, attn[2], attn[3].T],
    )
    piece = order.hold(piece)
    order.last = piece
    pieces = [[piece] + [partner(piece, "dp", offset * LAYER) for offset in range(1, layers)]]
    pieces.append([partner(piece, "dp", ROW)])
    attn_near = partner(after(attn_half, piece), "fsdp", 1)
    down_low, down_half = order.step(
        lambda values: call(
            down_shard_kernel,
            [place.vector] + values,
            [(down_t.shape, narrow_dtype), ((model, half_columns), narrow_dtype)],
            24,
        ),
        [down_t],
    )
    gate_low = order.step(narrowed, [pair[0]])
    up_low = order.step(narrowed, [pair[1]])
    def over_y(index):
        moved = order.last = order.hold(pieces[0][index])
        pieces[0][index] = moved
        pieces[1].append(partner(moved, "dp", ROW))

    def arrived(index):
        pieces[1][index] = order.last = order.hold(pieces[1][index])

    over_y(1)
    over_y(2)
    arrived(0)
    over_y(3)
    attn_near = order.last = order.hold(attn_near)
    down_near = partner(after(down_half, attn_near), "fsdp", 1)
    attn_other = partner(attn_near, "dp", CORE)

    def halves(target, first):
        size = (half, attn_width)
        return [
            (target, first, None, lambda at: ((), at[0] * model_rows, 0), (model_rows, size[1])),
            (target, first + 1, None, lambda at: ((), (1 - at[0]) * model_rows + at[1] * half, 0), size),
            (target, first + 2, None, lambda at: ((), (1 - at[0]) * model_rows + (1 - at[1]) * half, 0), size),
        ]

    first = Fetch([attn_low, attn_near, attn_other], halves("attn", 0))
    order.last = attn_other
    small_other = piece[half:, : small.shape[1]]
    small_rows = jnp.where(
        mine == 0, jnp.concatenate([small, small_other], axis=1), jnp.concatenate([small_other, small], axis=1)
    )
    beside(first, small_rows)
    arrived(1)
    arrived(2)
    arrived(3)
    pieces += [[partner(moved, "dp", CORE) for moved in group] for group in pieces]
    down_near = order.hold(down_near)
    down_other = partner(down_near, "dp", CORE)
    blocks = [
        ("pair", 6, None, lambda at: ((0,), at[0] * model_rows, 0), (model_rows, ff)),
        ("pair", 7, None, lambda at: ((1,), at[0] * model_rows, 0), (model_rows, ff)),
    ]
    for number in range(4):
        for offset in range(layers):

            def spot(at, number=number, offset=offset):
                lead = (at[2] ^ (number % 2),)
                return (lead, (1 - at[0]) * model_rows + (at[1] ^ (number // 2)) * half, (at[3] ^ offset) * columns)

            blocks.append(("pair", 8 + number * layers + offset, (pl.ds(0, half),), spot, (half, columns)))
    near = (model, half_columns)
    blocks += [
        ("down", 3, None, lambda at: ((), 0, at[0] * down_columns), (model, down_columns)),
        ("down", 4, None, lambda at: ((), 0, (1 - at[0]) * down_columns + at[1] * half_columns), near),
        ("down", 5, None, lambda at: ((), 0, (1 - at[0]) * down_columns + (1 - at[1]) * half_columns), near),
    ]
    blocks += halves("attn", 0)
    operands = [attn_low, attn_near, attn_other, down_low, down_near, down_other, gate_low, up_low] + sum(pieces, [])
    ffn_blocks = [(block[0], block[1] - 3) + block[2:] for block in blocks if block[0] != "attn"]
    return first, Fetch(operands, blocks), Fetch(operands[3:], ffn_blocks)


def local(
    hidden_in,
    cotangent,
    norm_attn,
    norm_ffn,
    router,
    w_query,
    key_weight,
    value_weight,
    w_out,
    w_gate,
    w_up,
    w_down,
    lengths,
    chosen_second,
    chosen_third,
):
    place = Place(*w_gate.shape)
    owners, layers = place.owners, place.layers
    mine = place.scalars[0]
    width = w_query.shape[1]
    kv_width = key_weight.shape[1]
    small = jnp.concatenate(
        [norm_attn[None, :], norm_ffn[None, :], router.T, jnp.zeros((11, norm_attn.shape[0]), wide_type)]
    ).astype(narrow_dtype)
    count_one, model = hidden_in.shape
    ff = w_gate.shape[1]
    attn_width = 2 * width + 2 * kv_width
    chosen_two, chosen_three = chosen_second[0], chosen_third[0]
    count_two, count_three = chosen_two.shape[0], chosen_three.shape[0]
    count_rest = count_two + count_three
    count_all = count_one + count_rest
    cos_one, sin_one = rotary_tables(jnp.arange(count_one))
    cos_two, sin_two = rotary_tables(chosen_two)
    cos_three, sin_three = rotary_tables(chosen_three)
    v_width = attn_width - V_START
    first_outputs, small_wide = [], None

    def first_attention(fetch, small_rows):
        nonlocal small_wide
        small_wide = small_rows[:8].astype(wide_type)
        first_outputs.extend(
            call(
                partial(first_attention_kernel, fetch),
                [lengths, place.vector, after(order.hold(hidden_in.T), cos_two, sin_two, cos_three, sin_three), cotangent.T, small_wide, cos_one, sin_one]
                + fetch.operands,
                [
                    ((count_one, model), narrow_dtype),
                    ((count_one, model), narrow_dtype),
                    ((count_one, model), narrow_dtype),
                    ((count_one, QK_WIDTH), narrow_dtype),
                    ((count_one, v_width), narrow_dtype),
                    ((count_one, model), narrow_dtype),
                    ((GROUP * count_one, 128), wide_type),
                    ((count_one, model), wide_type),
                    ((count_one, 128), wide_type),
                ],
                32,
                attn_scratch + [fetch.scratch()],
                hbm=fetch.count,
                scalars=2,
            )
        )
        order.last = first_outputs[0]

    order = Order()
    attn_scratch = [pltpu.VMEM((model, attn_width), narrow_dtype)]
    fetch_attn, fetch_all, fetch_ffn = gather_weights(
        place, order, small, (w_query, key_weight, w_out, value_weight), (w_gate, w_up), w_down.T, first_attention
    )
    hidden_rows, cotangent_rows, normed_one, qk_one, v_one, att_one, log_one, attn_out_one, gating_one = first_outputs
    rest = lambda width: ((count_rest, width), narrow_dtype)
    every = lambda width: ((count_all, width), narrow_dtype)
    turned = ((model, count_all), narrow_dtype)
    scratch_for = lambda count: [
        pltpu.VMEM((count, QK_WIDTH), narrow_dtype),
        pltpu.VMEM((count, v_width), narrow_dtype),
        pltpu.VMEM((GROUP * count, 128), wide_type),
    ]
    back_scratch = lambda count: [
        pltpu.VMEM((count, model), narrow_dtype),
        pltpu.VMEM((count, QK_WIDTH), wide_type),
    ]
    wide = lambda count, width: pltpu.VMEM((count, width), wide_type)
    attn_tiles = -(-model // 128) * 128
    (
        hidden_out, d_input, d_gating_one, small_middle, hidden, d_ffn_t, d_gate_rest, d_up_rest, d_attn_rest,
        att_rest, normed_rest, d_qk_rest, d_v_rest, ffn_one, ffn_rest, d_ffn_one,
    ) = call(
        partial(middle_kernel, fetch_all),
        [
            lengths, place.vector, hidden_rows, cotangent_rows, small_wide, attn_out_one, gating_one,
            cos_two, sin_two, cos_three, sin_three,
            chosen_two[None, :], chosen_three[None, :],
        ]
        + fetch_all.operands,
        [
            ((count_one, model), narrow_dtype), ((count_one, model), wide_type), ((count_one, 128), wide_type),
            ((8, model), wide_type), every(ff), turned, rest(ff), rest(ff), rest(attn_tiles),
            rest(model), rest(model), rest(QK_WIDTH), rest(v_width),
            ((count_one, model), narrow_dtype), rest(model), ((count_one, model), narrow_dtype),
        ],
        36,
        [
            pltpu.VMEM((model, attn_width), narrow_dtype),
            pltpu.VMEM((2, model, ff), narrow_dtype),
            pltpu.VMEM((model, ff), narrow_dtype),
            fetch_all.scratch(),
            wide(count_two, ff), wide(count_two, ff), wide(count_three, ff), wide(count_three, ff),
            wide(count_one, model), wide(count_two, model), wide(count_three, model),
        ]
        + scratch_for(count_two) + scratch_for(count_three) + back_scratch(count_two) + back_scratch(count_three)
        + [pltpu.VMEM((count_rest, model), narrow_dtype)],
        hbm=fetch_all.count,
        scalars=2,
    )

    small_tile = attn_width // layers
    attention, feed = [], []

    def last_ffn():
        feed.extend(
            call(
                partial(last_ffn_kernel, fetch_ffn),
                [
                    lengths, place.vector, hidden_rows, small_wide, attn_out_one, gating_one, d_input,
                    order.hold(d_ffn_one), ffn_one, ffn_rest, d_gate_rest, d_up_rest, d_attn_rest,
                    small_middle,
                ]
                + fetch_ffn.operands,
                [
                    every(ff), every(ff), every(attn_tiles), turned, ((count_one, model), wide_type),
                    ((8, model), wide_type),
                ],
                38,
                [
                    pltpu.VMEM((2, model, ff), narrow_dtype),
                    pltpu.VMEM((model, ff), narrow_dtype),
                    fetch_ffn.scratch(),
                ],
                hbm=fetch_ffn.count,
                scalars=2,
            )
        )
        order.last = feed[0]

    def last_attention():
        d_attn, d_input_last, small_feed = feed[2], feed[4], feed[5]
        attention.extend(
            call(
                partial(last_attention_kernel, fetch_attn),
                [
                    lengths, place.vector, hidden_rows, small_wide, cos_one, sin_one, normed_one, qk_one, v_one, att_one,
                    log_one, gating_one, d_gating_one, order.hold(d_attn), d_input_last, normed_rest, att_rest, d_qk_rest,
                    d_v_rest, small_feed, hidden_out,
                ]
                + fetch_attn.operands,
                [
                    every(QK_WIDTH), every(v_width), turned, turned, ((model, count_one), wide_type),
                    ((8, model), wide_type), ((owners, 8, small_tile), wide_type), ((model, count_one), narrow_dtype),
                ],
                26,
                back_scratch(count_one) + attn_scratch + [fetch_attn.scratch()],
                hbm=fetch_attn.count,
                scalars=2,
            )
        )
        order.last = attention[0]

    if not place.blocks:
        last_ffn()
        last_attention()
        d_gate, d_up, d_attn, ffn_t, _, _ = feed
        d_qk, d_v, normed_t, att_t, grad_hidden_t, small_all, _, hidden_out_t = attention
        narrow_dot = lambda left, right: rows_dot(left, right).astype(narrow_dtype)
        skip = V_HEAD * HEAD_SIZE
        down_t, *reduced = reduce_plain(
            [
                (narrow_dot(d_ffn_t, hidden), 1),
                (narrow_dot(ffn_t, d_gate), 0),
                (narrow_dot(ffn_t, d_up), 0),
                (narrow_dot(normed_t, d_qk), 0),
                (narrow_dot(att_t, d_attn[:, :model]), 0),
                (narrow_dot(normed_t, d_v[:, skip:]), 0),
            ]
        )
        small_all = lax.psum_scatter(lax.psum(small_all, "dp"), "fsdp", scatter_dimension=1, tiled=True)
        return (
            hidden_out_t.T, grad_hidden_t.T, small_all[0], small_all[1], small_all[2:5].T,
            reduced[2][:, :width], reduced[2][:, width:], reduced[4], reduced[3], reduced[0], reduced[1], down_t.T,
        )
    by_core = lambda left: left.reshape(owners * 2, model // owners // 2, left.shape[1])
    size = ff // owners // 2

    def down_product(owner, core, left, right):
        return rows_dot(left[...], right[:, pl.ds(pl.multiple_of((owner * 2 + core) * size, 128), size)])

    def plain_product(owner, core, left, right):
        return rows_dot(left[owner * 2 + core], right[...])

    def small_block(owner, normed, d_qk, att, d_attn, d_v, small_parts):
        return small_parts[owner]

    def attention_product(owner, core, normed, d_qk, att, d_attn, d_v, small_parts):
        left = normed[owner * 2 + core]
        out = rows_dot(att[owner * 2 + core], d_attn[...])
        value = rows_dot(left, d_v[...])
        shared = attn_tiles - 128
        return jnp.concatenate(
            [rows_dot(left, d_qk[...]), out[:, :shared], out[:, shared:] + value[:, :128], value[:, 128:]], axis=1
        )

    rows = model // owners // 4
    parts = [
        Part(place, down_product, model // 2 // layers, size, tall=True),
        Part(place, plain_product, rows, ff // layers),
        Part(place, plain_product, rows, ff // layers),
        Part(place, attention_product, rows, attn_width // layers, extra=small_block),
    ]
    operands = [
        lambda: [d_ffn_t, hidden],
        lambda: [by_core(feed[3]), feed[0]],
        lambda: [by_core(feed[3]), feed[1]],
        lambda: [by_core(attention[2]), attention[0], by_core(attention[3]), feed[2], attention[1], attention[6]],
    ]
    cuts = [
        (0, width, False),
        (width, width + kv_width, True),
        (width + kv_width, 2 * width + kv_width, False),
        (2 * width + kv_width, attn_width, True),
    ]
    reduced, small_sum = reduce_all(parts, operands, order, (last_ffn, last_attention), [None, None, None, cuts])
    down_t, gate_shard, up_shard, (query_shard, key_t, out_shard, value_t) = reduced
    small_sum = small_sum[0][0][:, : model // owners]
    return (
        attention[7].T,
        attention[4].T,
        small_sum[0],
        small_sum[1],
        small_sum[2:5].T,
        query_shard,
        key_t.T,
        value_t.T,
        out_shard,
        gate_shard,
        up_shard,
        down_t.T,
    )


def solution(mesh):
    in_specs = (
        P(("dp", "fsdp"), None),
        P(("dp", "fsdp"), None),
        P("fsdp"),
        P("fsdp"),
        P("fsdp", None),
        P("fsdp", None),
        P("fsdp", None),
        P("fsdp", None),
        P("fsdp", None),
        P("fsdp", None),
        P("fsdp", None),
        P("fsdp", None),
        P(("dp", "fsdp")),
        P(("dp", "fsdp"), None),
        P(("dp", "fsdp"), None),
    )
    out_specs = (
        P(("dp", "fsdp"), None),
        P(("dp", "fsdp"), None),
        P("fsdp"),
        P("fsdp"),
        P("fsdp", None),
        P("fsdp", None),
        P("fsdp", None),
        P("fsdp", None),
        P("fsdp", None),
        P("fsdp", None),
        P("fsdp", None),
        P("fsdp", None),
    )
    return jax.shard_map(local, mesh=mesh, in_specs=in_specs, out_specs=out_specs, check_vma=False)
```

```python
from functools import partial

import jax
import jax.numpy as jnp
from jax import lax
from jax.experimental import pallas as pl
from jax.experimental.pallas import tpu as pltpu
from jax.sharding import PartitionSpec as P

QUERY_HEADS = 15
KEY_VALUE_HEADS = 5
HEAD_SIZE = 64
GROUP = QUERY_HEADS // KEY_VALUE_HEADS
MODEL = QUERY_HEADS * HEAD_SIZE
QK_WIDTH = (QUERY_HEADS + KEY_VALUE_HEADS) * HEAD_SIZE
V_START = QK_WIDTH + MODEL - HEAD_SIZE
V_HEAD = 1
SCALE = HEAD_SIZE ** (-0.5)

PIECE = 4

epsilon = 1e-05
negative = -1e30
narrow_dtype = jnp.bfloat16
wide_type = jnp.float32


def rows_dot(left, right):
    return lax.dot_general(left, right, (((1,), (0,)), ((), ())), preferred_element_type=wide_type)


def rows_dot_t(left, right):
    return lax.dot_general(left, right, (((1,), (1,)), ((), ())), preferred_element_type=wide_type)


def columns_dot(left, right):
    return lax.dot_general(left, right, (((0,), (0,)), ((), ())), preferred_element_type=wide_type)


def inverse_rms(rows):
    return lax.rsqrt(jnp.mean(rows * rows, axis=-1, keepdims=True) + epsilon)


def norm_back(rows, inverse, gain, incoming):
    weighted = incoming * gain
    mean = jnp.mean(weighted * rows, axis=-1, keepdims=True)
    d_rows = inverse * weighted - rows * (inverse * inverse * inverse * mean)
    return d_rows, jnp.sum(incoming * rows * inverse, axis=0, keepdims=True)


def rotate(block, cosines, sines):
    lanes = lax.broadcasted_iota(jnp.int32, block.shape, 1)
    swapped = jnp.where(lanes % HEAD_SIZE < HEAD_SIZE // 2, pltpu.roll(block, 96, 1), pltpu.roll(block, 32, 1))
    return block * cosines + swapped * sines


def causal_bias(count, length):
    row = lax.broadcasted_iota(jnp.int32, (count, count), 0)
    column = lax.broadcasted_iota(jnp.int32, (count, count), 1)
    allowed = column <= row
    if length is not None:
        allowed = allowed & (column < length)
    bias = jnp.where(allowed, 0.0, negative)
    return jnp.concatenate([bias] * GROUP, axis=0)


def head_columns(ref, first, count):
    return jnp.concatenate(
        [ref[:, (first + i) * HEAD_SIZE : (first + i + 1) * HEAD_SIZE] for i in range(count)], axis=0
    )


def attention_forward(rows, gain, router_row, cosines, sines, bias, weight, normed_ref, qk_ref, v_ref, att_ref, log_ref):
    count = rows.shape[0]
    normed_ref[...] = (rows * inverse_rms(rows) * gain).astype(narrow_dtype)
    normed = normed_ref[...]
    gating = jax.nn.sigmoid(jnp.sum(normed.astype(wide_type) * router_row, axis=-1, keepdims=True))
    for block in range(QK_WIDTH // 256):
        product = rows_dot(normed, weight[:, block * 256 : (block + 1) * 256])
        for part in range(2):
            piece = rotate(product[:, part * 128 : (part + 1) * 128], cosines, sines)
            at = block * 256 + part * 128
            qk_ref[:, at : at + 128] = piece.astype(narrow_dtype)
    v_ref[...] = rows_dot(normed, weight[:, V_START:]).astype(narrow_dtype)
    for head in range(KEY_VALUE_HEADS):
        queries = head_columns(qk_ref, head * GROUP, GROUP)
        keys = head_columns(qk_ref, QUERY_HEADS + head, 1)
        values = head_columns(v_ref, V_HEAD + head, 1)
        scores = rows_dot_t(queries, keys) * SCALE + bias
        peak = jnp.max(scores, axis=-1, keepdims=True)
        expanded = jnp.exp(scores - peak)
        total = jnp.sum(expanded, axis=-1, keepdims=True)
        log_ref[:, head : head + 1] = peak + jnp.log(total)
        attended = rows_dot((expanded / total).astype(narrow_dtype), values).astype(narrow_dtype)
        for i in range(GROUP):
            at = (head * GROUP + i) * HEAD_SIZE
            att_ref[:, at : at + HEAD_SIZE] = attended[i * count : (i + 1) * count]
    return rows_dot(att_ref[...], weight[:, QK_WIDTH : QK_WIDTH + MODEL]), gating


def attention_backward(
    rows, gain, router_row, cosines, sines, bias, weight, normed_ref, qk_ref, v_ref, log_ref,
    d_attn_low, d_gating, gating, d_att_ref, d_raw_ref, d_qk_ref, d_v_ref,
):
    count = rows.shape[0]
    d_att_ref[...] = rows_dot_t(d_attn_low, weight[:, QK_WIDTH : QK_WIDTH + MODEL]).astype(narrow_dtype)
    d_v_ref[...] = jnp.zeros_like(d_v_ref)
    for head in range(KEY_VALUE_HEADS):
        queries = head_columns(qk_ref, head * GROUP, GROUP)
        keys = head_columns(qk_ref, QUERY_HEADS + head, 1)
        values = head_columns(v_ref, V_HEAD + head, 1)
        d_attended = head_columns(d_att_ref, head * GROUP, GROUP)
        scores = rows_dot_t(queries, keys) * SCALE + bias
        probabilities = jnp.exp(scores - log_ref[:, head : head + 1])
        d_probs = rows_dot_t(d_attended, values)
        row_dot = jnp.sum(probabilities * d_probs, axis=-1, keepdims=True)
        d_raw = (probabilities * (d_probs - row_dot) * SCALE).astype(narrow_dtype)
        d_queries = rows_dot(d_raw, keys)
        for i in range(GROUP):
            at = (head * GROUP + i) * HEAD_SIZE
            d_raw_ref[:, at : at + HEAD_SIZE] = d_queries[i * count : (i + 1) * count]
        at = (QUERY_HEADS + head) * HEAD_SIZE
        d_raw_ref[:, at : at + HEAD_SIZE] = columns_dot(queries, d_raw).T
        at = (V_HEAD + head) * HEAD_SIZE
        d_values = columns_dot(d_attended, probabilities.astype(narrow_dtype)).T
        d_v_ref[:, at : at + HEAD_SIZE] = d_values.astype(narrow_dtype)
    for block in range(QK_WIDTH // 128):
        at = block * 128
        d_qk_ref[:, at : at + 128] = rotate(d_raw_ref[:, at : at + 128], cosines, -sines).astype(narrow_dtype)
    d_normed = rows_dot_t(d_qk_ref[...], weight[:, :QK_WIDTH]) + rows_dot_t(d_v_ref[...], weight[:, V_START:])
    d_logit = d_gating * gating * (1.0 - gating)
    d_normed = d_normed + d_logit * router_row
    router_gradient = jnp.sum(d_logit * normed_ref[...].astype(wide_type), axis=0, keepdims=True)
    d_rows, gain_gradient = norm_back(rows, inverse_rms(rows), gain, d_normed)
    return d_rows, gain_gradient, router_gradient


def ffn_forward(after, gain, w_gate, w_up, w_down, ffn_ref, hidden_ref, gate_ref=None, up_ref=None, ready=()):
    ffn_ref[...] = (after * inverse_rms(after) * gain).astype(narrow_dtype)
    gate = rows_dot(ffn_ref[...], w_gate[...])
    up = rows_dot(ffn_ref[...], w_up[...])
    if gate_ref is not None:
        gate_ref[...] = gate
        up_ref[...] = up
    hidden_ref[...] = (gate * jax.nn.sigmoid(gate) * up).astype(narrow_dtype)
    for copy in ready:
        copy.wait()
    return rows_dot_t(hidden_ref[...], w_down[...])


def ffn_backward(after, gain, w_gate, w_up, w_down, d_ffn_ref, gate, up, d_gate_ref, d_up_ref):
    d_hidden = rows_dot(d_ffn_ref[...], w_down[...])
    sig = jax.nn.sigmoid(gate)
    d_gate_ref[...] = (d_hidden * up * sig * (1.0 + gate * (1.0 - sig))).astype(narrow_dtype)
    d_up_ref[...] = (d_hidden * gate * sig).astype(narrow_dtype)
    total = rows_dot_t(d_gate_ref[...], w_gate[...]) + rows_dot_t(d_up_ref[...], w_up[...])
    return norm_back(after, inverse_rms(after), gain, total)


def pick_exact(selector, rows):
    high = rows.astype(narrow_dtype)
    rest = rows - high.astype(wide_type)
    middle = rest.astype(narrow_dtype)
    low = (rest - middle.astype(wide_type)).astype(narrow_dtype)
    return rows_dot(selector, high) + rows_dot(selector, middle) + rows_dot(selector, low)


def first_attention_kernel(
    fetch, length_ref, at_ref, hidden_t, cotangent_t, small, cosines, sines, *refs
):
    sources, refs = refs[: fetch.count], refs[fetch.count :]
    hidden_in, cotangent, normed_ref, qk_ref, v_ref, att_ref, log_ref, out_ref, gating_ref, weight, sems = refs
    hidden_in[...] = hidden_t[...].T
    cotangent[...] = cotangent_t[...].T
    copies = fetch.start(at_ref, sources, {"attn": weight}, sems)
    rows = hidden_in[...].astype(wide_type)
    for copy in copies["attn"]:
        copy.wait()
    bias = causal_bias(rows.shape[0], length_ref[0])
    attn_out, gating = attention_forward(
        rows, small[0:1], small[2:3], cosines[...], sines[...], bias, weight, normed_ref, qk_ref, v_ref, att_ref, log_ref
    )
    out_ref[...] = attn_out
    gating_ref[...] = jnp.broadcast_to(gating, gating_ref.shape)


def last_attention_kernel(
    fetch, length_ref, at_ref, hidden_in, small, cosines, sines, normed_ref, qk_ref, v_ref, att_ref, log_ref, gating_ref,
    d_gating_ref, d_attn_ref, d_input_ref, normed_rest, att_rest, d_qk_rest, d_v_rest, small_middle, hidden_out, *refs,
):
    sources, refs = refs[: fetch.count], refs[fetch.count :]
    (
        d_qk_ref, d_v_ref, normed_t_ref, att_t_ref, grad_hidden_t, small_out, small_parts, hidden_out_t,
        d_att_ref, d_raw_ref, weight, sems,
    ) = refs
    copies = fetch.start(at_ref, sources, {"attn": weight}, sems)
    for copy in copies["attn"]:
        copy.wait()
    count = hidden_in.shape[0]
    one = pl.ds(0, count)
    rest = pl.ds(count, d_qk_ref.shape[0] - count)
    rows = hidden_in[...].astype(wide_type)
    bias = causal_bias(count, length_ref[0])
    d_rows, gain_gradient, router_gradient = attention_backward(
        rows, small[0:1], small[2:3], cosines[...], sines[...], bias, weight, normed_ref, qk_ref, v_ref, log_ref,
        d_attn_ref[one, :MODEL], d_gating_ref[:, 0:1], gating_ref[:, 0:1], d_att_ref, d_raw_ref, d_qk_ref.at[one], d_v_ref.at[one],
    )
    grad_hidden_t[...] = (d_input_ref[...] + d_rows).T
    hidden_out_t[...] = hidden_out[...].T
    small_out[...] = small_middle[...]
    small_out[0:1] += gain_gradient
    small_out[2:3] = router_gradient
    small_parts[...] = jnp.zeros_like(small_parts)
    size = MODEL // small_parts.shape[0]
    for owner in range(small_parts.shape[0]):
        small_parts[owner, :, 0:size] = small_out[:, owner * size : (owner + 1) * size]
    d_qk_ref[rest] = d_qk_rest[...]
    d_v_ref[rest] = d_v_rest[...]
    normed_t_ref[...] = jnp.concatenate([normed_ref[...], normed_rest[...]], axis=0).T
    att_t_ref[...] = jnp.concatenate([att_ref[...], att_rest[...]], axis=0).T


def middle_kernel(
    fetch, length_ref, at_ref, hidden_in, cotangent, small, attn_out_ref, gating_ref, cos_two, sin_two, cos_three, sin_three,
    row_two, row_three, *refs,
):
    sources, refs = refs[: fetch.count], refs[fetch.count :]
    (
        hidden_out, d_input_ref, d_gating_ref, small_out, hidden_all, d_ffn_t_ref, d_gate_rest, d_up_rest, d_attn_rest,
        att_rest, normed_rest, d_qk_rest, d_v_rest, ffn_one, ffn_rest, d_ffn_one,
        w_attn, w_pair, w_down, sems,
        gate_two, up_two, gate_three, up_three, change_one, change_two, change_three,
        qk_two, v_two, log_two, qk_three, v_three, log_three, d_att_two, d_raw_two, d_att_three, d_raw_three, d_ffn_rest,
    ) = refs
    copies = fetch.start(at_ref, sources, {"pair": w_pair, "down": w_down, "attn": w_attn}, sems)
    w_gate, w_up = w_pair.at[0], w_pair.at[1]
    count_two, count_three = row_two.shape[1], row_three.shape[1]
    count_one = hidden_in.shape[0]
    in_one, in_two = pl.ds(0, count_one), pl.ds(count_one, count_two)
    in_three = pl.ds(count_one + count_two, count_three)
    two = pl.ds(0, count_two)
    three = pl.ds(count_two, count_three)
    gain_attn, gain_ffn = small[0:1], small[1:2]

    def spread(row_ref):
        hit = lax.broadcasted_iota(jnp.int32, (count_one, row_ref.shape[1]), 0) == row_ref[...]
        return jnp.where(hit, 1.0, 0.0)

    put_two = spread(row_two)
    pick_two = put_two.T.astype(narrow_dtype)
    put_two = put_two.astype(narrow_dtype)
    put_three = rows_dot(pick_two, spread(row_three).astype(narrow_dtype))
    pick_three = put_three.T.astype(narrow_dtype)
    put_three = put_three.astype(narrow_dtype)

    after_one = hidden_in[...].astype(wide_type) + attn_out_ref[...]
    for copy in copies["pair"]:
        copy.wait()
    ffn_out = ffn_forward(
        after_one, gain_ffn, w_gate, w_up, w_down, ffn_one, hidden_all.at[in_one], ready=copies["down"]
    )
    valid = lax.broadcasted_iota(jnp.int32, (count_one, 1), 0) < length_ref[0]
    scale_one = jnp.where(valid, gating_ref[:, 0:1], 0.0)
    change_one[...] = attn_out_ref[...] + ffn_out
    d_input_ref[...] = hidden_in[...].astype(wide_type) + scale_one * change_one[...]

    for copy in copies["attn"]:
        copy.wait()
    d_attn_rest[...] = jnp.zeros_like(d_attn_rest)
    state_two = pick_exact(pick_two, d_input_ref[...])
    bias_two = causal_bias(count_two, None)
    attn_two, gating_two = attention_forward(
        state_two, gain_attn, small[3:4], cos_two[...], sin_two[...], bias_two, w_attn,
        normed_rest.at[two], qk_two, v_two, att_rest.at[two], log_two,
    )
    after_two = state_two + attn_two
    change_two[...] = attn_two + ffn_forward(
        after_two, gain_ffn, w_gate, w_up, w_down, ffn_rest.at[two], hidden_all.at[in_two], gate_two, up_two
    )
    delta_two = gating_two * change_two[...]

    state_three = pick_exact(pick_three, state_two + delta_two)
    bias_three = causal_bias(count_three, None)
    attn_three, gating_three = attention_forward(
        state_three, gain_attn, small[4:5], cos_three[...], sin_three[...], bias_three, w_attn,
        normed_rest.at[three], qk_three, v_three, att_rest.at[three], log_three,
    )
    after_three = state_three + attn_three
    change_three[...] = attn_three + ffn_forward(
        after_three, gain_ffn, w_gate, w_up, w_down, ffn_rest.at[three], hidden_all.at[in_three], gate_three, up_three
    )
    added = delta_two + pick_exact(put_three, gating_three * change_three[...])
    hidden_out[...] = (d_input_ref[...] + pick_exact(put_two, added)).astype(narrow_dtype)

    incoming_two = rows_dot(pick_two, cotangent[...])
    incoming_three = rows_dot(pick_three, incoming_two.astype(narrow_dtype))
    d_change = gating_three * incoming_three
    d_gating = jnp.sum(change_three[...] * incoming_three, axis=-1, keepdims=True)
    d_ffn_rest[three] = d_change.astype(narrow_dtype)
    d_after, gain_ffn_three = ffn_backward(
        after_three, gain_ffn, w_gate, w_up, w_down, d_ffn_rest.at[three], gate_three[...], up_three[...],
        d_gate_rest.at[three], d_up_rest.at[three],
    )
    d_attn_rest[three, :MODEL] = (d_change + d_after).astype(narrow_dtype)
    d_rows, gain_attn_three, router_three = attention_backward(
        state_three, gain_attn, small[4:5], cos_three[...], sin_three[...], bias_three, w_attn, normed_rest.at[three],
        qk_three, v_three, log_three, d_attn_rest[three, :MODEL], d_gating, gating_three, d_att_three, d_raw_three,
        d_qk_rest.at[three], d_v_rest.at[three],
    )
    back_three = pick_exact(put_three, d_rows + d_after)

    incoming_two = incoming_two + back_three
    d_change = gating_two * incoming_two
    d_gating = jnp.sum(change_two[...] * incoming_two, axis=-1, keepdims=True)
    d_ffn_rest[two] = d_change.astype(narrow_dtype)
    d_after, gain_ffn_two = ffn_backward(
        after_two, gain_ffn, w_gate, w_up, w_down, d_ffn_rest.at[two], gate_two[...], up_two[...],
        d_gate_rest.at[two], d_up_rest.at[two],
    )
    d_attn_rest[two, :MODEL] = (d_change + d_after).astype(narrow_dtype)
    d_rows, gain_attn_two, router_two = attention_backward(
        state_two, gain_attn, small[3:4], cos_two[...], sin_two[...], bias_two, w_attn, normed_rest.at[two],
        qk_two, v_two, log_two, d_attn_rest[two, :MODEL], d_gating, gating_two, d_att_two, d_raw_two,
        d_qk_rest.at[two], d_v_rest.at[two],
    )
    back_two = back_three + d_rows + d_after

    incoming = cotangent[...].astype(wide_type) + pick_exact(put_two, back_two)
    d_input_ref[...] = incoming
    d_gating = jnp.where(valid, jnp.sum(change_one[...] * incoming, axis=-1, keepdims=True), 0.0)
    d_gating_ref[...] = jnp.broadcast_to(d_gating, d_gating_ref.shape)
    d_ffn_one[...] = (scale_one * incoming).astype(narrow_dtype)
    small_out[...] = jnp.zeros_like(small_out)
    small_out[0:1] = gain_attn_two + gain_attn_three
    small_out[1:2] = gain_ffn_two + gain_ffn_three
    small_out[3:4] = router_two
    small_out[4:5] = router_three
    d_ffn_t_ref[...] = jnp.concatenate([d_ffn_one[...], d_ffn_rest[...]], axis=0).T


def last_ffn_kernel(
    fetch, length_ref, at_ref, hidden_in, small, attn_out_ref, gating_ref, d_input_in, d_ffn_one,
    ffn_one, ffn_rest, d_gate_rest, d_up_rest, d_attn_rest, small_middle, *refs,
):
    sources, refs = refs[: fetch.count], refs[fetch.count :]
    d_gate_all, d_up_all, d_attn_all, ffn_t_ref, d_input_ref, small_out, w_pair, w_down, sems = refs
    copies = fetch.start(at_ref, sources, {"pair": w_pair, "down": w_down}, sems)
    count = hidden_in.shape[0]
    one, rest = pl.ds(0, count), pl.ds(count, d_gate_all.shape[0] - count)
    d_gate_all[rest] = d_gate_rest[...]
    d_up_all[rest] = d_up_rest[...]
    d_attn_all[rest] = d_attn_rest[...]
    d_attn_all[one] = jnp.zeros((count, d_attn_all.shape[1]), narrow_dtype)
    ffn_t_ref[...] = jnp.concatenate([ffn_one[...], ffn_rest[...]], axis=0).T
    valid = lax.broadcasted_iota(jnp.int32, (count, 1), 0) < length_ref[0]
    scale = jnp.where(valid, gating_ref[:, 0:1], 0.0)
    after_one = hidden_in[...].astype(wide_type) + attn_out_ref[...]
    for copy in copies["pair"]:
        copy.wait()
    gate = rows_dot(ffn_one[...], w_pair[0])
    up = rows_dot(ffn_one[...], w_pair[1])
    for copy in copies["down"]:
        copy.wait()
    d_after, gain_gradient = ffn_backward(
        after_one, small[1:2], w_pair.at[0], w_pair.at[1], w_down, d_ffn_one, gate, up,
        d_gate_all.at[one], d_up_all.at[one],
    )
    d_attn_all[one, :MODEL] = (scale * d_input_in[...] + d_after).astype(narrow_dtype)
    d_input_ref[...] = d_input_in[...] + d_after
    small_out[...] = small_middle[...]
    small_out[1:2] += gain_gradient


def rotary_tables(positions):
    half = HEAD_SIZE // 2
    lanes = jnp.arange(2 * HEAD_SIZE)
    frequency = 10000.0 ** (-(lanes % half).astype(wide_type) / half)
    angles = positions.astype(wide_type)[:, None] * frequency[None, :]
    sign = jnp.where(lanes % HEAD_SIZE < half, -1.0, 1.0)
    return jnp.cos(angles), jnp.sin(angles) * sign[None, :]


def call(kernel, operands, outputs, limit, scratch=(), hbm=0, scalars=1):
    specs = [
        pl.BlockSpec(memory_space=pltpu.SMEM if i < scalars else (pl.ANY if i >= len(operands) - hbm else pltpu.VMEM))
        for i in range(len(operands))
    ]
    return pl.pallas_call(
        kernel,
        out_shape=[jax.ShapeDtypeStruct(shape, kind) for shape, kind in outputs],
        in_specs=specs,
        out_specs=[pl.BlockSpec(memory_space=pltpu.VMEM)] * len(outputs),
        scratch_shapes=list(scratch),
        compiler_params=pltpu.CompilerParams(vmem_limit_bytes=limit * 2**20),
        cost_estimate=pl.CostEstimate(flops=1000, bytes_accessed=1000, transcendentals=0),
    )(*operands)


def partner(value, axis, bit):
    count = lax.axis_size(axis)
    return lax.ppermute(value, axis, [(i, i ^ bit) for i in range(count)])


def after(value, *others):
    return lax.optimization_barrier((value,) + others)[0]


def bits_of(axis, low):
    found = []
    bit = low
    while bit < lax.axis_size(axis):
        found.append(bit)
        bit = bit * 2
    return found


CORE, ROW, LAYER = 1, 2, 4


class Place:
    def __init__(self, model_rows, ff):
        group = lax.axis_index("dp")
        self.owners = lax.axis_size("fsdp")
        self.layers = lax.axis_size("dp") // LAYER
        self.blocks = self.owners == 2 and self.layers == 4 and model_rows % 32 == 0 and ff % (128 * self.layers) == 0
        self.scalars = (lax.axis_index("fsdp"), group % 2, group // ROW % 2, group // LAYER)
        self.vector = jnp.stack(self.scalars).astype(jnp.int32)


def local_step(place, fn, operands, outputs, limit):
    shapes = [((count, rows, columns), kind) for count, rows, columns, kind in outputs]

    def kernel(at_ref, *refs):
        made = fn(tuple(at_ref[i] for i in range(4)), *refs[: len(operands)])
        for blocks, ref in zip(made, refs[len(operands) :]):
            for i, block in enumerate(blocks):
                ref[i] = block.astype(ref.dtype)

    return call(kernel, (place.vector,) + tuple(operands), shapes, limit)


def wide_sum(*blocks):
    total = blocks[0].astype(wide_type)
    for block in blocks[1:]:
        total = total + block.astype(wide_type)
    return total


class Part:
    def __init__(self, place, product, rows, columns, tall=False, extra=None):
        self.place, self.product, self.rows, self.columns, self.tall = place, product, rows, columns, tall
        self.extra, self.tail = extra, 0 if extra is None else 8
        self.count = 2 * place.layers

    def out(self, count):
        return (count, self.rows + self.tail, self.columns, narrow_dtype)

    def step(self, fn, operands, counts, limit=12):
        return local_step(self.place, fn, operands, [self.out(count) for count in counts], limit)

    def blocks(self, value):
        r, c = self.rows, self.columns
        if self.tall:
            return [value[i * r : (i + 1) * r] for i in range(self.count)]
        return [value[y * r : (y + 1) * r, z * c : (z + 1) * c] for y in range(2) for z in range(self.place.layers)]

    def made(self, owner, core, refs):
        found = self.blocks(self.product(owner, core, *refs))
        if self.tail:
            below = self.extra(owner, *refs)
            found = [jnp.concatenate([block, below], axis=0) for block in found]
        return found

    def away(self, operands, sides):
        def fn(at, *refs):
            blocks = sum((self.made(at[0] ^ offset, 1 - at[1], refs) for offset in sides), [])
            return [blocks[i : i + PIECE] for i in range(0, len(blocks), PIECE)]

        return self.step(fn, operands, [PIECE] * (len(sides) * self.count // PIECE), 18)

    def keep(self, received, operands, sides):
        def fn(at, *refs):
            received, refs = refs[: -len(operands)], refs[-len(operands) :]
            return [
                [
                    wide_sum(block, received[(number * self.count + i) // PIECE][i % PIECE])
                    for i, block in enumerate(self.made(at[0] ^ offset, at[1], refs))
                ]
                for number, offset in enumerate(sides)
            ]

        return self.step(fn, tuple(received) + tuple(operands), [self.count] * len(sides), 18)

    def add_x(self, values):
        def fn(at, keep, received):
            layers = self.place.layers
            return [
                [wide_sum(keep[row * layers + z], received[row * layers + z]) for z in range(layers)]
                for row in (at[2], 1 - at[2])
            ]

        return self.step(fn, values, [self.place.layers] * 2)

    def add_y(self, values):
        def fn(at, keep, received):
            odd = at[3] % 2
            return [[wide_sum(keep[2 * j + side], received[2 * j + side]) for j in range(2)] for side in (odd, 1 - odd)]

        return self.step(fn, values, [2, 2])

    def add_z(self, values):
        return self.step(lambda at, keep, received: [[wide_sum(keep[j], received[j]) for j in range(2)]], values, [2])[0]

    def add_last(self, values):
        def fn(at, keep, received):
            totals = [wide_sum(keep[j], received[j]) for j in range(2)]
            return [[total[: self.rows] for total in totals], [totals[0][self.rows :]]][: 1 + (self.tail > 0)]

        outputs = [(2, self.rows, self.columns, narrow_dtype), (1, self.tail, self.columns, wide_type)]
        return local_step(self.place, fn, values, outputs[: 1 + (self.tail > 0)], 12)

    def join_z(self, values):
        def fn(at, own, received):
            odd = at[3] % 2
            return [[jnp.where(odd == i % 2, own[i // 2], received[i // 2]) for i in range(4)]]

        return local_step(self.place, fn, values, [(4, self.rows, self.columns, narrow_dtype)], 12)[0]

    def final(self, values, kind, cuts=None):
        place = self.place
        shape = (self.rows * 4, self.columns * place.layers)
        if self.tall:
            shape = (self.rows * self.count, self.columns * 2)

        def kernel(at_ref, *refs):
            out = refs[-1]
            outs = refs[len(values) : -1]
            for source in range(4):
                core, y = at_ref[1] ^ (source // 2), at_ref[2] ^ (source % 2)
                for z in range(place.layers):
                    if self.tall:
                        row, column = (y * place.layers + z) * self.rows, pl.multiple_of(core * self.columns, 128)
                    else:
                        row, column = (core * 2 + y) * self.rows, z * self.columns
                    spot = (pl.ds(pl.multiple_of(row, 8), self.rows), pl.ds(column, self.columns))
                    out[spot] = refs[source][z].astype(kind)
            for (start, stop, turned), ref in zip(cuts or (), outs):
                piece = out[:, start:stop]
                ref[...] = piece.T if turned else piece

        if cuts is None:
            return call(kernel, (place.vector,) + tuple(values), [(shape, kind)], 14)[0]
        shapes = [
            ((stop - start, shape[0]) if turned else (shape[0], stop - start), kind) for start, stop, turned in cuts
        ]
        return call(kernel, (place.vector,) + tuple(values), shapes, 20, [pltpu.VMEM(shape, kind)])


class Order:
    def __init__(self):
        self.last = None

    def hold(self, value):
        return value if self.last is None else after(value, self.last)

    def step(self, work, values):
        result = work([self.hold(values[0])] + list(values[1:]))
        self.last = result[0] if isinstance(result, (list, tuple)) else result
        return result


def reduce_all(parts, operands, order, beside, cuts):
    count = len(parts)
    state = [{} for _ in parts]
    done, extras = [None] * count, []

    def step(k, work, *names):
        return order.step(work, [state[k][name] for name in names])

    def away(k, sides=(0, 1)):
        made = order.step(lambda values: parts[k].away(values, sides), operands[k]())
        state[k]["core"] = [partner(piece, "dp", CORE) for piece in made]

    def keep(k, sides=(0, 1)):
        taken = operands[k]()
        taken[0] = order.hold(taken[0])
        made = parts[k].keep(state[k]["core"], taken, sides)
        order.last = made[0]
        for side, value in zip(sides, made):
            state[k][("keep", "go")[side]] = value

    def start_x(k):
        state[k]["moved"] = partner(order.hold(state[k]["go"]), "fsdp", 1)

    away(0, (1,))
    going = state[0]["core"]
    away(0, (0,))
    staying, state[0]["core"] = state[0]["core"], going
    keep(0, (1,))
    start_x(0)
    state[0]["core"] = staying
    keep(0, (0,))
    beside[0]()
    away(1)
    keep(1)
    for k in range(count + 3):
        now, last, before = k < count, 1 <= k <= count, 2 <= k <= count + 1
        if now:
            state[k]["y"], moved = step(k, parts[k].add_x, "keep", "moved")
            state[k]["y moved"] = partner(moved, "dp", ROW)
        if k + 1 < count:
            start_x(k + 1)
        if 3 <= k:
            done[k - 3] = order.step(lambda values: parts[k - 3].final(values, wide_type, cuts[k - 3]), state[k - 3]["cores"])
        if k == 0:
            beside[1]()
        if now:
            state[k]["z"], moved = step(k, parts[k].add_y, "y", "y moved")
            state[k]["z moved"] = partner(moved, "dp", LAYER)
        if last:
            state[k - 1]["sum"], *more = step(k - 1, parts[k - 1].add_last, "half", "half moved")
            extras += more
            state[k - 1]["sum moved"] = partner(state[k - 1]["sum"], "dp", LAYER)
        if before:
            own, moved = order.hold(state[k - 2]["four"]), order.hold(state[k - 2]["four moved"])
            order.last = moved
            state[k - 2]["cores"] = [own, moved] + [partner(value, "dp", CORE) for value in (own, moved)]
        if k + 2 < count:
            away(k + 2)
            keep(k + 2)
        if now:
            state[k]["half"] = step(k, parts[k].add_z, "z", "z moved")
            state[k]["half moved"] = partner(state[k]["half"], "dp", 2 * LAYER)
        if last:
            state[k - 1]["four"] = step(k - 1, parts[k - 1].join_z, "sum", "sum moved")
            state[k - 1]["four moved"] = partner(state[k - 1]["four"], "dp", ROW)
    return done, extras


def reduce_plain(matrices):
    return [
        lax.psum(lax.psum_scatter(matrix, "fsdp", scatter_dimension=dim, tiled=True), "dp").astype(wide_type)
        for matrix, dim in matrices
    ]


class Fetch:
    def __init__(self, operands, blocks):
        self.operands, self.blocks, self.count = operands, blocks, len(operands)

    def scratch(self):
        return pltpu.SemaphoreType.DMA((len(self.blocks),))

    def start(self, at_ref, sources, targets, sems):
        at = tuple(at_ref[i] for i in range(4))
        copies = {}
        for number, (target, operand, index, spot, (rows, columns)) in enumerate(self.blocks):
            source = sources[operand] if index is None else sources[operand].at[index]
            lead, row, column = spot(at)
            row = row if isinstance(row, int) else pl.multiple_of(row, 16)
            column = column if isinstance(column, int) else pl.multiple_of(column, 128)
            place = lead + (pl.ds(row, rows), pl.ds(column, columns))
            copy = pltpu.make_async_copy(source, targets[target].at[place], sems.at[number])
            copy.start()
            copies.setdefault(target, []).append(copy)
        return copies


def attention_shard_kernel(at_ref, query, key_t, out, value_t, low_ref, half_ref):
    start = 0
    for block in (query[...], key_t[...].T, out[...], value_t[...].T):
        low_ref[:, start : start + block.shape[1]] = block.astype(narrow_dtype)
        start += block.shape[1]
    rows = half_ref.shape[0]
    half_ref[...] = low_ref[pl.ds(pl.multiple_of(at_ref[1] * rows, 16), rows), :]


def down_shard_kernel(at_ref, down_t, low_ref, half_ref):
    low_ref[...] = down_t[...].astype(narrow_dtype)
    columns = half_ref.shape[1]
    half_ref[...] = low_ref[:, pl.ds(pl.multiple_of(at_ref[1] * columns, 128), columns)]


def narrow_kernel(wide_ref, narrow_ref):
    narrow_ref[...] = wide_ref[...].astype(narrow_dtype)


def narrowed(values):
    rows, columns = values[0].shape
    width = 512
    spec = pl.BlockSpec((rows, width), lambda i: (0, i))
    return pl.pallas_call(
        narrow_kernel,
        grid=(columns // width,),
        out_shape=jax.ShapeDtypeStruct((rows, columns), narrow_dtype),
        in_specs=[spec],
        out_specs=spec,
        compiler_params=pltpu.CompilerParams(vmem_limit_bytes=16 * 2**20),
        cost_estimate=pl.CostEstimate(flops=1000, bytes_accessed=1000, transcendentals=0),
    )(values[0])


def gather_weights(place, order, small, attn, pair, down_t, beside):
    mine, core, row, layer = place.scalars
    layers = place.layers
    model_rows, ff = pair[0].shape
    model, down_columns = down_t.shape
    low = lambda value: value.astype(narrow_dtype)
    attn_width = sum(value.shape[1] for value in attn)
    if not place.blocks:
        attn_full, gate, up, down_full = (
            lax.all_gather(low(value), "fsdp", axis=axis, tiled=True)
            for value, axis in ((jnp.concatenate(attn, axis=1), 0), (pair[0], 0), (pair[1], 0), (down_t, 1))
        )
        zero = lambda at: ((), 0, 0)
        first = Fetch([attn_full], [("attn", 0, None, zero, attn_full.shape)])
        every = Fetch(
            [attn_full, gate, up, down_full],
            [
                ("pair", 1, None, lambda at: ((0,), 0, 0), gate.shape),
                ("pair", 2, None, lambda at: ((1,), 0, 0), up.shape),
                ("down", 3, None, zero, down_full.shape),
                ("attn", 0, None, zero, attn_full.shape),
            ],
        )
        beside(first, lax.all_gather(small, "fsdp", axis=1, tiled=True))
        return first, every, Fetch(every.operands, every.blocks[:3])
    columns = ff // layers
    half = model_rows // 2
    half_columns = down_columns // 2
    own_piece = jnp.where(
        row == 0,
        lax.dynamic_slice(pair[0], (core * half, layer * columns), (half, columns)),
        lax.dynamic_slice(pair[1], (core * half, layer * columns), (half, columns)),
    )
    small_block = jnp.pad(small, ((0, 0), (0, columns - small.shape[1])))
    own_piece = jnp.concatenate([low(own_piece), small_block], axis=0)
    piece = partner(own_piece, "fsdp", 1)
    order.last = own_piece
    attn_low, attn_half = order.step(
        lambda values: call(
            attention_shard_kernel,
            [place.vector] + values,
            [((model_rows, attn_width), narrow_dtype), ((half, attn_width), narrow_dtype)],
            24,
        ),
        [attn[0], attn[1].T, attn[2], attn[3].T],
    )
    piece = order.hold(piece)
    order.last = piece
    pieces = [[piece] + [partner(piece, "dp", offset * LAYER) for offset in range(1, layers)]]
    pieces.append([partner(piece, "dp", ROW)])
    attn_near = partner(after(attn_half, piece), "fsdp", 1)
    down_low, down_half = order.step(
        lambda values: call(
            down_shard_kernel,
            [place.vector] + values,
            [(down_t.shape, narrow_dtype), ((model, half_columns), narrow_dtype)],
            24,
        ),
        [down_t],
    )
    gate_low = order.step(narrowed, [pair[0]])
    up_low = order.step(narrowed, [pair[1]])
    def over_y(index):
        moved = order.last = order.hold(pieces[0][index])
        pieces[0][index] = moved
        pieces[1].append(partner(moved, "dp", ROW))

    def arrived(index):
        pieces[1][index] = order.last = order.hold(pieces[1][index])

    over_y(1)
    over_y(2)
    arrived(0)
    over_y(3)
    attn_near = order.last = order.hold(attn_near)
    down_near = partner(after(down_half, attn_near), "fsdp", 1)
    attn_other = partner(attn_near, "dp", CORE)

    def halves(target, first):
        size = (half, attn_width)
        return [
            (target, first, None, lambda at: ((), at[0] * model_rows, 0), (model_rows, size[1])),
            (target, first + 1, None, lambda at: ((), (1 - at[0]) * model_rows + at[1] * half, 0), size),
            (target, first + 2, None, lambda at: ((), (1 - at[0]) * model_rows + (1 - at[1]) * half, 0), size),
        ]

    first = Fetch([attn_low, attn_near, attn_other], halves("attn", 0))
    order.last = attn_other
    small_other = piece[half:, : small.shape[1]]
    small_rows = jnp.where(
        mine == 0, jnp.concatenate([small, small_other], axis=1), jnp.concatenate([small_other, small], axis=1)
    )
    beside(first, small_rows)
    arrived(1)
    arrived(2)
    arrived(3)
    pieces += [[partner(moved, "dp", CORE) for moved in group] for group in pieces]
    down_near = order.hold(down_near)
    down_other = partner(down_near, "dp", CORE)
    blocks = [
        ("pair", 6, None, lambda at: ((0,), at[0] * model_rows, 0), (model_rows, ff)),
        ("pair", 7, None, lambda at: ((1,), at[0] * model_rows, 0), (model_rows, ff)),
    ]
    for number in range(4):
        for offset in range(layers):

            def spot(at, number=number, offset=offset):
                lead = (at[2] ^ (number % 2),)
                return (lead, (1 - at[0]) * model_rows + (at[1] ^ (number // 2)) * half, (at[3] ^ offset) * columns)

            blocks.append(("pair", 8 + number * layers + offset, (pl.ds(0, half),), spot, (half, columns)))
    near = (model, half_columns)
    blocks += [
        ("down", 3, None, lambda at: ((), 0, at[0] * down_columns), (model, down_columns)),
        ("down", 4, None, lambda at: ((), 0, (1 - at[0]) * down_columns + at[1] * half_columns), near),
        ("down", 5, None, lambda at: ((), 0, (1 - at[0]) * down_columns + (1 - at[1]) * half_columns), near),
    ]
    blocks += halves("attn", 0)
    operands = [attn_low, attn_near, attn_other, down_low, down_near, down_other, gate_low, up_low] + sum(pieces, [])
    ffn_blocks = [(block[0], block[1] - 3) + block[2:] for block in blocks if block[0] != "attn"]
    return first, Fetch(operands, blocks), Fetch(operands[3:], ffn_blocks)


def local(
    hidden_in,
    cotangent,
    norm_attn,
    norm_ffn,
    router,
    w_query,
    key_weight,
    value_weight,
    w_out,
    w_gate,
    w_up,
    w_down,
    lengths,
    chosen_second,
    chosen_third,
):
    place = Place(*w_gate.shape)
    owners, layers = place.owners, place.layers
    mine = place.scalars[0]
    width = w_query.shape[1]
    kv_width = key_weight.shape[1]
    small = jnp.concatenate(
        [norm_attn[None, :], norm_ffn[None, :], router.T, jnp.zeros((11, norm_attn.shape[0]), wide_type)]
    ).astype(narrow_dtype)
    count_one, model = hidden_in.shape
    ff = w_gate.shape[1]
    attn_width = 2 * width + 2 * kv_width
    chosen_two, chosen_three = chosen_second[0], chosen_third[0]
    count_two, count_three = chosen_two.shape[0], chosen_three.shape[0]
    count_rest = count_two + count_three
    count_all = count_one + count_rest
    cos_one, sin_one = rotary_tables(jnp.arange(count_one))
    cos_two, sin_two = rotary_tables(chosen_two)
    cos_three, sin_three = rotary_tables(chosen_three)
    v_width = attn_width - V_START
    first_outputs, small_wide = [], None

    def first_attention(fetch, small_rows):
        nonlocal small_wide
        small_wide = small_rows[:8].astype(wide_type)
        first_outputs.extend(
            call(
                partial(first_attention_kernel, fetch),
                [lengths, place.vector, after(order.hold(hidden_in.T), cos_two, sin_two, cos_three, sin_three), cotangent.T, small_wide, cos_one, sin_one]
                + fetch.operands,
                [
                    ((count_one, model), narrow_dtype),
                    ((count_one, model), narrow_dtype),
                    ((count_one, model), narrow_dtype),
                    ((count_one, QK_WIDTH), narrow_dtype),
                    ((count_one, v_width), narrow_dtype),
                    ((count_one, model), narrow_dtype),
                    ((GROUP * count_one, 128), wide_type),
                    ((count_one, model), wide_type),
                    ((count_one, 128), wide_type),
                ],
                26,
                attn_scratch + [fetch.scratch()],
                hbm=fetch.count,
                scalars=2,
            )
        )
        order.last = first_outputs[0]

    order = Order()
    attn_scratch = [pltpu.VMEM((model, attn_width), narrow_dtype)]
    fetch_attn, fetch_all, fetch_ffn = gather_weights(
        place, order, small, (w_query, key_weight, w_out, value_weight), (w_gate, w_up), w_down.T, first_attention
    )
    hidden_rows, cotangent_rows, normed_one, qk_one, v_one, att_one, log_one, attn_out_one, gating_one = first_outputs
    rest = lambda width: ((count_rest, width), narrow_dtype)
    every = lambda width: ((count_all, width), narrow_dtype)
    turned = ((model, count_all), narrow_dtype)
    scratch_for = lambda count: [
        pltpu.VMEM((count, QK_WIDTH), narrow_dtype),
        pltpu.VMEM((count, v_width), narrow_dtype),
        pltpu.VMEM((GROUP * count, 128), wide_type),
    ]
    back_scratch = lambda count: [
        pltpu.VMEM((count, model), narrow_dtype),
        pltpu.VMEM((count, QK_WIDTH), wide_type),
    ]
    wide = lambda count, width: pltpu.VMEM((count, width), wide_type)
    attn_tiles = -(-model // 128) * 128
    (
        hidden_out, d_input, d_gating_one, small_middle, hidden, d_ffn_t, d_gate_rest, d_up_rest, d_attn_rest,
        att_rest, normed_rest, d_qk_rest, d_v_rest, ffn_one, ffn_rest, d_ffn_one,
    ) = call(
        partial(middle_kernel, fetch_all),
        [
            lengths, place.vector, hidden_rows, cotangent_rows, small_wide, attn_out_one, gating_one,
            cos_two, sin_two, cos_three, sin_three,
            chosen_two[None, :], chosen_three[None, :],
        ]
        + fetch_all.operands,
        [
            ((count_one, model), narrow_dtype), ((count_one, model), wide_type), ((count_one, 128), wide_type),
            ((8, model), wide_type), every(ff), turned, rest(ff), rest(ff), rest(attn_tiles),
            rest(model), rest(model), rest(QK_WIDTH), rest(v_width),
            ((count_one, model), narrow_dtype), rest(model), ((count_one, model), narrow_dtype),
        ],
        36,
        [
            pltpu.VMEM((model, attn_width), narrow_dtype),
            pltpu.VMEM((2, model, ff), narrow_dtype),
            pltpu.VMEM((model, ff), narrow_dtype),
            fetch_all.scratch(),
            wide(count_two, ff), wide(count_two, ff), wide(count_three, ff), wide(count_three, ff),
            wide(count_one, model), wide(count_two, model), wide(count_three, model),
        ]
        + scratch_for(count_two) + scratch_for(count_three) + back_scratch(count_two) + back_scratch(count_three)
        + [pltpu.VMEM((count_rest, model), narrow_dtype)],
        hbm=fetch_all.count,
        scalars=2,
    )

    small_tile = attn_width // layers
    attention, feed = [], []

    def last_ffn():
        feed.extend(
            call(
                partial(last_ffn_kernel, fetch_ffn),
                [
                    lengths, place.vector, hidden_rows, small_wide, attn_out_one, gating_one, d_input,
                    order.hold(d_ffn_one), ffn_one, ffn_rest, d_gate_rest, d_up_rest, d_attn_rest,
                    small_middle,
                ]
                + fetch_ffn.operands,
                [
                    every(ff), every(ff), every(attn_tiles), turned, ((count_one, model), wide_type),
                    ((8, model), wide_type),
                ],
                38,
                [
                    pltpu.VMEM((2, model, ff), narrow_dtype),
                    pltpu.VMEM((model, ff), narrow_dtype),
                    fetch_ffn.scratch(),
                ],
                hbm=fetch_ffn.count,
                scalars=2,
            )
        )
        order.last = feed[0]

    def last_attention():
        d_attn, d_input_last, small_feed = feed[2], feed[4], feed[5]
        attention.extend(
            call(
                partial(last_attention_kernel, fetch_attn),
                [
                    lengths, place.vector, hidden_rows, small_wide, cos_one, sin_one, normed_one, qk_one, v_one, att_one,
                    log_one, gating_one, d_gating_one, order.hold(d_attn), d_input_last, normed_rest, att_rest, d_qk_rest,
                    d_v_rest, small_feed, hidden_out,
                ]
                + fetch_attn.operands,
                [
                    every(QK_WIDTH), every(v_width), turned, turned, ((model, count_one), wide_type),
                    ((8, model), wide_type), ((owners, 8, small_tile), wide_type), ((model, count_one), narrow_dtype),
                ],
                26,
                back_scratch(count_one) + attn_scratch + [fetch_attn.scratch()],
                hbm=fetch_attn.count,
                scalars=2,
            )
        )
        order.last = attention[0]

    if not place.blocks:
        last_ffn()
        last_attention()
        d_gate, d_up, d_attn, ffn_t, _, _ = feed
        d_qk, d_v, normed_t, att_t, grad_hidden_t, small_all, _, hidden_out_t = attention
        narrow_dot = lambda left, right: rows_dot(left, right).astype(narrow_dtype)
        skip = V_HEAD * HEAD_SIZE
        down_t, *reduced = reduce_plain(
            [
                (narrow_dot(d_ffn_t, hidden), 1),
                (narrow_dot(ffn_t, d_gate), 0),
                (narrow_dot(ffn_t, d_up), 0),
                (narrow_dot(normed_t, d_qk), 0),
                (narrow_dot(att_t, d_attn[:, :model]), 0),
                (narrow_dot(normed_t, d_v[:, skip:]), 0),
            ]
        )
        small_all = lax.psum_scatter(lax.psum(small_all, "dp"), "fsdp", scatter_dimension=1, tiled=True)
        return (
            hidden_out_t.T, grad_hidden_t.T, small_all[0], small_all[1], small_all[2:5].T,
            reduced[2][:, :width], reduced[2][:, width:], reduced[4], reduced[3], reduced[0], reduced[1], down_t.T,
        )
    by_core = lambda left: left.reshape(owners * 2, model // owners // 2, left.shape[1])
    size = ff // owners // 2

    def down_product(owner, core, left, right):
        return rows_dot(left[...], right[:, pl.ds(pl.multiple_of((owner * 2 + core) * size, 128), size)])

    def plain_product(owner, core, left, right):
        return rows_dot(left[owner * 2 + core], right[...])

    def small_block(owner, normed, d_qk, att, d_attn, d_v, small_parts):
        return small_parts[owner]

    def attention_product(owner, core, normed, d_qk, att, d_attn, d_v, small_parts):
        left = normed[owner * 2 + core]
        out = rows_dot(att[owner * 2 + core], d_attn[...])
        value = rows_dot(left, d_v[...])
        shared = attn_tiles - 128
        return jnp.concatenate(
            [rows_dot(left, d_qk[...]), out[:, :shared], out[:, shared:] + value[:, :128], value[:, 128:]], axis=1
        )

    rows = model // owners // 4
    parts = [
        Part(place, down_product, model // 2 // layers, size, tall=True),
        Part(place, plain_product, rows, ff // layers),
        Part(place, plain_product, rows, ff // layers),
        Part(place, attention_product, rows, attn_width // layers, extra=small_block),
    ]
    operands = [
        lambda: [d_ffn_t, hidden],
        lambda: [by_core(feed[3]), feed[0]],
        lambda: [by_core(feed[3]), feed[1]],
        lambda: [by_core(attention[2]), attention[0], by_core(attention[3]), feed[2], attention[1], attention[6]],
    ]
    cuts = [
        (0, width, False),
        (width, width + kv_width, True),
        (width + kv_width, 2 * width + kv_width, False),
        (2 * width + kv_width, attn_width, True),
    ]
    reduced, small_sum = reduce_all(parts, operands, order, (last_ffn, last_attention), [None, None, None, cuts])
    down_t, gate_shard, up_shard, (query_shard, key_t, out_shard, value_t) = reduced
    small_sum = small_sum[0][0][:, : model // owners]
    return (
        attention[7].T,
        attention[4].T,
        small_sum[0],
        small_sum[1],
        small_sum[2:5].T,
        query_shard,
        key_t.T,
        value_t.T,
        out_shard,
        gate_shard,
        up_shard,
        down_t.T,
    )


def solution(mesh):
    in_specs = (
        P(("dp", "fsdp"), None),
        P(("dp", "fsdp"), None),
        P("fsdp"),
        P("fsdp"),
        P("fsdp", None),
        P("fsdp", None),
        P("fsdp", None),
        P("fsdp", None),
        P("fsdp", None),
        P("fsdp", None),
        P("fsdp", None),
        P("fsdp", None),
        P(("dp", "fsdp")),
        P(("dp", "fsdp"), None),
        P(("dp", "fsdp"), None),
    )
    out_specs = (
        P(("dp", "fsdp"), None),
        P(("dp", "fsdp"), None),
        P("fsdp"),
        P("fsdp"),
        P("fsdp", None),
        P("fsdp", None),
        P("fsdp", None),
        P("fsdp", None),
        P("fsdp", None),
        P("fsdp", None),
        P("fsdp", None),
        P("fsdp", None),
    )
    return jax.shard_map(local, mesh=mesh, in_specs=in_specs, out_specs=out_specs, check_vma=False)
```
